32 devices in a mesh: omega: 4 (over x, core), row: 4 (over z), col: 2 (over y).
Axes of the slice: x: 2, y: 2, z: 4, core: 2. Of those that a mesh axis runs over, the one named last changes fastest.
Arguments:
- frames: bfloat16 [2, 64, 512, 2048], P(None, 'omega', 'row', 'col'), may hold values from -6 to 6
- omega_taps: float32 [15], replicated, may hold values from 0.1 to 1
- smooth_kernel: float32 [5, 5], replicated, may hold values from 0.05 to 0.15
- spots: int32 [2, 3, 4096], P(None, None, ('omega', 'row', 'col')), may hold values from 0 to 2032, as said below
- counts: int32 [2, 32], P(None, ('omega', 'row', 'col')), may hold values from 1 to 128, as said below
Outputs:
- smoothed: bfloat16 [2, 64, 512, 2048], P(None, 'omega', 'row', 'col')
- scores: float32 [4096, 128], P(('omega', 'row', 'col'))
The draws below stay inside these ranges and needn't reach their ends.
Inputs may be any that keep to these rules, and one draw needn't show every extreme that they name: `spots`: slot i belongs to block i div 128; its spot's frame lies in that block's frames and its whole 16 x 16 patch lies in that block's rows and columns. `counts`: some block of each slab has all 128 slots live.
All inputs are finite; a program needn't handle non-finite values.
Results may differ from the reference program's by a relative error of at most 0.0022.
Values may be sent and summed in bfloat16 or wider, within the bound.
No kernel may reach another device: no remote copies, remote signals or barrier semaphores. Data moves between devices by JAX's collectives and lax.ppermute only.
A program may use at most 192 MiB of HBM per device.

```python
import math
import jax
import jax.numpy as jnp
from jax import lax

FD = 16
RD = 128
CD = 1024
K = 128
TAPS = 15
PATCH = 16
FRAMES = 64
ROWS = 512
COLS = 2048
BANDS = 4
HALVES = 2
BLOCKS = 32
N_OMEGA = 4
N_ROW = 4
N_COL = 2


def draw_spots(key, part):
    slot_total = K * BLOCKS
    block = jnp.arange(slot_total, dtype=jnp.int32) // K
    frame_block = block // (BANDS * HALVES)
    band = block // HALVES % BANDS
    half = block % HALVES
    key_frame, key_row, key_col = jax.random.split(key, 3)
    frame_off = jax.random.randint(key_frame, (2, slot_total), 0, FD)
    row_off = jax.random.randint(key_row, (2, slot_total), 0, RD - PATCH + 1)
    col_off = jax.random.randint(key_col, (2, slot_total), 0, CD - PATCH + 1)
    frame_off = frame_off.at[:, 0].set(0).at[:, slot_total - 1].set(FD - 1)
    row_off = row_off.at[:, 0].set(0).at[:, slot_total - 1].set(RD - PATCH)
    col_off = col_off.at[:, 0].set(0).at[:, slot_total - 1].set(CD - PATCH)
    frame = frame_block * FD + frame_off
    row = band * RD + row_off
    col = half * CD + col_off
    return jnp.stack([frame, row, col], axis=1).astype(jnp.int32)


def draw_counts(key, part):
    key_base, key_top = jax.random.split(key)
    base = jax.random.randint(key_base, (2, BLOCKS), max(1, K // 8), K + 1)
    top = jax.random.randint(key_top, (2,), 0, BLOCKS)
    return base.at[jnp.arange(2), top].set(K).astype(jnp.int32)


def steps_of(stream_key, extent, cuts, low, largest):
    def one(axis_at, shards_of):
        draws = jax.random.uniform(jax.random.fold_in(jax.random.fold_in(stream_key, 6), axis_at), (shards_of,), jnp.float32, low / len(cuts), largest / len(cuts))
        return jnp.repeat(jnp.exp(draws), extent[axis_at] // shards_of).reshape((-1,) + (1,) * (len(extent) - axis_at - 1))

    factor_of = one(*cuts[0])
    for cut in cuts[1:]:
        factor_of = factor_of * one(*cut)
    return factor_of


def gaussian(key, shape, width, bound, pieces=(), kind=jnp.bfloat16):
    values = jax.random.normal(key, shape, jnp.float32) * width
    if len(pieces) > 0:
        values = steps_of(key, shape, pieces, -0.22, 0.18) * values
    return jnp.clip(values, min=-bound, max=bound).astype(kind)


def setup_inputs(seed: int = 0) -> dict:
    arg_keys = jax.random.split(jax.random.key(seed), 6)
    frames = gaussian(arg_keys[0], (2, FRAMES, ROWS, COLS), 1.0, 6.0, ((1, 4), (2, 4), (3, 2)))
    omega_taps = jnp.clip(jnp.exp(jax.random.uniform(arg_keys[1], (TAPS,), jnp.float32, math.log(0.1), math.log(1.0))), 0.1, 1.0)
    smooth_kernel = jnp.clip(jax.random.uniform(arg_keys[2], (5, 5), jnp.float32, 0.05, 0.15), 0.05, 0.15)
    spots = draw_spots(jax.random.fold_in(arg_keys[5], 71), 0)
    counts = draw_counts(jax.random.fold_in(arg_keys[5], 71), 0)
    return dict(frames=frames, omega_taps=omega_taps, smooth_kernel=smooth_kernel, spots=spots, counts=counts)


def normalize(values, live):
    mean_value = lax.optimization_barrier(jnp.mean(values, axis=1, keepdims=True))
    centered = values - mean_value
    spread = lax.optimization_barrier(jnp.mean(centered * centered, axis=1, keepdims=True))
    normed = centered / jnp.sqrt(spread + 1e-05)
    return jnp.where(live[:, None], normed, 0.0).astype(jnp.bfloat16)

def reference(frames, omega_taps, smooth_kernel, spots, counts):
    frame_total = frames.shape[1]
    row_total = frames.shape[2]
    col_total = frames.shape[3]

    def one_frame(index):
        slab = (index // frame_total).astype(jnp.int32)
        frame = (index % frame_total).astype(jnp.int32)
        center = lax.dynamic_slice(frames, (slab, frame, jnp.int32(0), jnp.int32(0)), (1, 1, row_total, col_total))[0, 0].astype(jnp.float32)
        background = jnp.zeros((row_total, col_total), jnp.float32)
        norm = jnp.float32(0.0)
        for offset in range(TAPS):
            source = frame + offset - 7
            valid = ((source >= 0) & (source < frame_total)).astype(jnp.float32)
            clipped = jnp.clip(source, 0, frame_total - 1).astype(jnp.int32)
            plane = lax.dynamic_slice(frames, (slab, clipped, jnp.int32(0), jnp.int32(0)), (1, 1, row_total, col_total))[0, 0].astype(jnp.float32)
            background = background + omega_taps[offset] * valid * plane
            norm = norm + omega_taps[offset] * valid
        corrected = center - background / norm
        padded = jnp.pad(corrected, 2)
        result = jnp.zeros((row_total, col_total), jnp.float32)
        for row_shift in range(5):
            for col_shift in range(5):
                result = result + smooth_kernel[row_shift, col_shift] * padded[row_shift:row_shift + row_total, col_shift:col_shift + col_total]
        return result.astype(jnp.bfloat16)
    flat = lax.map(one_frame, jnp.arange(2 * frame_total, dtype=jnp.int32))
    smoothed = flat.reshape(2, frame_total, row_total, col_total)
    slot_total = spots.shape[2]
    slot_ids = jnp.arange(slot_total, dtype=jnp.int32)

    def patches_of(slab):

        def take(frame, row, col):
            return lax.dynamic_slice(smoothed[slab], (frame, row, col), (1, PATCH, PATCH)).reshape(PATCH * PATCH)
        values = jax.vmap(take)(spots[slab, 0], spots[slab, 1], spots[slab, 2]).astype(jnp.float32)
        live = slot_ids % K < counts[slab][slot_ids // K]
        return normalize(values, live)
    first = patches_of(0).reshape(N_OMEGA, N_ROW * N_COL, K, PATCH * PATCH)
    second = patches_of(1).reshape(N_OMEGA, N_ROW * N_COL, K, PATCH * PATCH)[:, ::-1]
    scores = jnp.einsum('obik,objk->obij', first.astype(jnp.float32), second.astype(jnp.float32)) / 256.0
    return (smoothed, scores.reshape(slot_total, K))
```

```python
import functools
import jax
import jax.numpy as jnp
from jax import lax
from jax.experimental import pallas as pl
from jax.experimental.pallas import tpu as pltpu
from jax.sharding import PartitionSpec as P

TAPS = 15
HALF = TAPS // 2
PATCH = 16
SIDE = 5
REACH = SIDE // 2
TILE = 128
WIN = 48
PAD = 16
bf16 = jnp.bfloat16
f32 = jnp.float32


def shifted(block, axis, step):
    count = lax.axis_size(axis)
    route = [(i, i + step) for i in range(count) if 0 <= i + step < count]
    return lax.ppermute(block, axis, route)


def split(values):
    high = lax.reduce_precision(values, 8, 7)
    return high.astype(bf16), (values - high).astype(bf16)


def omega_matrix(omega_taps, first_frame, frame_count, frame_total):
    out_ids = jnp.arange(frame_count, dtype=jnp.int32)[:, None]
    in_ids = jnp.arange(frame_count + 2 * HALF, dtype=jnp.int32)[None, :]
    source = first_frame + in_ids - HALF
    valid = (source >= 0) & (source < frame_total)
    tap = jnp.where(valid, in_ids - out_ids, -1)
    hit = tap[:, :, None] == jnp.arange(TAPS, dtype=jnp.int32)
    weights = jnp.sum(jnp.where(hit, omega_taps, 0.0), axis=2)
    norm = jnp.sum(weights, axis=1, keepdims=True)
    center = (in_ids - out_ids == HALF).astype(f32)
    matrix = center - weights / norm
    same = jnp.eye(8, dtype=bf16)
    parts = jnp.stack(split(matrix))
    wide = parts[:, :, None, :, None] * same[None, None, :, None, :]
    return wide.reshape(2 * frame_count * 8, (frame_count + 2 * HALF) * 8)


def smooth_matrix(smooth_kernel, rows):
    depth = rows + 2 * PAD
    out_ids = jnp.arange(rows, dtype=jnp.int32)[:, None]
    in_ids = jnp.arange(depth, dtype=jnp.int32)[None, :]
    step = in_ids - out_ids - (PAD - REACH)
    hit = step[None, :, :, None] == jnp.arange(SIDE, dtype=jnp.int32)
    table = jnp.sum(jnp.where(hit, smooth_kernel.T[:, None, None, :], 0.0), axis=3)
    high, low = split(table)
    return jnp.concatenate([high, high, low], axis=2).reshape(SIDE * rows, 3 * depth)


def windows_of(row_count):
    return [(at, min(WIN, row_count - at)) for at in range(0, row_count, WIN)]


def slab_kernel(
    slab, row_step, frame_step, with_scores,
    spots_ref, w1_ref, w2_refs, low_ref, own_ref, high_ref, edge_ref, halo_ref, other_ref,
    out_ref, last_ref, chi, clo, kept, window, flat,
):
    frame_count, row_count, col_count = kept.shape
    half_rows = frame_count * 8
    steps_1 = row_count // row_step
    steps_2 = frame_count // frame_step
    at = pl.program_id(0)

    def filtered(block):
        wide = block.astype(f32)
        outs = []
        for q in range(block.shape[1] // 8):
            part = wide[:, 8 * q : 8 * q + 8, :]
            part = part.reshape(part.shape[0] * 8, part.shape[2]).astype(bf16)
            both = jnp.dot(w1_ref[...], part, preferred_element_type=f32)
            outs.append((both[:half_rows] + both[half_rows:]).reshape(frame_count, 8, -1))
        return outs

    def keep(outs, place, cols):
        value = jnp.concatenate(outs, axis=1)
        high = value.astype(bf16)
        chi[:, place, cols] = high
        clo[:, place, cols] = (value - high.astype(f32)).astype(bf16)

    col_cuts = [(c, min(256, col_count - c)) for c in range(0, col_count, 256)]

    @pl.when(at == 0)
    def _():
        for c, n in col_cuts + [(col_count, TILE)]:
            one = filtered(halo_ref[0, :, :, c : c + n])[0]
            keep([one, one], slice(0, PAD), slice(c, c + n))
            keep([one, one], slice(PAD + row_count, 2 * PAD + row_count), slice(c, c + n))

    @pl.when(at < steps_1)
    def _():
        for h in range(row_step // 16):
            rows = slice(16 * h, 16 * h + 16)
            place = pl.ds(pl.multiple_of(PAD + at * row_step + 16 * h, 16), 16)
            for c, n in col_cuts:
                cols = slice(c, c + n)
                block = jnp.concatenate(
                    [low_ref[:, rows, cols], own_ref[0, :, rows, cols], high_ref[:, rows, cols]],
                    axis=0,
                )
                keep(filtered(block), place, cols)
            keep(filtered(edge_ref[0, :, rows, :]), place, slice(col_count, col_count + TILE))

    @pl.when((at >= steps_1) & (at < steps_1 + steps_2))
    def _():
        def one_frame(k, carry):
            frame = (at - steps_1) * frame_step + k
            for (row, n), w2_ref in zip(windows_of(row_count), w2_refs):
                depth = n + 2 * PAD
                high = chi[frame, row : row + depth, :]
                low = clo[frame, row : row + depth, :]
                stacked = jnp.concatenate([high, low, high], axis=0)
                cols = jnp.dot(w2_ref[...], stacked, preferred_element_type=f32)
                total = cols[REACH * n : (REACH + 1) * n]
                for b in range(SIDE):
                    if b != REACH:
                        turn = (REACH - b) % cols.shape[1]
                        total = total + pltpu.roll(cols[b * n : (b + 1) * n], turn, 1)
                value = total[:, :col_count].astype(bf16)
                out_ref[0, k, row : row + n, :] = value
                kept[frame, row : row + n, :] = value
            return carry

        lax.fori_loop(0, frame_step, one_frame, 0)

    @pl.when(at == steps_1 + steps_2)
    def _():
        slot_count = flat.shape[0] // PATCH
        def some(i8, carry):
            for j in range(8):
                i = i8 * 8 + j
                frame, row, col = spots_ref[0, i], spots_ref[1, i], spots_ref[2, i]
                row_at = pl.multiple_of(jnp.minimum(row // 16 * 16, row_count - 32), 16)
                col_at = pl.multiple_of(jnp.minimum(col // TILE * TILE, col_count - 256), TILE)
                found = kept[frame, pl.ds(row_at, 32), pl.ds(col_at, 256)].astype(f32)
                window[j, :32] = found[:, :TILE]
                window[j, 32:] = found[:, TILE:]
                part = jnp.concatenate(
                    [window[j, pl.ds(row - row_at + k, PATCH), :] for k in (0, 32)], axis=1
                )
                part = pltpu.roll(part, 256 - (col - col_at), 1)[:, :TILE]
                flat[pl.ds(pl.multiple_of(i * PATCH, PATCH), PATCH), :] = part.astype(bf16)
            return carry

        lax.fori_loop(0, slot_count // 8, some, 0)
        lane = lax.broadcasted_iota(jnp.int32, (TILE, PATCH * PATCH), 1)
        sub = lax.broadcasted_iota(jnp.int32, (TILE, PATCH * PATCH), 0)
        spread_out = (lane % PATCH == sub).astype(bf16)
        rows = jnp.dot(flat[...], spread_out, preferred_element_type=f32)
        lane = lax.broadcasted_iota(jnp.int32, rows.shape, 1)
        sub = lax.broadcasted_iota(jnp.int32, rows.shape, 0)
        rows = jnp.where(lane // PATCH == sub % PATCH, rows, 0.0).astype(bf16)
        lane = lax.broadcasted_iota(jnp.int32, (slot_count, rows.shape[0]), 1)
        sub = lax.broadcasted_iota(jnp.int32, (slot_count, rows.shape[0]), 0)
        values = jnp.dot(
            (lane // PATCH == sub).astype(bf16), rows, preferred_element_type=f32
        )
        mean = jnp.sum(values, axis=1, keepdims=True) / (PATCH * PATCH)
        centered = values - mean
        spread = jnp.sum(centered * centered, axis=1, keepdims=True) / (PATCH * PATCH)
        normed = centered / jnp.sqrt(spread + 1e-05)
        slot = lax.broadcasted_iota(jnp.int32, (slot_count, 1), 0)
        normed = jnp.where(slot < spots_ref[3, 0], normed, 0.0).astype(bf16)
        if with_scores:
            last_ref[...] = lax.dot_general(
                normed, other_ref[...], (((1,), (1,)), ((), ())), preferred_element_type=f32
            ) / (PATCH * PATCH)
        else:
            last_ref[...] = normed


def run_slab(slab, smoothed, other, spots, w1, w2s, low, frames, high, edge, halo):
    _, frame_count, row_count, col_count = frames.shape
    slot_count = spots.shape[1]
    row_step, frame_step = 32, 4
    steps_1 = row_count // row_step
    steps_2 = frame_count // frame_step
    wide = col_count + TILE
    near = frame_count + 2 * HALF

    def row_block(at):
        return jnp.minimum(at, steps_1 - 1)

    def whole(array):
        return pl.BlockSpec(array.shape, lambda at: (0,) * array.ndim)

    def body(*refs):
        refs = list(refs)
        spots_ref, w1_ref = refs[:2]
        w2_refs = refs[2 : 2 + len(w2s)]
        refs = refs[2 + len(w2s) :]
        low_ref, own_ref, high_ref, edge_ref, halo_ref = refs[:5]
        refs = refs[5:]
        other_ref = None
        if other is not None:
            other_ref = refs[0]
            refs = refs[2:]
        slab_kernel(
            slab, row_step, frame_step, other is not None,
            spots_ref, w1_ref, w2_refs, low_ref, own_ref, high_ref, edge_ref, halo_ref, other_ref,
            *refs,
        )

    operands = [spots, w1, *w2s, low, frames, high, edge, halo]
    in_specs = [
        pl.BlockSpec(memory_space=pltpu.SMEM),
        whole(w1),
        *[whole(w2) for w2 in w2s],
        pl.BlockSpec((HALF, row_step, col_count), lambda at: (0, row_block(at), 0)),
        pl.BlockSpec((1, frame_count, row_step, col_count), lambda at: (slab, 0, row_block(at), 0)),
        pl.BlockSpec((HALF, row_step, col_count), lambda at: (0, row_block(at), 0)),
        pl.BlockSpec((1, near, row_step, TILE), lambda at: (slab, 0, row_block(at), 0)),
        pl.BlockSpec((1, near, 8, wide), lambda at: (slab, 0, 0, 0)),
    ]
    aliases = {}
    last_shape = jax.ShapeDtypeStruct((slot_count, PATCH * PATCH), bf16)
    if other is not None:
        operands += [other, smoothed]
        in_specs += [whole(other), pl.BlockSpec(memory_space=pl.ANY)]
        aliases = {len(operands) - 1: 0}
        last_shape = jax.ShapeDtypeStruct((slot_count, other.shape[0]), f32)
    return pl.pallas_call(
        body,
        grid=(steps_1 + steps_2 + 1,),
        in_specs=in_specs,
        out_specs=[
            pl.BlockSpec(
                (1, frame_step, row_count, col_count),
                lambda at: (slab, jnp.clip(at - steps_1, 0, steps_2 - 1), 0, 0),
            ),
            pl.BlockSpec(last_shape.shape, lambda at: (0, 0)),
        ],
        out_shape=[jax.ShapeDtypeStruct(frames.shape, bf16), last_shape],
        scratch_shapes=[
            pltpu.VMEM((frame_count, row_count + 2 * PAD, wide), bf16),
            pltpu.VMEM((frame_count, row_count + 2 * PAD, wide), bf16),
            pltpu.VMEM((frame_count, row_count, col_count), bf16),
            pltpu.VMEM((8, 64, TILE), f32),
            pltpu.VMEM((slot_count * PATCH, TILE), bf16),
        ],
        input_output_aliases=aliases,
        compiler_params=pltpu.CompilerParams(vmem_limit_bytes=56 * 1024 * 1024),
        cost_estimate=pl.CostEstimate(
            flops=20_000_000_000, bytes_accessed=16_000_000, transcendentals=0
        ),
        name=f"slab_{slab}",
    )(*operands)


def shards(frames, omega_taps, smooth_kernel, spots, counts):
    _, frame_count, row_count, col_count = frames.shape
    first_frame = lax.axis_index("omega") * frame_count
    first_row = lax.axis_index("row") * row_count
    first_col = lax.axis_index("col") * col_count

    rows = jnp.concatenate([frames[:, :, :REACH], frames[:, :, -REACH:]], axis=2)
    cols = jnp.concatenate([frames[..., :REACH], frames[..., -REACH:]], axis=3)
    rim = jnp.concatenate([rows, jnp.swapaxes(cols, 2, 3)], axis=3)
    rim = jnp.concatenate(
        [shifted(rim[:, -HALF:], "omega", 1), rim, shifted(rim[:, :HALF], "omega", -1)], axis=1
    )
    low1 = shifted(frames[1, -HALF:], "omega", 1)
    high1 = shifted(frames[1, :HALF], "omega", -1)
    low0 = shifted(frames[0, -HALF:], "omega", 1)
    high0 = shifted(frames[0, :HALF], "omega", -1)
    left = shifted(rim[:, :, REACH:, col_count:], "col", 1)
    right = shifted(rim[:, :, :REACH, col_count:], "col", -1)
    place = jnp.arange(2 * REACH, dtype=jnp.int32)
    place = jnp.where(place < REACH, place, TILE - 2 * REACH + place)
    place = (place[:, None] == jnp.arange(TILE, dtype=jnp.int32)[None, :]).astype(bf16)
    edge = jnp.einsum(
        "sfkr,kc->sfrc", jnp.concatenate([right, left], axis=2), place, preferred_element_type=bf16
    )
    ends = jnp.concatenate([edge[:, :, :REACH], edge[:, :, -REACH:]], axis=2)
    line = jnp.concatenate([rim[..., :col_count], ends], axis=3)
    above = shifted(line[:, :, REACH:], "row", 1)
    below = shifted(line[:, :, :REACH], "row", -1)
    gap = jnp.zeros(above.shape[:2] + (8 - 2 * REACH, line.shape[3]), bf16)
    halo = jnp.concatenate([below, gap, above], axis=2)

    w1 = omega_matrix(omega_taps, first_frame, frame_count, frame_count * lax.axis_size("omega"))
    sizes = [n for _, n in windows_of(row_count)]
    w2 = {n: smooth_matrix(smooth_kernel, n) for n in set(sizes)}
    w2s = [w2[n] for n in sizes]
    base = jnp.stack([first_frame, first_row, first_col]).astype(jnp.int32)
    local = spots - base[None, :, None]
    live = jnp.broadcast_to(counts[:, :, None], (2, 1, spots.shape[2]))
    local = jnp.concatenate([local, live], axis=1)

    smoothed, second = run_slab(
        1, None, None, local[1], w1, w2s, low1, frames, high1, edge, halo
    )
    count = lax.axis_size("row") * lax.axis_size("col")
    second = lax.ppermute(second, ("row", "col"), [(i, count - 1 - i) for i in range(count)])
    smoothed, scores = run_slab(
        0, smoothed, second, local[0], w1, w2s, low0, frames, high0, edge, halo
    )
    return (smoothed, scores)


def solution(mesh):
    return jax.shard_map(
        shards,
        mesh=mesh,
        in_specs=(
            P(None, "omega", "row", "col"),
            P(),
            P(),
            P(None, None, ("omega", "row", "col")),
            P(None, ("omega", "row", "col")),
        ),
        out_specs=(P(None, "omega", "row", "col"), P(("omega", "row", "col"), None)),
        check_vma=False,
    )
```

```python
import jax
import jax.numpy as jnp
from jax import lax
from jax.experimental import pallas as pl
from jax.experimental.pallas import tpu as pltpu
from jax.sharding import PartitionSpec as P

TAPS = 15
HALF = TAPS // 2
PATCH = 16
SIDE = 5
REACH = SIDE // 2
TILE = 128
BLOCK = 16
bf16 = jnp.bfloat16
f32 = jnp.float32


def shifted(block, axis, step):
    count = lax.axis_size(axis)
    route = [(i, i + step) for i in range(count) if 0 <= i + step < count]
    return lax.ppermute(block, axis, route)


def split(values):
    high = lax.reduce_precision(values, 8, 7)
    return high.astype(bf16), (values - high).astype(bf16)


def omega_matrix(omega_taps, first_frame, frame_count, frame_total):
    out_ids = jnp.arange(frame_count, dtype=jnp.int32)[:, None]
    in_ids = jnp.arange(frame_count + 2 * HALF, dtype=jnp.int32)[None, :]
    source = first_frame + in_ids - HALF
    valid = (source >= 0) & (source < frame_total)
    tap = jnp.where(valid, in_ids - out_ids, -1)
    hit = tap[:, :, None] == jnp.arange(TAPS, dtype=jnp.int32)
    weights = jnp.sum(jnp.where(hit, omega_taps, 0.0), axis=2)
    norm = jnp.sum(weights, axis=1, keepdims=True)
    center = (in_ids - out_ids == HALF).astype(f32)
    matrix = center - weights / norm
    return jnp.stack(split(matrix), axis=1).reshape(2 * frame_count, matrix.shape[1])


def smooth_matrix(smooth_kernel):
    depth = 3 * BLOCK
    out_ids = jnp.arange(BLOCK, dtype=jnp.int32)[:, None]
    in_ids = jnp.arange(depth, dtype=jnp.int32)[None, :]
    step = in_ids - out_ids - (BLOCK - REACH)
    hit = step[None, :, :, None] == jnp.arange(SIDE, dtype=jnp.int32)
    table = jnp.sum(jnp.where(hit, smooth_kernel.T[:, None, None, :], 0.0), axis=3)
    high, low = split(table)
    return jnp.concatenate([high, high, low], axis=2).reshape(SIDE * BLOCK, 3 * depth)


def iota(shape, dim):
    return lax.broadcasted_iota(jnp.int32, shape, dim)


def slab_kernel(
    row_step, frame_step,
    spots_ref, taps_ref, w2_ref, low_ref, own_ref, high_ref, edge_ref, halo_ref,
    out_ref, last_ref, w1, chi, clo, kept, window, flat,
):
    frame_count, row_count, col_count = kept.shape
    near = taps_ref.shape[1]
    tiles = col_count // TILE
    steps_1 = row_count // row_step
    steps_2 = frame_count // frame_step
    at = pl.program_id(0)

    def filtered(block):
        part = block.reshape(near * 8, block.shape[2]).astype(bf16)
        both = jnp.dot(w1[...], part, preferred_element_type=f32)
        both = both.reshape(frame_count, 2, 8, block.shape[2])
        return both[:, 0] + both[:, 1]

    def keep(value, tile, place):
        high = value.astype(bf16)
        chi[:, tile, place, :] = high
        clo[:, tile, place, :] = (value - high.astype(f32)).astype(bf16)

    @pl.when(at == 0)
    def _():
        count = 2 * frame_count
        tall = (iota((8 * count, count), 0) // 8 == iota((8 * count, count), 1)).astype(bf16)
        wide = (iota((near, 8 * near), 1) // 8 == iota((near, 8 * near), 0)).astype(bf16)
        full = jnp.dot(tall, taps_ref[...], preferred_element_type=f32).astype(bf16)
        full = jnp.dot(full, wide, preferred_element_type=f32)
        same = iota(full.shape, 0) % 8 == iota(full.shape, 1) % 8
        w1[...] = jnp.where(same, full, 0.0).astype(bf16)
        for tile in range(tiles + 1):
            cols = slice(tile * TILE, tile * TILE + TILE)
            one = filtered(halo_ref[0, :, :, cols].astype(f32))
            two = jnp.concatenate([one, one], axis=1)
            keep(two, tile, slice(0, BLOCK))
            keep(two, tile, slice(BLOCK + row_count, 2 * BLOCK + row_count))

    @pl.when(at < steps_1)
    def _():
        for h in range(row_step // BLOCK):
            rows = slice(BLOCK * h, BLOCK * h + BLOCK)
            place = pl.ds(pl.multiple_of(BLOCK + at * row_step + BLOCK * h, BLOCK), BLOCK)
            for tile in range(0, tiles, 2):
                cols = slice(tile * TILE, (tile + 2) * TILE)
                block = jnp.concatenate(
                    [low_ref[:, rows, cols], own_ref[0, :, rows, cols], high_ref[:, rows, cols]],
                    axis=0,
                ).astype(f32)
                value = jnp.concatenate([filtered(block[:, :8]), filtered(block[:, 8:])], axis=1)
                keep(value[..., :TILE], tile, place)
                keep(value[..., TILE:], tile + 1, place)
            block = edge_ref[0, :, rows, :].astype(f32)
            value = filtered(jnp.concatenate([block[:, :8], block[:, 8:]], axis=2))
            value = jnp.concatenate([value[..., :TILE], value[..., TILE:]], axis=1)
            keep(value, tiles, place)

    @pl.when((at >= steps_1) & (at < steps_1 + steps_2))
    def _():
        lane = iota((BLOCK, TILE), 1)
        edge_of = [lane < 2, lane < 1, None, lane >= TILE - 1, lane >= TILE - 2]

        def one_frame(k, carry):
            frame = (at - steps_1) * frame_step + k
            for row in range(0, row_count, BLOCK):
                turned = {}
                order = [tiles] + list(range(tiles))
                for p in range(0, len(order), 2):
                    pair = order[p : p + 2]
                    parts = []
                    for tile in pair:
                        high = chi[frame, tile, row : row + 3 * BLOCK, :]
                        low = clo[frame, tile, row : row + 3 * BLOCK, :]
                        parts.append(jnp.concatenate([high, low, high], axis=0))
                    both = jnp.dot(
                        w2_ref[...], jnp.concatenate(parts, axis=1), preferred_element_type=f32
                    )
                    for q, tile in enumerate(pair):
                        for b in range(SIDE):
                            part = both[b * BLOCK : (b + 1) * BLOCK, q * TILE : (q + 1) * TILE]
                            if b != REACH:
                                part = pltpu.roll(part, (REACH - b) % TILE, 1)
                            turned[b, tile] = part
                for tile in range(tiles):
                    total = turned[REACH, tile]
                    for b in range(SIDE):
                        if b != REACH:
                            beside = (tile + (1 if b > REACH else -1)) % (tiles + 1)
                            total = total + jnp.where(
                                edge_of[b], turned[b, beside], turned[b, tile]
                            )
                    value = total.astype(bf16)
                    out_ref[0, k, row : row + BLOCK, tile * TILE : (tile + 1) * TILE] = value
                    kept[frame, row : row + BLOCK, tile * TILE : (tile + 1) * TILE] = value
            return carry

        lax.fori_loop(0, frame_step, one_frame, 0)

    @pl.when(at == steps_1 + steps_2)
    def _():
        slot_count = flat.shape[0] // PATCH

        def some(i8, carry):
            for j in range(8):
                i = i8 * 8 + j
                frame, row, col = spots_ref[0, i], spots_ref[1, i], spots_ref[2, i]
                row_at = pl.multiple_of(jnp.minimum(row // 16 * 16, row_count - 32), 16)
                col_at = pl.multiple_of(jnp.minimum(col // TILE * TILE, col_count - 256), TILE)
                found = kept[frame, pl.ds(row_at, 32), pl.ds(col_at, 256)].astype(f32)
                window[j, :32] = found[:, :TILE]
                window[j, 32:] = found[:, TILE:]
                part = jnp.concatenate(
                    [window[j, pl.ds(row - row_at + k, PATCH), :] for k in (0, 32)], axis=1
                )
                part = pltpu.roll(part, 256 - (col - col_at), 1)[:, :TILE]
                flat[pl.ds(pl.multiple_of(i * PATCH, PATCH), PATCH), :] = part.astype(bf16)
            return carry

        lax.fori_loop(0, slot_count // 8, some, 0)
        shape = (TILE, PATCH * PATCH)
        repeat = (iota(shape, 1) % PATCH == iota(shape, 0)).astype(bf16)
        rows = jnp.dot(flat[...], repeat, preferred_element_type=f32)
        mine = iota(rows.shape, 1) // PATCH == iota(rows.shape, 0) % PATCH
        rows = jnp.where(mine, rows, 0.0).astype(bf16)
        shape = (slot_count, rows.shape[0])
        owner = (iota(shape, 1) // PATCH == iota(shape, 0)).astype(bf16)
        values = jnp.dot(owner, rows, preferred_element_type=f32)
        mean = jnp.sum(values, axis=1, keepdims=True) / (PATCH * PATCH)
        centered = values - mean
        spread = jnp.sum(centered * centered, axis=1, keepdims=True) / (PATCH * PATCH)
        normed = centered / jnp.sqrt(spread + 1e-05)
        live = iota((slot_count, 1), 0) < spots_ref[3, 0]
        last_ref[...] = jnp.where(live, normed, 0.0).astype(bf16)


def run_slab(slab, smoothed, spots, taps, w2, low, frames, high, edge, halo):
    _, frame_count, row_count, col_count = frames.shape
    slot_count = spots.shape[1]
    row_step, frame_step = 32, 4
    steps_1 = row_count // row_step
    steps_2 = frame_count // frame_step
    wide = col_count + TILE
    near = frame_count + 2 * HALF

    def row_block(at):
        return jnp.minimum(at, steps_1 - 1)

    def whole(array):
        return pl.BlockSpec(array.shape, lambda at: (0,) * array.ndim)

    operands = [spots, taps, w2, low, frames, high, edge, halo]
    in_specs = [
        pl.BlockSpec(memory_space=pltpu.SMEM),
        whole(taps),
        whole(w2),
        pl.BlockSpec((HALF, row_step, col_count), lambda at: (0, row_block(at), 0)),
        pl.BlockSpec((1, frame_count, row_step, col_count), lambda at: (slab, 0, row_block(at), 0)),
        pl.BlockSpec((HALF, row_step, col_count), lambda at: (0, row_block(at), 0)),
        pl.BlockSpec((1, near, row_step, TILE), lambda at: (slab, 0, row_block(at), 0)),
        pl.BlockSpec((1, near, 8, wide), lambda at: (slab, 0, 0, 0)),
    ]
    aliases = {}
    if smoothed is not None:
        operands.append(smoothed)
        in_specs.append(pl.BlockSpec(memory_space=pl.ANY))
        aliases = {len(operands) - 1: 0}
    count = len(operands)

    def body(*refs):
        slab_kernel(row_step, frame_step, *refs[:8], *refs[count:])

    tall = row_count + 2 * BLOCK
    return pl.pallas_call(
        body,
        grid=(steps_1 + steps_2 + 1,),
        in_specs=in_specs,
        out_specs=[
            pl.BlockSpec(
                (1, frame_step, row_count, col_count),
                lambda at: (slab, jnp.clip(at - steps_1, 0, steps_2 - 1), 0, 0),
            ),
            pl.BlockSpec((slot_count, PATCH * PATCH), lambda at: (0, 0)),
        ],
        out_shape=[
            jax.ShapeDtypeStruct(frames.shape, bf16),
            jax.ShapeDtypeStruct((slot_count, PATCH * PATCH), bf16),
        ],
        scratch_shapes=[
            pltpu.VMEM((16 * frame_count, 8 * near), bf16),
            pltpu.VMEM((frame_count, wide // TILE, tall, TILE), bf16),
            pltpu.VMEM((frame_count, wide // TILE, tall, TILE), bf16),
            pltpu.VMEM((frame_count, row_count, col_count), bf16),
            pltpu.VMEM((8, 64, TILE), f32),
            pltpu.VMEM((slot_count * PATCH, TILE), bf16),
        ],
        input_output_aliases=aliases,
        compiler_params=pltpu.CompilerParams(vmem_limit_bytes=56 * 1024 * 1024),
        cost_estimate=pl.CostEstimate(
            flops=20_000_000_000, bytes_accessed=16_000_000, transcendentals=0
        ),
        name=f"slab_{slab}",
    )(*operands)


def shards(frames, omega_taps, smooth_kernel, spots, counts):
    _, frame_count, row_count, col_count = frames.shape
    first_frame = lax.axis_index("omega") * frame_count
    first_row = lax.axis_index("row") * row_count
    first_col = lax.axis_index("col") * col_count

    rows = jnp.concatenate([frames[:, :, :REACH], frames[:, :, -REACH:]], axis=2)
    cols = jnp.concatenate([frames[..., :REACH], frames[..., -REACH:]], axis=3)
    rim = jnp.concatenate([rows, jnp.swapaxes(cols, 2, 3)], axis=3)
    send1 = (frames[1, -HALF:], frames[1, :HALF])
    later, send1, rim = lax.optimization_barrier((frames, send1, rim))
    rim = jnp.concatenate(
        [shifted(rim[:, -HALF:], "omega", 1), rim, shifted(rim[:, :HALF], "omega", -1)], axis=1
    )
    low1 = shifted(send1[0], "omega", 1)
    high1 = shifted(send1[1], "omega", -1)
    low0 = shifted(later[0, -HALF:], "omega", 1)
    high0 = shifted(later[0, :HALF], "omega", -1)
    lane = jnp.arange(TILE, dtype=jnp.int32)[None, :]
    step = jnp.arange(REACH, dtype=jnp.int32)[:, None]
    after = (lane == step).astype(bf16)
    before = (lane == TILE - REACH + step).astype(bf16)
    if lax.axis_size("col") == 2:
        first = lax.axis_index("col") == 0
        sides = jnp.where(first, rim[:, :, REACH:, col_count:], rim[:, :, :REACH, col_count:])
        sides = lax.ppermute(sides, "col", [(0, 1), (1, 0)])
        place = jnp.where(first, after, before)
    else:
        left = shifted(rim[:, :, REACH:, col_count:], "col", 1)
        right = shifted(rim[:, :, :REACH, col_count:], "col", -1)
        sides = jnp.concatenate([right, left], axis=2)
        place = jnp.concatenate([after, before], axis=0)
    edge = jnp.einsum("sfkr,kc->sfrc", sides, place, preferred_element_type=bf16)
    ends = jnp.concatenate([edge[:, :, :REACH], edge[:, :, -REACH:]], axis=2)
    line = jnp.concatenate([rim[..., :col_count], ends], axis=3)
    above = shifted(line[:, :, REACH:], "row", 1)
    below = shifted(line[:, :, :REACH], "row", -1)
    gap = jnp.zeros(above.shape[:2] + (8 - 2 * REACH, line.shape[3]), bf16)
    halo = jnp.concatenate([below, gap, above], axis=2)

    taps = omega_matrix(
        omega_taps, first_frame, frame_count, frame_count * lax.axis_size("omega")
    )
    w2 = smooth_matrix(smooth_kernel)
    base = jnp.stack([first_frame, first_row, first_col]).astype(jnp.int32)
    local = spots - base[None, :, None]
    live = jnp.broadcast_to(counts[:, :, None], (2, 1, spots.shape[2]))
    local = jnp.concatenate([local, live], axis=1)

    smoothed, second = run_slab(1, None, local[1], taps, w2, low1, frames, high1, edge, halo)
    count = lax.axis_size("row") * lax.axis_size("col")
    second = lax.ppermute(second, ("row", "col"), [(i, count - 1 - i) for i in range(count)])
    smoothed, first = run_slab(0, smoothed, local[0], taps, w2, low0, frames, high0, edge, halo)
    scores = (
        lax.dot_general(first, second, (((1,), (1,)), ((), ())), preferred_element_type=f32)
        / float(PATCH * PATCH)
    )
    return (smoothed, scores)


def solution(mesh):
    return jax.shard_map(
        shards,
        mesh=mesh,
        in_specs=(
            P(None, "omega", "row", "col"),
            P(),
            P(),
            P(None, None, ("omega", "row", "col")),
            P(None, ("omega", "row", "col")),
        ),
        out_specs=(P(None, "omega", "row", "col"), P(("omega", "row", "col"), None)),
        check_vma=False,
    )
```

```python
import jax
import jax.numpy as jnp
from jax import lax
from jax.experimental import pallas as pl
from jax.experimental.pallas import tpu as pltpu
from jax.sharding import PartitionSpec as P

TAPS = 15
HALF = TAPS // 2
PATCH = 16
SIDE = 5
REACH = SIDE // 2
TILE = 128
BLOCK = 16
bf16 = jnp.bfloat16
f32 = jnp.float32


def shifted(block, axis, step):
    count = lax.axis_size(axis)
    route = [(i, i + step) for i in range(count) if 0 <= i + step < count]
    return lax.ppermute(block, axis, route)


def split(values):
    high = lax.reduce_precision(values, 8, 7)
    return high.astype(bf16), (values - high).astype(bf16)


def omega_matrix(omega_taps, first_frame, frame_count, frame_total):
    out_ids = jnp.arange(frame_count, dtype=jnp.int32)[:, None]
    in_ids = jnp.arange(frame_count + 2 * HALF, dtype=jnp.int32)[None, :]
    source = first_frame + in_ids - HALF
    valid = (source >= 0) & (source < frame_total)
    tap = jnp.where(valid, in_ids - out_ids, -1)
    hit = tap[:, :, None] == jnp.arange(TAPS, dtype=jnp.int32)
    weights = jnp.sum(jnp.where(hit, omega_taps, 0.0), axis=2)
    norm = jnp.sum(weights, axis=1, keepdims=True)
    center = (in_ids - out_ids == HALF).astype(f32)
    matrix = center - weights / norm
    return jnp.stack(split(matrix), axis=1).reshape(2 * frame_count, matrix.shape[1])


def smooth_matrix(smooth_kernel):
    depth = 3 * BLOCK
    out_ids = jnp.arange(BLOCK, dtype=jnp.int32)[:, None]
    in_ids = jnp.arange(depth, dtype=jnp.int32)[None, :]
    step = in_ids - out_ids - (BLOCK - REACH)
    hit = step[None, :, :, None] == jnp.arange(SIDE, dtype=jnp.int32)
    table = jnp.sum(jnp.where(hit, smooth_kernel.T[:, None, None, :], 0.0), axis=3)
    high, low = split(table)
    return jnp.concatenate([high, high, low], axis=2).reshape(SIDE * BLOCK, 3 * depth)


def iota(shape, dim):
    return lax.broadcasted_iota(jnp.int32, shape, dim)


def slab_kernel(
    row_step, frame_step,
    spots_ref, taps_ref, w2_ref, low_ref, own_ref, high_ref, edge_ref, below_ref, above_ref,
    out_ref, last_ref, w1, chi, clo, kept, flat,
):
    frame_count, tiles, row_count, _ = kept.shape
    near = taps_ref.shape[1]
    steps_1 = row_count // row_step
    steps_2 = frame_count // frame_step
    at = pl.program_id(0)

    def filtered(block):
        part = block.reshape(near * 8, block.shape[2]).astype(bf16)
        both = jnp.dot(w1[...], part, preferred_element_type=f32)
        both = both.reshape(frame_count, 2, 8, block.shape[2])
        return both[:, 0] + both[:, 1]

    def keep(value, tile, place):
        high = value.astype(bf16)
        chi[:, tile, place, :] = high
        clo[:, tile, place, :] = (value - high.astype(f32)).astype(bf16)

    @pl.when(at == 0)
    def _():
        count = 2 * frame_count
        tall = (iota((8 * count, count), 0) // 8 == iota((8 * count, count), 1)).astype(bf16)
        wide = (iota((near, 8 * near), 1) // 8 == iota((near, 8 * near), 0)).astype(bf16)
        full = jnp.dot(tall, taps_ref[...], preferred_element_type=f32).astype(bf16)
        full = jnp.dot(full, wide, preferred_element_type=f32)
        same = iota(full.shape, 0) % 8 == iota(full.shape, 1) % 8
        w1[...] = jnp.where(same, full, 0.0).astype(bf16)
        for tile in range(tiles + 1):
            cols = slice(tile * TILE, tile * TILE + TILE)
            below = below_ref[0, :, :, cols].astype(f32)
            above = above_ref[0, :, :, cols].astype(f32)
            gap = jnp.zeros((near, 8 - 2 * REACH, TILE), f32)
            one = filtered(jnp.concatenate([below, gap, above], axis=1))
            two = jnp.concatenate([one, one], axis=1)
            keep(two, tile, slice(0, BLOCK))
            keep(two, tile, slice(BLOCK + row_count, 2 * BLOCK + row_count))

    @pl.when(at < steps_1)
    def _():
        for h in range(row_step // BLOCK):
            rows = slice(BLOCK * h, BLOCK * h + BLOCK)
            place = pl.ds(pl.multiple_of(BLOCK + at * row_step + BLOCK * h, BLOCK), BLOCK)
            for tile in range(0, tiles, 2):
                cols = slice(tile * TILE, (tile + 2) * TILE)
                block = jnp.concatenate(
                    [low_ref[:, rows, cols], own_ref[0, :, rows, cols], high_ref[:, rows, cols]],
                    axis=0,
                ).astype(f32)
                value = jnp.concatenate([filtered(block[:, :8]), filtered(block[:, 8:])], axis=1)
                keep(value[..., :TILE], tile, place)
                keep(value[..., TILE:], tile + 1, place)
            block = edge_ref[0, :, rows, :].astype(f32)
            value = filtered(jnp.concatenate([block[:, :8], block[:, 8:]], axis=2))
            value = jnp.concatenate([value[..., :TILE], value[..., TILE:]], axis=1)
            keep(value, tiles, place)

    @pl.when((at >= steps_1) & (at < steps_1 + steps_2))
    def _():
        lane = iota((BLOCK, TILE), 1)
        edge_of = [lane < 2, lane < 1, None, lane >= TILE - 1, lane >= TILE - 2]

        def one_frame(k, carry):
            frame = (at - steps_1) * frame_step + k
            for row in range(0, row_count, BLOCK):
                turned = {}
                order = [tiles] + list(range(tiles))
                for p in range(0, len(order), 2):
                    pair = order[p : p + 2]
                    parts = []
                    for tile in pair:
                        high = chi[frame, tile, row : row + 3 * BLOCK, :]
                        low = clo[frame, tile, row : row + 3 * BLOCK, :]
                        parts.append(jnp.concatenate([high, low, high], axis=0))
                    both = jnp.dot(
                        w2_ref[...], jnp.concatenate(parts, axis=1), preferred_element_type=f32
                    )
                    for q, tile in enumerate(pair):
                        for b in range(SIDE):
                            part = both[b * BLOCK : (b + 1) * BLOCK, q * TILE : (q + 1) * TILE]
                            if b != REACH:
                                part = pltpu.roll(part, (REACH - b) % TILE, 1)
                            turned[b, tile] = part
                for tile in range(tiles):
                    total = turned[REACH, tile]
                    for b in range(SIDE):
                        if b != REACH:
                            beside = (tile + (1 if b > REACH else -1)) % (tiles + 1)
                            total = total + jnp.where(
                                edge_of[b], turned[b, beside], turned[b, tile]
                            )
                    value = total.astype(bf16)
                    out_ref[0, k, row : row + BLOCK, tile * TILE : (tile + 1) * TILE] = value
                    kept[frame, tile, row : row + BLOCK, :] = value.astype(f32)
            return carry

        lax.fori_loop(0, frame_step, one_frame, 0)

    @pl.when(at == steps_1 + steps_2)
    def _():
        slot_count = flat.shape[0] // PATCH

        lane = iota((PATCH, TILE), 1)

        def some(i8, carry):
            for j in range(8):
                i = i8 * 8 + j
                frame, row, tile = spots_ref[0, i], spots_ref[1, i], spots_ref[2, i]
                beside, turn = spots_ref[3, i], spots_ref[4, i]
                here = kept[frame, tile, pl.ds(row, PATCH), :]
                there = kept[frame, beside, pl.ds(row, PATCH), :]
                shift = turn & (TILE - 1)
                here, there = pltpu.roll(here, shift, 1), pltpu.roll(there, shift, 1)
                part = jnp.where(lane < turn, here, there)
                flat[pl.ds(pl.multiple_of(i * PATCH, PATCH), PATCH), :] = part.astype(bf16)
            return carry

        lax.fori_loop(0, slot_count // 8, some, 0)
        low_bits = PATCH - 1
        bits = low_bits.bit_length()
        shape = (TILE, PATCH * PATCH)
        repeat = (iota(shape, 1) & low_bits == iota(shape, 0)).astype(bf16)
        rows = jnp.dot(flat[...], repeat, preferred_element_type=f32)
        mine = iota(rows.shape, 1) >> bits == iota(rows.shape, 0) & low_bits
        rows = jnp.where(mine, rows, 0.0).astype(bf16)
        shape = (slot_count, rows.shape[0])
        owner = (iota(shape, 1) >> bits == iota(shape, 0)).astype(bf16)
        values = jnp.dot(owner, rows, preferred_element_type=f32)
        mean = jnp.sum(values, axis=1, keepdims=True) / (PATCH * PATCH)
        centered = values - mean
        spread = jnp.sum(centered * centered, axis=1, keepdims=True) / (PATCH * PATCH)
        normed = centered / jnp.sqrt(spread + 1e-05)
        live = iota((slot_count, 1), 0) < spots_ref[5, 0]
        last_ref[...] = jnp.where(live, normed, 0.0).astype(bf16)


def cut_kernel(frames, rim, low1, high1, low0, high0, top, bottom, left, right, sems):
    slabs, frame_count, row_count, col_count = frames.shape
    narrow = row_count
    reads = [
        (frames.at[:, :, pl.ds(0, BLOCK), :], top),
        (frames.at[:, :, pl.ds(row_count - BLOCK, BLOCK), :], bottom),
        (frames.at[:, :, :, pl.ds(0, TILE)], left),
        (frames.at[:, :, :, pl.ds(col_count - TILE, TILE)], right),
    ]
    writes = [
        (frames.at[1, pl.ds(frame_count - HALF, HALF)], low1),
        (frames.at[1, pl.ds(0, HALF)], high1),
        (frames.at[0, pl.ds(frame_count - HALF, HALF)], low0),
        (frames.at[0, pl.ds(0, HALF)], high0),
    ]
    copies = [
        pltpu.make_async_copy(source, target, sems.at[i])
        for i, (source, target) in enumerate(reads + writes)
    ]
    for copy in copies:
        copy.start()
    for copy in copies[:4]:
        copy.wait()
    for s in range(slabs):
        rows = jnp.concatenate(
            [
                top[s, :, :8, :].astype(f32)[:, :REACH],
                bottom[s, :, BLOCK - 8 :, :].astype(f32)[:, 8 - REACH :],
            ],
            axis=1,
        )
        rim[s, :, :, :col_count] = rows.astype(bf16)
        line = iota((8, TILE), 0)
        lane = iota((8, TILE), 1)
        first = ((line == lane) & (line < REACH)).astype(bf16)
        last = ((line + TILE - 2 * REACH == lane) & (line >= REACH)).astype(bf16)
        over_lanes = (((1,), (1,)), ((), ()))
        for f in range(frame_count):
            cols = lax.dot_general(first, left[s, f], over_lanes, preferred_element_type=f32)
            cols += lax.dot_general(last, right[s, f], over_lanes, preferred_element_type=f32)
            rim[s, f, :, col_count : col_count + narrow] = cols[: 2 * REACH].astype(bf16)
    for copy in copies[4:]:
        copy.wait()


def cut(frames):
    slabs, frame_count, row_count, col_count = frames.shape
    piece = jax.ShapeDtypeStruct((HALF, row_count, col_count), bf16)
    anywhere = pl.BlockSpec(memory_space=pl.ANY)
    return pl.pallas_call(
        cut_kernel,
        in_specs=[anywhere],
        out_specs=[pl.BlockSpec(memory_space=pltpu.VMEM)] + [anywhere] * 4,
        out_shape=[
            jax.ShapeDtypeStruct((slabs, frame_count, 2 * REACH, col_count + row_count), bf16),
            piece, piece, piece, piece,
        ],
        scratch_shapes=[
            pltpu.VMEM((slabs, frame_count, BLOCK, col_count), bf16),
            pltpu.VMEM((slabs, frame_count, BLOCK, col_count), bf16),
            pltpu.VMEM((slabs, frame_count, row_count, TILE), bf16),
            pltpu.VMEM((slabs, frame_count, row_count, TILE), bf16),
            pltpu.SemaphoreType.DMA((8,)),
        ],
        compiler_params=pltpu.CompilerParams(vmem_limit_bytes=60 * 1024 * 1024),
        name="cut",
    )(frames)


def run_slab(slab, smoothed, spots, taps, w2, low, frames, high, edge, below, above):
    _, frame_count, row_count, col_count = frames.shape
    slot_count = spots.shape[1]
    row_step, frame_step = 32, 4
    steps_1 = row_count // row_step
    steps_2 = frame_count // frame_step
    wide = col_count + TILE
    near = frame_count + 2 * HALF

    def row_block(at):
        return jnp.minimum(at, steps_1 - 1)

    def whole(array):
        return pl.BlockSpec(array.shape, lambda at: (0,) * array.ndim)

    operands = [spots, taps, w2, low, frames, high, edge, below, above]
    in_specs = [
        pl.BlockSpec(memory_space=pltpu.SMEM),
        whole(taps),
        whole(w2),
        pl.BlockSpec((HALF, row_step, col_count), lambda at: (0, row_block(at), 0)),
        pl.BlockSpec((1, frame_count, row_step, col_count), lambda at: (slab, 0, row_block(at), 0)),
        pl.BlockSpec((HALF, row_step, col_count), lambda at: (0, row_block(at), 0)),
        pl.BlockSpec((1, near, row_step, TILE), lambda at: (slab, 0, row_block(at), 0)),
        pl.BlockSpec((1, near, REACH, wide), lambda at: (slab, 0, 0, 0)),
        pl.BlockSpec((1, near, REACH, wide), lambda at: (slab, 0, 0, 0)),
    ]
    aliases = {}
    if smoothed is not None:
        operands.append(smoothed)
        in_specs.append(pl.BlockSpec(memory_space=pl.ANY))
        aliases = {len(operands) - 1: 0}
    count = len(operands)

    def body(*refs):
        slab_kernel(row_step, frame_step, *refs[:9], *refs[count:])

    tall = row_count + 2 * BLOCK
    return pl.pallas_call(
        body,
        grid=(steps_1 + steps_2 + 1,),
        in_specs=in_specs,
        out_specs=[
            pl.BlockSpec(
                (1, frame_step, row_count, col_count),
                lambda at: (slab, jnp.clip(at - steps_1, 0, steps_2 - 1), 0, 0),
            ),
            pl.BlockSpec((slot_count, PATCH * PATCH), lambda at: (0, 0)),
        ],
        out_shape=[
            jax.ShapeDtypeStruct(frames.shape, bf16),
            jax.ShapeDtypeStruct((slot_count, PATCH * PATCH), bf16),
        ],
        scratch_shapes=[
            pltpu.VMEM((16 * frame_count, 8 * near), bf16),
            pltpu.VMEM((frame_count, wide // TILE, tall, TILE), bf16),
            pltpu.VMEM((frame_count, wide // TILE, tall, TILE), bf16),
            pltpu.VMEM((frame_count, col_count // TILE, row_count, TILE), f32),
            pltpu.VMEM((slot_count * PATCH, TILE), bf16),
        ],
        input_output_aliases=aliases,
        compiler_params=pltpu.CompilerParams(vmem_limit_bytes=60 * 1024 * 1024),
        cost_estimate=pl.CostEstimate(
            flops=20_000_000_000, bytes_accessed=16_000_000, transcendentals=0
        ),
        name=f"slab_{slab}",
    )(*operands)


def shards(frames, omega_taps, smooth_kernel, spots, counts):
    _, frame_count, row_count, col_count = frames.shape
    first_frame = lax.axis_index("omega") * frame_count
    first_row = lax.axis_index("row") * row_count
    first_col = lax.axis_index("col") * col_count

    rim, send_low1, send_high1, send_low0, send_high0 = cut(frames)
    rim = jnp.concatenate(
        [shifted(rim[:, -HALF:], "omega", 1), rim, shifted(rim[:, :HALF], "omega", -1)], axis=1
    )
    low1 = shifted(send_low1, "omega", 1)
    high1 = shifted(send_high1, "omega", -1)
    low0 = shifted(send_low0, "omega", 1)
    high0 = shifted(send_high0, "omega", -1)
    lane = jnp.arange(TILE, dtype=jnp.int32)[None, :]
    step = jnp.arange(REACH, dtype=jnp.int32)[:, None]
    after = (lane == step).astype(bf16)
    before = (lane == TILE - REACH + step).astype(bf16)
    if lax.axis_size("col") == 2:
        first = lax.axis_index("col") == 0
        sides = jnp.where(first, rim[:, :, REACH:, col_count:], rim[:, :, :REACH, col_count:])
        sides = lax.ppermute(sides, "col", [(0, 1), (1, 0)])
        place = jnp.where(first, after, before)
    else:
        left = shifted(rim[:, :, REACH:, col_count:], "col", 1)
        right = shifted(rim[:, :, :REACH, col_count:], "col", -1)
        sides = jnp.concatenate([right, left], axis=2)
        place = jnp.concatenate([after, before], axis=0)
    edge = jnp.einsum("sfkr,kc->sfrc", sides, place, preferred_element_type=bf16)
    ends = jnp.concatenate([edge[:, :, :REACH], edge[:, :, -REACH:]], axis=2)
    line = jnp.concatenate([rim[..., :col_count], ends], axis=3)
    above = shifted(line[:, :, REACH:], "row", 1)
    below = shifted(line[:, :, :REACH], "row", -1)

    taps = omega_matrix(
        omega_taps, first_frame, frame_count, frame_count * lax.axis_size("omega")
    )
    w2 = smooth_matrix(smooth_kernel)
    frame, row, col = spots[:, 0] - first_frame, spots[:, 1] - first_row, spots[:, 2] - first_col
    tile = col // TILE
    beside = jnp.minimum(tile + 1, col_count // TILE - 1)
    live = jnp.broadcast_to(counts, frame.shape)
    local = jnp.stack([frame, row, tile, beside, TILE - col % TILE, live], axis=1)

    smoothed, second = run_slab(1, None, local[1], taps, w2, low1, frames, high1, edge, below, above)
    count = lax.axis_size("row") * lax.axis_size("col")
    second = lax.ppermute(second, ("row", "col"), [(i, count - 1 - i) for i in range(count)])
    smoothed, first = run_slab(0, smoothed, local[0], taps, w2, low0, frames, high0, edge, below, above)
    scores = (
        lax.dot_general(first, second, (((1,), (1,)), ((), ())), preferred_element_type=f32)
        / float(PATCH * PATCH)
    )
    return (smoothed, scores)


def solution(mesh):
    return jax.shard_map(
        shards,
        mesh=mesh,
        in_specs=(
            P(None, "omega", "row", "col"),
            P(),
            P(),
            P(None, None, ("omega", "row", "col")),
            P(None, ("omega", "row", "col")),
        ),
        out_specs=(P(None, "omega", "row", "col"), P(("omega", "row", "col"), None)),
        check_vma=False,
    )
```

```python
import jax
import jax.numpy as jnp
from jax import lax
from jax.experimental import pallas as pl
from jax.experimental.pallas import tpu as pltpu
from jax.sharding import PartitionSpec as P

TAPS = 15
HALF = TAPS // 2
PATCH = 16
SIDE = 5
REACH = SIDE // 2
TILE = 128
BLOCK = 16
WINDOW = 64
EDGE = 8
bf16 = jnp.bfloat16
f32 = jnp.float32


def shifted(block, axis, step):
    count = lax.axis_size(axis)
    route = [(i, i + step) for i in range(count) if 0 <= i + step < count]
    return lax.ppermute(block, axis, route)


def split(values):
    high = lax.reduce_precision(values, 8, 7)
    return high.astype(bf16), (values - high).astype(bf16)


def omega_matrix(omega_taps, first_frame, frame_count, frame_total):
    out_ids = jnp.arange(frame_count, dtype=jnp.int32)[:, None]
    in_ids = jnp.arange(frame_count + 2 * HALF, dtype=jnp.int32)[None, :]
    source = first_frame + in_ids - HALF
    valid = (source >= 0) & (source < frame_total)
    tap = jnp.where(valid, in_ids - out_ids, -1)
    hit = tap[:, :, None] == jnp.arange(TAPS, dtype=jnp.int32)
    weights = jnp.sum(jnp.where(hit, omega_taps, 0.0), axis=2)
    norm = jnp.sum(weights, axis=1, keepdims=True)
    center = (in_ids - out_ids == HALF).astype(f32)
    matrix = center - weights / norm
    return jnp.stack(split(matrix), axis=1).reshape(2 * frame_count, matrix.shape[1])


def smooth_matrix(smooth_kernel):
    depth = WINDOW + 2 * EDGE
    out_ids = jnp.arange(WINDOW, dtype=jnp.int32)[:, None]
    in_ids = jnp.arange(depth, dtype=jnp.int32)[None, :]
    step = in_ids - out_ids - (EDGE - REACH)
    hit = step[None, :, :, None] == jnp.arange(SIDE, dtype=jnp.int32)
    table = jnp.sum(jnp.where(hit, smooth_kernel.T[:, None, None, :], 0.0), axis=3)
    table = jnp.swapaxes(table.reshape(SIDE, WINDOW // BLOCK, BLOCK, depth), 0, 1)
    high, low = split(table)
    return jnp.concatenate([high, high, low], axis=3).reshape(SIDE * WINDOW, 3 * depth)


def iota(shape, dim):
    return lax.broadcasted_iota(jnp.int32, shape, dim)


def slab_kernel(
    row_step, frame_step,
    spots_ref, taps_ref, w2_ref, low_ref, own_ref, high_ref, edge_ref, below_ref, above_ref,
    out_ref, last_ref, w1, chi, clo, carry, outer, kept, flat,
):
    frame_count, tiles, row_count, _ = kept.shape
    near = taps_ref.shape[1]
    steps_1 = row_count // row_step
    steps_2 = frame_count // frame_step
    at = pl.program_id(0)

    def filtered(block):
        part = block.reshape(near * 8, block.shape[2]).astype(bf16)
        both = jnp.dot(w1[...], part, preferred_element_type=f32)
        both = both.reshape(frame_count, 2, 8, block.shape[2])
        return both[:, 0] + both[:, 1]

    def keep(above, below, tile, place):
        value = jnp.concatenate([above, below], axis=1)
        high = value.astype(bf16)
        chi[:, tile, place, :] = high
        clo[:, tile, place, :] = (value - high.astype(f32)).astype(bf16)

    @pl.when(at == 0)
    def _():
        count = 2 * frame_count
        tall = (iota((8 * count, count), 0) // 8 == iota((8 * count, count), 1)).astype(bf16)
        wide = (iota((near, 8 * near), 1) // 8 == iota((near, 8 * near), 0)).astype(bf16)
        full = jnp.dot(tall, taps_ref[...], preferred_element_type=f32).astype(bf16)
        full = jnp.dot(full, wide, preferred_element_type=f32)
        same = iota(full.shape, 0) % 8 == iota(full.shape, 1) % 8
        w1[...] = jnp.where(same, full, 0.0).astype(bf16)
        for tile in range(tiles + 1):
            cols = slice(tile * TILE, tile * TILE + TILE)
            below = below_ref[0, :, :, cols].astype(f32)
            above = above_ref[0, :, :, cols].astype(f32)
            gap = jnp.zeros((near, 8 - 2 * REACH, TILE), f32)
            one = filtered(jnp.concatenate([below, gap, above], axis=1))
            carry[:, tile] = one
            outer[:, tile] = one

    @pl.when(at < steps_1)
    def _():
        def keep_all(tile, parts):
            parts = [carry[:, tile]] + parts
            for q in range(0, len(parts) - 1, 2):
                place = pl.ds(pl.multiple_of(at * row_step + EDGE * q, BLOCK), BLOCK)
                keep(parts[q], parts[q + 1], tile, place)
            carry[:, tile] = parts[-1]

        for tile in range(0, tiles, 2):
            cols = slice(tile * TILE, (tile + 2) * TILE)
            parts = []
            for h in range(0, row_step, BLOCK):
                rows = slice(h, h + BLOCK)
                block = jnp.concatenate(
                    [low_ref[:, rows, cols], own_ref[0, :, rows, cols], high_ref[:, rows, cols]],
                    axis=0,
                ).astype(f32)
                parts += [filtered(block[:, :EDGE]), filtered(block[:, EDGE:])]
            keep_all(tile, [part[..., :TILE] for part in parts])
            keep_all(tile + 1, [part[..., TILE:] for part in parts])
        parts = []
        for h in range(0, row_step, BLOCK):
            block = edge_ref[0, :, h : h + BLOCK, :].astype(f32)
            both = filtered(jnp.concatenate([block[:, :EDGE], block[:, EDGE:]], axis=2))
            parts += [both[..., :TILE], both[..., TILE:]]
        keep_all(tiles, parts)

    @pl.when(at == steps_1 - 1)
    def _():
        for tile in range(tiles + 1):
            keep(carry[:, tile], outer[:, tile], tile, slice(row_count, row_count + BLOCK))

    @pl.when((at >= steps_1) & (at < steps_1 + steps_2))
    def _():
        lane = iota((BLOCK, TILE), 1)
        edge_of = [lane < 2, lane < 1, None, lane >= TILE - 1, lane >= TILE - 2]

        def one_frame(k, unused):
            frame = (at - steps_1) * frame_step + k
            depth = WINDOW + 2 * EDGE
            parts_of = range(WINDOW // BLOCK)
            for row in range(0, row_count, WINDOW):
                turned = {}

                def finish(tile):
                    for m in parts_of:
                        total = turned[m, REACH, tile]
                        for b in range(SIDE):
                            if b != REACH:
                                beside = (tile + (1 if b > REACH else -1)) % (tiles + 1)
                                total = total + jnp.where(
                                    edge_of[b], turned[m, b, beside], turned[m, b, tile]
                                )
                        value = total.astype(bf16)
                        rows = slice(row + m * BLOCK, row + (m + 1) * BLOCK)
                        out_ref[0, k, rows, tile * TILE : (tile + 1) * TILE] = value
                        kept[frame, tile, rows, :] = value.astype(f32)

                order = [tiles] + list(range(tiles))
                done = 0
                for p in range(0, len(order), 2):
                    pair = order[p : p + 2]
                    stacks = []
                    for tile in pair:
                        high = chi[frame, tile, row : row + depth, :]
                        low = clo[frame, tile, row : row + depth, :]
                        stacks.append(jnp.concatenate([high, low, high], axis=0))
                    both = jnp.dot(
                        w2_ref[...], jnp.concatenate(stacks, axis=1), preferred_element_type=f32
                    )
                    for q, tile in enumerate(pair):
                        for m in parts_of:
                            for b in range(SIDE):
                                at_row = (m * SIDE + b) * BLOCK
                                part = both[at_row : at_row + BLOCK, q * TILE : (q + 1) * TILE]
                                if b != REACH:
                                    part = pltpu.roll(part, (REACH - b) % TILE, 1)
                                turned[m, b, tile] = part
                    while done < pair[-1] or (done < tiles and pair[-1] == tiles - 1):
                        finish(done)
                        done += 1
            return unused

        lax.fori_loop(0, frame_step, one_frame, 0)

    @pl.when(at == steps_1 + steps_2)
    def _():
        slot_count = flat.shape[0] // PATCH

        lane = iota((PATCH, TILE), 1)

        def some(i8, unused):
            for j in range(8):
                i = i8 * 8 + j
                frame, row, tile = spots_ref[0, i], spots_ref[1, i], spots_ref[2, i]
                beside, turn = spots_ref[3, i], spots_ref[4, i]
                here = kept[frame, tile, pl.ds(row, PATCH), :]
                there = kept[frame, beside, pl.ds(row, PATCH), :]
                shift = turn & (TILE - 1)
                here, there = pltpu.roll(here, shift, 1), pltpu.roll(there, shift, 1)
                part = jnp.where(lane < turn, here, there)
                flat[pl.ds(pl.multiple_of(i * PATCH, PATCH), PATCH), :] = part.astype(bf16)
            return unused

        lax.fori_loop(0, slot_count // 8, some, 0)
        low_bits = PATCH - 1
        bits = low_bits.bit_length()
        shape = (TILE, PATCH * PATCH)
        repeat = (iota(shape, 1) & low_bits == iota(shape, 0)).astype(bf16)
        rows = jnp.dot(flat[...], repeat, preferred_element_type=f32)
        mine = iota(rows.shape, 1) >> bits == iota(rows.shape, 0) & low_bits
        rows = jnp.where(mine, rows, 0.0).astype(bf16)
        shape = (slot_count, rows.shape[0])
        owner = (iota(shape, 1) >> bits == iota(shape, 0)).astype(bf16)
        values = jnp.dot(owner, rows, preferred_element_type=f32)
        mean = jnp.sum(values, axis=1, keepdims=True) / (PATCH * PATCH)
        centered = values - mean
        spread = jnp.sum(centered * centered, axis=1, keepdims=True) / (PATCH * PATCH)
        normed = centered / jnp.sqrt(spread + 1e-05)
        live = iota((slot_count, 1), 0) < spots_ref[5, 0]
        last_ref[...] = jnp.where(live, normed, 0.0).astype(bf16)


def cut_kernel(frames, rim, low1, high1, low0, high0, top, bottom, left, right, pieces, sems):
    slabs, frame_count, row_count, col_count = frames.shape
    narrow = row_count
    reads = [
        (frames.at[:, :, pl.ds(0, BLOCK), :], top),
        (frames.at[:, :, pl.ds(row_count - BLOCK, BLOCK), :], bottom),
        (frames.at[:, :, :, pl.ds(0, TILE)], left),
        (frames.at[:, :, :, pl.ds(col_count - TILE, TILE)], right),
    ]
    fetches = [
        (frames.at[1, pl.ds(frame_count - HALF, HALF)], pieces.at[0]),
        (frames.at[1, pl.ds(0, HALF)], pieces.at[1]),
        (frames.at[0, pl.ds(frame_count - HALF, HALF)], pieces.at[2]),
        (frames.at[0, pl.ds(0, HALF)], pieces.at[3]),
    ]
    writes = [
        (pieces.at[i], target) for i, target in enumerate([low1, high1, low0, high0])
    ]
    copies = [
        pltpu.make_async_copy(source, target, sems.at[i])
        for i, (source, target) in enumerate(reads + fetches + writes)
    ]
    for copy in copies[:8]:
        copy.start()
    for copy in copies[:4]:
        copy.wait()
    for s in range(slabs):
        rows = jnp.concatenate(
            [
                top[s, :, :8, :].astype(f32)[:, :REACH],
                bottom[s, :, BLOCK - 8 :, :].astype(f32)[:, 8 - REACH :],
            ],
            axis=1,
        )
        rim[s, :, :, :col_count] = rows.astype(bf16)
        line = iota((8, TILE), 0)
        lane = iota((8, TILE), 1)
        first = ((line == lane) & (line < REACH)).astype(bf16)
        last = ((line + TILE - 2 * REACH == lane) & (line >= REACH)).astype(bf16)
        over_lanes = (((1,), (1,)), ((), ()))
        for f in range(frame_count):
            cols = lax.dot_general(first, left[s, f], over_lanes, preferred_element_type=f32)
            cols += lax.dot_general(last, right[s, f], over_lanes, preferred_element_type=f32)
            rim[s, f, :, col_count : col_count + narrow] = cols[: 2 * REACH].astype(bf16)
    for fetch, write in zip(copies[4:8], copies[8:]):
        fetch.wait()
        write.start()
    for copy in copies[8:]:
        copy.wait()


def cut(frames):
    slabs, frame_count, row_count, col_count = frames.shape
    piece = jax.ShapeDtypeStruct((HALF, row_count, col_count), bf16)
    anywhere = pl.BlockSpec(memory_space=pl.ANY)
    return pl.pallas_call(
        cut_kernel,
        in_specs=[anywhere],
        out_specs=[pl.BlockSpec(memory_space=pltpu.VMEM)] + [anywhere] * 4,
        out_shape=[
            jax.ShapeDtypeStruct((slabs, frame_count, 2 * REACH, col_count + row_count), bf16),
            piece, piece, piece, piece,
        ],
        scratch_shapes=[
            pltpu.VMEM((slabs, frame_count, BLOCK, col_count), bf16),
            pltpu.VMEM((slabs, frame_count, BLOCK, col_count), bf16),
            pltpu.VMEM((slabs, frame_count, row_count, TILE), bf16),
            pltpu.VMEM((slabs, frame_count, row_count, TILE), bf16),
            pltpu.VMEM((4, HALF, row_count, col_count), bf16),
            pltpu.SemaphoreType.DMA((12,)),
        ],
        compiler_params=pltpu.CompilerParams(vmem_limit_bytes=60 * 1024 * 1024),
        name="cut",
    )(frames)


def run_slab(slab, smoothed, spots, taps, w2, low, frames, high, edge, below, above):
    _, frame_count, row_count, col_count = frames.shape
    slot_count = spots.shape[1]
    row_step, frame_step = 32, 4
    steps_1 = row_count // row_step
    steps_2 = frame_count // frame_step
    wide = col_count + TILE
    near = frame_count + 2 * HALF

    def row_block(at):
        return jnp.minimum(at, steps_1 - 1)

    def whole(array):
        return pl.BlockSpec(array.shape, lambda at: (0,) * array.ndim)

    operands = [spots, taps, w2, low, frames, high, edge, below, above]
    in_specs = [
        pl.BlockSpec(memory_space=pltpu.SMEM),
        whole(taps),
        whole(w2),
        pl.BlockSpec((HALF, row_step, col_count), lambda at: (0, row_block(at), 0)),
        pl.BlockSpec((1, frame_count, row_step, col_count), lambda at: (slab, 0, row_block(at), 0)),
        pl.BlockSpec((HALF, row_step, col_count), lambda at: (0, row_block(at), 0)),
        pl.BlockSpec((1, near, row_step, TILE), lambda at: (slab, 0, row_block(at), 0)),
        pl.BlockSpec((1, near, REACH, wide), lambda at: (slab, 0, 0, 0)),
        pl.BlockSpec((1, near, REACH, wide), lambda at: (slab, 0, 0, 0)),
    ]
    aliases = {}
    if smoothed is not None:
        operands.append(smoothed)
        in_specs.append(pl.BlockSpec(memory_space=pl.ANY))
        aliases = {len(operands) - 1: 0}
    count = len(operands)

    def body(*refs):
        slab_kernel(row_step, frame_step, *refs[:9], *refs[count:])

    tall = row_count + 2 * EDGE
    return pl.pallas_call(
        body,
        grid=(steps_1 + steps_2 + 1,),
        in_specs=in_specs,
        out_specs=[
            pl.BlockSpec(
                (1, frame_step, row_count, col_count),
                lambda at: (slab, jnp.clip(at - steps_1, 0, steps_2 - 1), 0, 0),
            ),
            pl.BlockSpec((slot_count, PATCH * PATCH), lambda at: (0, 0)),
        ],
        out_shape=[
            jax.ShapeDtypeStruct(frames.shape, bf16),
            jax.ShapeDtypeStruct((slot_count, PATCH * PATCH), bf16),
        ],
        scratch_shapes=[
            pltpu.VMEM((16 * frame_count, 8 * near), bf16),
            pltpu.VMEM((frame_count, wide // TILE, tall, TILE), bf16),
            pltpu.VMEM((frame_count, wide // TILE, tall, TILE), bf16),
            pltpu.VMEM((frame_count, wide // TILE, EDGE, TILE), f32),
            pltpu.VMEM((frame_count, wide // TILE, EDGE, TILE), f32),
            pltpu.VMEM((frame_count, col_count // TILE, row_count, TILE), f32),
            pltpu.VMEM((slot_count * PATCH, TILE), bf16),
        ],
        input_output_aliases=aliases,
        compiler_params=pltpu.CompilerParams(vmem_limit_bytes=60 * 1024 * 1024),
        cost_estimate=pl.CostEstimate(
            flops=20_000_000_000, bytes_accessed=16_000_000, transcendentals=0
        ),
        name=f"slab_{slab}",
    )(*operands)


def shards(frames, omega_taps, smooth_kernel, spots, counts):
    _, frame_count, row_count, col_count = frames.shape
    first_frame = lax.axis_index("omega") * frame_count
    first_row = lax.axis_index("row") * row_count
    first_col = lax.axis_index("col") * col_count

    rim, send_low1, send_high1, send_low0, send_high0 = cut(frames)
    rim = jnp.concatenate(
        [shifted(rim[:, -HALF:], "omega", 1), rim, shifted(rim[:, :HALF], "omega", -1)], axis=1
    )
    low1 = shifted(send_low1, "omega", 1)
    high1 = shifted(send_high1, "omega", -1)
    lane = jnp.arange(TILE, dtype=jnp.int32)[None, :]
    step = jnp.arange(REACH, dtype=jnp.int32)[:, None]
    after = (lane == step).astype(bf16)
    before = (lane == TILE - REACH + step).astype(bf16)
    if lax.axis_size("col") == 2:
        first = lax.axis_index("col") == 0
        sides = jnp.where(first, rim[:, :, REACH:, col_count:], rim[:, :, :REACH, col_count:])
        sides = lax.ppermute(sides, "col", [(0, 1), (1, 0)])
        place = jnp.where(first, after, before)
    else:
        left = shifted(rim[:, :, REACH:, col_count:], "col", 1)
        right = shifted(rim[:, :, :REACH, col_count:], "col", -1)
        sides = jnp.concatenate([right, left], axis=2)
        place = jnp.concatenate([after, before], axis=0)
    send_low0, send_high0, sides = lax.optimization_barrier((send_low0, send_high0, sides))
    low0 = shifted(send_low0, "omega", 1)
    high0 = shifted(send_high0, "omega", -1)
    edge = jnp.einsum("sfkr,kc->sfrc", sides, place, preferred_element_type=bf16)
    ends = jnp.concatenate([edge[:, :, :REACH], edge[:, :, -REACH:]], axis=2)
    line = jnp.concatenate([rim[..., :col_count], ends], axis=3)
    above = shifted(line[:, :, REACH:], "row", 1)
    below = shifted(line[:, :, :REACH], "row", -1)

    taps = omega_matrix(
        omega_taps, first_frame, frame_count, frame_count * lax.axis_size("omega")
    )
    w2 = smooth_matrix(smooth_kernel)
    frame, row, col = spots[:, 0] - first_frame, spots[:, 1] - first_row, spots[:, 2] - first_col
    tile = col // TILE
    beside = jnp.minimum(tile + 1, col_count // TILE - 1)
    live = jnp.broadcast_to(counts, frame.shape)
    local = jnp.stack([frame, row, tile, beside, TILE - col % TILE, live], axis=1)

    smoothed, second = run_slab(1, None, local[1], taps, w2, low1, frames, high1, edge, below, above)
    count = lax.axis_size("row") * lax.axis_size("col")
    second = lax.ppermute(second, ("row", "col"), [(i, count - 1 - i) for i in range(count)])
    smoothed, first = run_slab(0, smoothed, local[0], taps, w2, low0, frames, high0, edge, below, above)
    scores = (
        lax.dot_general(first, second, (((1,), (1,)), ((), ())), preferred_element_type=f32)
        / float(PATCH * PATCH)
    )
    return (smoothed, scores)


def solution(mesh):
    return jax.shard_map(
        shards,
        mesh=mesh,
        in_specs=(
            P(None, "omega", "row", "col"),
            P(),
            P(),
            P(None, None, ("omega", "row", "col")),
            P(None, ("omega", "row", "col")),
        ),
        out_specs=(P(None, "omega", "row", "col"), P(("omega", "row", "col"), None)),
        check_vma=False,
    )
```

```python
import jax
import jax.numpy as jnp
from jax import lax
from jax.experimental import pallas as pl
from jax.experimental.pallas import tpu as pltpu
from jax.sharding import PartitionSpec as P

TAPS = 15
HALF = TAPS // 2
PATCH = 16
SIDE = 5
REACH = SIDE // 2
TILE = 128
BLOCK = 16
WINDOW = 64
EDGE = 8
bf16 = jnp.bfloat16
f32 = jnp.float32


def shifted(block, axis, step):
    count = lax.axis_size(axis)
    route = [(i, i + step) for i in range(count) if 0 <= i + step < count]
    return lax.ppermute(block, axis, route)


def split(values):
    high = lax.reduce_precision(values, 8, 7)
    return high.astype(bf16), (values - high).astype(bf16)


def omega_matrix(omega_taps, first_frame, frame_count, frame_total):
    out_ids = jnp.arange(frame_count, dtype=jnp.int32)[:, None]
    in_ids = jnp.arange(frame_count + 2 * HALF, dtype=jnp.int32)[None, :]
    source = first_frame + in_ids - HALF
    valid = (source >= 0) & (source < frame_total)
    tap = jnp.where(valid, in_ids - out_ids, -1)
    hit = tap[:, :, None] == jnp.arange(TAPS, dtype=jnp.int32)
    weights = jnp.sum(jnp.where(hit, omega_taps, 0.0), axis=2)
    norm = jnp.sum(weights, axis=1, keepdims=True)
    center = (in_ids - out_ids == HALF).astype(f32)
    matrix = center - weights / norm
    return jnp.stack(split(matrix), axis=1).reshape(2 * frame_count, matrix.shape[1])


def smooth_matrix(smooth_kernel):
    depth = WINDOW + 2 * EDGE
    out_ids = jnp.arange(WINDOW, dtype=jnp.int32)[:, None]
    in_ids = jnp.arange(depth, dtype=jnp.int32)[None, :]
    step = in_ids - out_ids - (EDGE - REACH)
    hit = step[None, :, :, None] == jnp.arange(SIDE, dtype=jnp.int32)
    table = jnp.sum(jnp.where(hit, smooth_kernel.T[:, None, None, :], 0.0), axis=3)
    table = jnp.swapaxes(table.reshape(SIDE, WINDOW // BLOCK, BLOCK, depth), 0, 1)
    high, low = split(table)
    return jnp.concatenate([high, high, low], axis=3).reshape(SIDE * WINDOW, 3 * depth)


def iota(shape, dim):
    return lax.broadcasted_iota(jnp.int32, shape, dim)


def slab_kernel(
    row_step, frame_step,
    spots_ref, taps_ref, w2_ref, low_ref, own_ref, high_ref, edge_ref, below_ref, above_ref,
    out_ref, last_ref, w1, chi, clo, carry, outer, kept, flat,
):
    frame_count, tiles, row_count, _ = kept.shape
    near = taps_ref.shape[1]
    steps_1 = row_count // row_step
    steps_2 = frame_count // frame_step
    at = pl.program_id(0)

    def filtered(block):
        part = block.reshape(near * BLOCK, block.shape[2])
        both = jnp.dot(w1[...], part, preferred_element_type=f32)
        both = both.reshape(frame_count, 2, BLOCK, block.shape[2])
        both = both[:, 0] + both[:, 1]
        return [both[:, :EDGE], both[:, EDGE:]]

    def keep(above, below, tile, place):
        value = jnp.concatenate([above, below], axis=1)
        high = value.astype(bf16)
        chi[:, tile, place, :] = high
        clo[:, tile, place, :] = (value - high.astype(f32)).astype(bf16)

    @pl.when(at == 0)
    def _():
        count = 2 * frame_count
        bits = BLOCK.bit_length() - 1
        shape = (BLOCK * count, count)
        tall = (iota(shape, 0) >> bits == iota(shape, 1)).astype(bf16)
        shape = (near, BLOCK * near)
        wide = (iota(shape, 1) >> bits == iota(shape, 0)).astype(bf16)
        full = jnp.dot(tall, taps_ref[...], preferred_element_type=f32).astype(bf16)
        full = jnp.dot(full, wide, preferred_element_type=f32)
        same = iota(full.shape, 0) & (BLOCK - 1) == iota(full.shape, 1) & (BLOCK - 1)
        w1[...] = jnp.where(same, full, 0.0).astype(bf16)
        for tile in range(tiles + 1):
            cols = slice(tile * TILE, tile * TILE + TILE)
            below = below_ref[0, :, :, cols].astype(f32)
            above = above_ref[0, :, :, cols].astype(f32)
            gap = jnp.zeros((near, BLOCK - 2 * REACH, TILE), f32)
            block = jnp.concatenate([below, gap, above], axis=1).astype(bf16)
            outer[:, tile], carry[:, tile] = filtered(block)

    @pl.when(at < steps_1)
    def _():
        def keep_all(tile, parts):
            parts = [carry[:, tile]] + parts
            for q in range(0, len(parts) - 1, 2):
                place = pl.ds(pl.multiple_of(at * row_step + EDGE * q, BLOCK), BLOCK)
                keep(parts[q], parts[q + 1], tile, place)
            carry[:, tile] = parts[-1]

        for tile in range(0, tiles, 2):
            cols = slice(tile * TILE, (tile + 2) * TILE)
            parts = []
            for h in range(0, row_step, BLOCK):
                rows = slice(h, h + BLOCK)
                block = jnp.concatenate(
                    [low_ref[:, rows, cols], own_ref[0, :, rows, cols], high_ref[:, rows, cols]],
                    axis=0,
                )
                parts += filtered(block)
            keep_all(tile, [part[..., :TILE] for part in parts])
            keep_all(tile + 1, [part[..., TILE:] for part in parts])
        both = jnp.concatenate(
            [edge_ref[0, :, h : h + BLOCK, :] for h in range(0, row_step, BLOCK)], axis=2
        )
        parts = []
        upper, lower = filtered(both)
        for q in range(row_step // BLOCK):
            parts += [part[..., q * TILE : (q + 1) * TILE] for part in (upper, lower)]
        keep_all(tiles, parts)

    @pl.when(at == steps_1 - 1)
    def _():
        for tile in range(tiles + 1):
            keep(carry[:, tile], outer[:, tile], tile, slice(row_count, row_count + BLOCK))

    @pl.when((at >= steps_1) & (at < steps_1 + steps_2))
    def _():
        lane = iota((BLOCK, TILE), 1)
        edge_of = [lane < 2, lane < 1, None, lane >= TILE - 1, lane >= TILE - 2]

        def one_frame(k, unused):
            frame = (at - steps_1) * frame_step + k
            depth = WINDOW + 2 * EDGE
            parts_of = range(WINDOW // BLOCK)
            for row in range(0, row_count, WINDOW):
                turned = {}

                def finish(tile):
                    for m in parts_of:
                        total = turned[m, REACH, tile]
                        for b in range(SIDE):
                            if b != REACH:
                                beside = (tile + (1 if b > REACH else -1)) % (tiles + 1)
                                total = total + jnp.where(
                                    edge_of[b], turned[m, b, beside], turned[m, b, tile]
                                )
                        value = total.astype(bf16)
                        rows = slice(row + m * BLOCK, row + (m + 1) * BLOCK)
                        out_ref[0, k, rows, tile * TILE : (tile + 1) * TILE] = value
                        kept[frame, tile, rows, :] = value.astype(f32)

                order = [tiles] + list(range(tiles))
                done = 0
                for p in range(0, len(order), 2):
                    pair = order[p : p + 2]
                    stacks = []
                    for tile in pair:
                        high = chi[frame, tile, row : row + depth, :]
                        low = clo[frame, tile, row : row + depth, :]
                        stacks.append(jnp.concatenate([high, low, high], axis=0))
                    both = jnp.dot(
                        w2_ref[...], jnp.concatenate(stacks, axis=1), preferred_element_type=f32
                    )
                    for q, tile in enumerate(pair):
                        for m in parts_of:
                            for b in range(SIDE):
                                at_row = (m * SIDE + b) * BLOCK
                                part = both[at_row : at_row + BLOCK, q * TILE : (q + 1) * TILE]
                                if b != REACH:
                                    part = pltpu.roll(part, (REACH - b) % TILE, 1)
                                turned[m, b, tile] = part
                    while done < pair[-1] or (done < tiles and pair[-1] == tiles - 1):
                        finish(done)
                        done += 1
            return unused

        lax.fori_loop(0, frame_step, one_frame, 0)

    @pl.when(at == steps_1 + steps_2)
    def _():
        slot_count = flat.shape[0] // PATCH

        lane = iota((PATCH, TILE), 1)

        def some(i8, unused):
            for j in range(8):
                i = i8 * 8 + j
                frame, row, tile = spots_ref[0, i], spots_ref[1, i], spots_ref[2, i]
                beside, turn = spots_ref[3, i], spots_ref[4, i]
                here = kept[frame, tile, pl.ds(row, PATCH), :]
                there = kept[frame, beside, pl.ds(row, PATCH), :]
                shift = turn & (TILE - 1)
                here, there = pltpu.roll(here, shift, 1), pltpu.roll(there, shift, 1)
                part = jnp.where(lane < turn, here, there)
                flat[pl.ds(pl.multiple_of(i * PATCH, PATCH), PATCH), :] = part.astype(bf16)
            return unused

        lax.fori_loop(0, slot_count // 8, some, 0)
        low_bits = PATCH - 1
        bits = low_bits.bit_length()
        shape = (TILE, PATCH * PATCH)
        repeat = (iota(shape, 1) & low_bits == iota(shape, 0)).astype(bf16)
        rows = jnp.dot(flat[...], repeat, preferred_element_type=f32)
        mine = iota(rows.shape, 1) >> bits == iota(rows.shape, 0) & low_bits
        rows = jnp.where(mine, rows, 0.0).astype(bf16)
        shape = (slot_count, rows.shape[0])
        owner = (iota(shape, 1) >> bits == iota(shape, 0)).astype(bf16)
        values = jnp.dot(owner, rows, preferred_element_type=f32)
        mean = jnp.sum(values, axis=1, keepdims=True) / (PATCH * PATCH)
        centered = values - mean
        spread = jnp.sum(centered * centered, axis=1, keepdims=True) / (PATCH * PATCH)
        normed = centered / jnp.sqrt(spread + 1e-05)
        live = iota((slot_count, 1), 0) < spots_ref[5, 0]
        last_ref[...] = jnp.where(live, normed, 0.0).astype(bf16)


def cut_kernel(frames, rim, low1, high1, low0, high0, top, bottom, left, right, pieces, sems):
    slabs, frame_count, row_count, col_count = frames.shape
    narrow = row_count
    reads = [
        (frames.at[:, :, pl.ds(0, BLOCK), :], top),
        (frames.at[:, :, pl.ds(row_count - BLOCK, BLOCK), :], bottom),
        (frames.at[:, :, :, pl.ds(0, TILE)], left),
        (frames.at[:, :, :, pl.ds(col_count - TILE, TILE)], right),
    ]
    fetches = [
        (frames.at[1, pl.ds(frame_count - HALF, HALF)], pieces.at[0]),
        (frames.at[1, pl.ds(0, HALF)], pieces.at[1]),
        (frames.at[0, pl.ds(frame_count - HALF, HALF)], pieces.at[2]),
        (frames.at[0, pl.ds(0, HALF)], pieces.at[3]),
    ]
    writes = [
        (pieces.at[i], target) for i, target in enumerate([low1, high1, low0, high0])
    ]
    copies = [
        pltpu.make_async_copy(source, target, sems.at[i])
        for i, (source, target) in enumerate(reads + fetches + writes)
    ]
    for copy in copies[:8]:
        copy.start()
    for copy in copies[:4]:
        copy.wait()
    for s in range(slabs):
        rows = jnp.concatenate(
            [
                top[s, :, :8, :].astype(f32)[:, :REACH],
                bottom[s, :, BLOCK - 8 :, :].astype(f32)[:, 8 - REACH :],
            ],
            axis=1,
        )
        rim[s, :, :, :col_count] = rows.astype(bf16)
        line = iota((8, TILE), 0)
        lane = iota((8, TILE), 1)
        first = ((line == lane) & (line < REACH)).astype(bf16)
        last = ((line + TILE - 2 * REACH == lane) & (line >= REACH)).astype(bf16)
        over_lanes = (((1,), (1,)), ((), ()))
        for f in range(frame_count):
            cols = lax.dot_general(first, left[s, f], over_lanes, preferred_element_type=f32)
            cols += lax.dot_general(last, right[s, f], over_lanes, preferred_element_type=f32)
            rim[s, f, :, col_count : col_count + narrow] = cols[: 2 * REACH].astype(bf16)
    for fetch, write in zip(copies[4:8], copies[8:]):
        fetch.wait()
        write.start()
    for copy in copies[8:]:
        copy.wait()


def cut(frames):
    slabs, frame_count, row_count, col_count = frames.shape
    piece = jax.ShapeDtypeStruct((HALF, row_count, col_count), bf16)
    anywhere = pl.BlockSpec(memory_space=pl.ANY)
    return pl.pallas_call(
        cut_kernel,
        in_specs=[anywhere],
        out_specs=[pl.BlockSpec(memory_space=pltpu.VMEM)] + [anywhere] * 4,
        out_shape=[
            jax.ShapeDtypeStruct((slabs, frame_count, 2 * REACH, col_count + row_count), bf16),
            piece, piece, piece, piece,
        ],
        scratch_shapes=[
            pltpu.VMEM((slabs, frame_count, BLOCK, col_count), bf16),
            pltpu.VMEM((slabs, frame_count, BLOCK, col_count), bf16),
            pltpu.VMEM((slabs, frame_count, row_count, TILE), bf16),
            pltpu.VMEM((slabs, frame_count, row_count, TILE), bf16),
            pltpu.VMEM((4, HALF, row_count, col_count), bf16),
            pltpu.SemaphoreType.DMA((12,)),
        ],
        compiler_params=pltpu.CompilerParams(vmem_limit_bytes=60 * 1024 * 1024),
        name="cut",
    )(frames)


def run_slab(slab, smoothed, spots, taps, w2, low, frames, high, edge, below, above):
    _, frame_count, row_count, col_count = frames.shape
    slot_count = spots.shape[1]
    row_step, frame_step = 32, 4
    steps_1 = row_count // row_step
    steps_2 = frame_count // frame_step
    wide = col_count + TILE
    near = frame_count + 2 * HALF

    def row_block(at):
        return jnp.minimum(at, steps_1 - 1)

    def whole(array):
        return pl.BlockSpec(array.shape, lambda at: (0,) * array.ndim)

    operands = [spots, taps, w2, low, frames, high, edge, below, above]
    in_specs = [
        pl.BlockSpec(memory_space=pltpu.SMEM),
        whole(taps),
        whole(w2),
        pl.BlockSpec((HALF, row_step, col_count), lambda at: (0, row_block(at), 0)),
        pl.BlockSpec((1, frame_count, row_step, col_count), lambda at: (slab, 0, row_block(at), 0)),
        pl.BlockSpec((HALF, row_step, col_count), lambda at: (0, row_block(at), 0)),
        pl.BlockSpec((1, near, row_step, TILE), lambda at: (slab, 0, row_block(at), 0)),
        pl.BlockSpec((1, near, REACH, wide), lambda at: (slab, 0, 0, 0)),
        pl.BlockSpec((1, near, REACH, wide), lambda at: (slab, 0, 0, 0)),
    ]
    aliases = {}
    if smoothed is not None:
        operands.append(smoothed)
        in_specs.append(pl.BlockSpec(memory_space=pl.ANY))
        aliases = {len(operands) - 1: 0}
    count = len(operands)

    def body(*refs):
        slab_kernel(row_step, frame_step, *refs[:9], *refs[count:])

    tall = row_count + 2 * EDGE
    return pl.pallas_call(
        body,
        grid=(steps_1 + steps_2 + 1,),
        in_specs=in_specs,
        out_specs=[
            pl.BlockSpec(
                (1, frame_step, row_count, col_count),
                lambda at: (slab, jnp.clip(at - steps_1, 0, steps_2 - 1), 0, 0),
            ),
            pl.BlockSpec((slot_count, PATCH * PATCH), lambda at: (0, 0)),
        ],
        out_shape=[
            jax.ShapeDtypeStruct(frames.shape, bf16),
            jax.ShapeDtypeStruct((slot_count, PATCH * PATCH), bf16),
        ],
        scratch_shapes=[
            pltpu.VMEM((2 * BLOCK * frame_count, BLOCK * near), bf16),
            pltpu.VMEM((frame_count, wide // TILE, tall, TILE), bf16),
            pltpu.VMEM((frame_count, wide // TILE, tall, TILE), bf16),
            pltpu.VMEM((frame_count, wide // TILE, EDGE, TILE), f32),
            pltpu.VMEM((frame_count, wide // TILE, EDGE, TILE), f32),
            pltpu.VMEM((frame_count, col_count // TILE, row_count, TILE), f32),
            pltpu.VMEM((slot_count * PATCH, TILE), bf16),
        ],
        input_output_aliases=aliases,
        compiler_params=pltpu.CompilerParams(vmem_limit_bytes=60 * 1024 * 1024),
        cost_estimate=pl.CostEstimate(
            flops=20_000_000_000, bytes_accessed=16_000_000, transcendentals=0
        ),
        name=f"slab_{slab}",
    )(*operands)


def shards(frames, omega_taps, smooth_kernel, spots, counts):
    _, frame_count, row_count, col_count = frames.shape
    first_frame = lax.axis_index("omega") * frame_count
    first_row = lax.axis_index("row") * row_count
    first_col = lax.axis_index("col") * col_count

    rim, send_low1, send_high1, send_low0, send_high0 = cut(frames)
    rim = jnp.concatenate(
        [shifted(rim[:, -HALF:], "omega", 1), rim, shifted(rim[:, :HALF], "omega", -1)], axis=1
    )
    low1 = shifted(send_low1, "omega", 1)
    high1 = shifted(send_high1, "omega", -1)
    lane = jnp.arange(TILE, dtype=jnp.int32)[None, :]
    step = jnp.arange(REACH, dtype=jnp.int32)[:, None]
    after = (lane == step).astype(bf16)
    before = (lane == TILE - REACH + step).astype(bf16)
    if lax.axis_size("col") == 2:
        first = lax.axis_index("col") == 0
        sides = jnp.where(first, rim[:, :, REACH:, col_count:], rim[:, :, :REACH, col_count:])
        sides = lax.ppermute(sides, "col", [(0, 1), (1, 0)])
        place = jnp.where(first, after, before)
    else:
        left = shifted(rim[:, :, REACH:, col_count:], "col", 1)
        right = shifted(rim[:, :, :REACH, col_count:], "col", -1)
        sides = jnp.concatenate([right, left], axis=2)
        place = jnp.concatenate([after, before], axis=0)
    send_low0, send_high0, sides = lax.optimization_barrier((send_low0, send_high0, sides))
    low0 = shifted(send_low0, "omega", 1)
    high0 = shifted(send_high0, "omega", -1)
    edge = jnp.einsum("sfkr,kc->sfrc", sides, place, preferred_element_type=bf16)
    ends = jnp.concatenate([edge[:, :, :REACH], edge[:, :, -REACH:]], axis=2)
    line = jnp.concatenate([rim[..., :col_count], ends], axis=3)
    above = shifted(line[:, :, REACH:], "row", 1)
    below = shifted(line[:, :, :REACH], "row", -1)

    taps = omega_matrix(
        omega_taps, first_frame, frame_count, frame_count * lax.axis_size("omega")
    )
    w2 = smooth_matrix(smooth_kernel)
    frame, row, col = spots[:, 0] - first_frame, spots[:, 1] - first_row, spots[:, 2] - first_col
    tile = col // TILE
    beside = jnp.minimum(tile + 1, col_count // TILE - 1)
    live = jnp.broadcast_to(counts, frame.shape)
    local = jnp.stack([frame, row, tile, beside, TILE - col % TILE, live], axis=1)

    smoothed, second = run_slab(1, None, local[1], taps, w2, low1, frames, high1, edge, below, above)
    second = lax.all_gather(second, ("row", "col"))
    mirror = second.shape[0] - 1 - lax.axis_index(("row", "col"))
    second = lax.dynamic_index_in_dim(second, mirror, keepdims=False)
    smoothed, first = run_slab(0, smoothed, local[0], taps, w2, low0, frames, high0, edge, below, above)
    scores = (
        lax.dot_general(first, second, (((1,), (1,)), ((), ())), preferred_element_type=f32)
        / float(PATCH * PATCH)
    )
    return (smoothed, scores)


def solution(mesh):
    return jax.shard_map(
        shards,
        mesh=mesh,
        in_specs=(
            P(None, "omega", "row", "col"),
            P(),
            P(),
            P(None, None, ("omega", "row", "col")),
            P(None, ("omega", "row", "col")),
        ),
        out_specs=(P(None, "omega", "row", "col"), P(("omega", "row", "col"), None)),
        check_vma=False,
    )
```

```python
import functools
import jax
import jax.numpy as jnp
from jax import lax
from jax.experimental import pallas as pl
from jax.experimental.pallas import tpu as pltpu
from jax.sharding import PartitionSpec as P

TAPS = 15
HALF = TAPS // 2
PATCH = 16
SIDE = 5
REACH = SIDE // 2
TILE = 128
BLOCK = 16
WINDOW = 32
EDGE = 8
bf16 = jnp.bfloat16
f32 = jnp.float32


def shifted(block, axis, step):
    count = lax.axis_size(axis)
    route = [(i, i + step) for i in range(count) if 0 <= i + step < count]
    return lax.ppermute(block, axis, route)


def split(values):
    high = lax.reduce_precision(values, 8, 7)
    return high.astype(bf16), (values - high).astype(bf16)


def omega_matrix(omega_taps, first_frame, frame_count, frame_total):
    out_ids = jnp.arange(frame_count, dtype=jnp.int32)[:, None]
    in_ids = jnp.arange(frame_count + 2 * HALF, dtype=jnp.int32)[None, :]
    source = first_frame + in_ids - HALF
    valid = (source >= 0) & (source < frame_total)
    tap = jnp.where(valid, in_ids - out_ids, -1)
    hit = tap[:, :, None] == jnp.arange(TAPS, dtype=jnp.int32)
    weights = jnp.sum(jnp.where(hit, omega_taps, 0.0), axis=2)
    norm = jnp.sum(weights, axis=1, keepdims=True)
    center = (in_ids - out_ids == HALF).astype(f32)
    matrix = center - weights / norm
    return jnp.stack(split(matrix), axis=1).reshape(2 * frame_count, matrix.shape[1])


def smooth_matrix(smooth_kernel):
    depth = WINDOW + 2 * EDGE
    out_ids = jnp.arange(WINDOW, dtype=jnp.int32)[:, None]
    in_ids = jnp.arange(depth, dtype=jnp.int32)[None, :]
    step = in_ids - out_ids - (EDGE - REACH)
    hit = step[None, :, :, None] == jnp.arange(SIDE, dtype=jnp.int32)
    table = jnp.sum(jnp.where(hit, smooth_kernel.T[:, None, None, :], 0.0), axis=3)
    table = jnp.swapaxes(table.reshape(SIDE, WINDOW // BLOCK, BLOCK, depth), 0, 1)
    high, low = split(table)
    return jnp.concatenate([high, high, low], axis=3).reshape(SIDE * WINDOW, 3 * depth)


def iota(shape, dim):
    return lax.broadcasted_iota(jnp.int32, shape, dim)


def slab_kernel(
    row_step, frame_step,
    spots_ref, taps_ref, w2_ref, low_ref, own_ref, high_ref, edge_ref, below_ref, above_ref,
    out_ref, last_ref, w1, chi, clo, carry, outer, kept, flat,
):
    frame_count, tiles, row_count, _ = kept.shape
    near = taps_ref.shape[1]
    steps_1 = row_count // row_step
    steps_2 = frame_count // frame_step
    at = pl.program_id(0)

    def filtered(block):
        part = block.reshape(near * 8, block.shape[2]).astype(bf16)
        both = jnp.dot(w1[...], part, preferred_element_type=f32)
        both = both.reshape(frame_count, 2, 8, block.shape[2])
        return both[:, 0] + both[:, 1]

    def keep(above, below, tile, place):
        value = jnp.concatenate([above, below], axis=1)
        high = value.astype(bf16)
        chi[:, tile, place, :] = high
        clo[:, tile, place, :] = (value - high.astype(f32)).astype(bf16)

    @pl.when(at == 0)
    def _():
        count = 2 * frame_count
        tall = (iota((8 * count, count), 0) // 8 == iota((8 * count, count), 1)).astype(bf16)
        wide = (iota((near, 8 * near), 1) // 8 == iota((near, 8 * near), 0)).astype(bf16)
        full = jnp.dot(tall, taps_ref[...], preferred_element_type=f32).astype(bf16)
        full = jnp.dot(full, wide, preferred_element_type=f32)
        same = iota(full.shape, 0) % 8 == iota(full.shape, 1) % 8
        w1[...] = jnp.where(same, full, 0.0).astype(bf16)
        for tile in range(0, tiles + 1, 2):
            pair = range(tile, min(tile + 2, tiles + 1))
            cols = slice(tile * TILE, (tile + len(pair)) * TILE)
            below = below_ref[0, :, :, cols].astype(f32)
            above = above_ref[0, :, :, cols].astype(f32)
            gap = jnp.zeros((near, 8 - 2 * REACH, below.shape[2]), f32)
            both = filtered(jnp.concatenate([below, gap, above], axis=1))
            for q, one in enumerate(pair):
                carry[:, one] = both[..., q * TILE : (q + 1) * TILE]
                outer[:, one] = both[..., q * TILE : (q + 1) * TILE]

    @pl.when(at < steps_1)
    def _():
        def keep_all(tile, parts):
            parts = [carry[:, tile]] + parts
            for q in range(0, len(parts) - 1, 2):
                place = pl.ds(pl.multiple_of(at * row_step + EDGE * q, BLOCK), BLOCK)
                keep(parts[q], parts[q + 1], tile, place)
            carry[:, tile] = parts[-1]

        for tile in range(0, tiles, 2):
            cols = slice(tile * TILE, (tile + 2) * TILE)
            parts = []
            for h in range(0, row_step, BLOCK):
                rows = slice(h, h + BLOCK)
                block = jnp.concatenate(
                    [low_ref[:, rows, cols], own_ref[0, :, rows, cols], high_ref[:, rows, cols]],
                    axis=0,
                ).astype(f32)
                parts += [filtered(block[:, :EDGE]), filtered(block[:, EDGE:])]
            keep_all(tile, [part[..., :TILE] for part in parts])
            keep_all(tile + 1, [part[..., TILE:] for part in parts])
        parts = []
        for h in range(0, row_step, BLOCK):
            block = edge_ref[0, :, h : h + BLOCK, :].astype(f32)
            both = filtered(jnp.concatenate([block[:, :EDGE], block[:, EDGE:]], axis=2))
            parts += [both[..., :TILE], both[..., TILE:]]
        keep_all(tiles, parts)

    @pl.when(at == steps_1 - 1)
    def _():
        for tile in range(tiles + 1):
            keep(carry[:, tile], outer[:, tile], tile, slice(row_count, row_count + BLOCK))

    @pl.when((at >= steps_1) & (at < steps_1 + steps_2))
    def _():
        lane = iota((BLOCK, TILE), 1)
        edge_of = [lane < 2, lane < 1, None, lane >= TILE - 1, lane >= TILE - 2]

        depth = WINDOW + 2 * EDGE
        parts_of = range(WINDOW // BLOCK)

        def two_frames(k2, unused):
            for row in range(0, row_count, WINDOW):
                turned = {}
                done = [0, 0]

                def finish(f, tile):
                    k = k2 * 2 + f
                    frame = (at - steps_1) * frame_step + k
                    for m in parts_of:
                        total = turned[f, m, REACH, tile]
                        for b in range(SIDE):
                            if b != REACH:
                                beside = (tile + (1 if b > REACH else -1)) % (tiles + 1)
                                total = total + jnp.where(
                                    edge_of[b], turned[f, m, b, beside], turned[f, m, b, tile]
                                )
                        value = total.astype(bf16)
                        rows = slice(row + m * BLOCK, row + (m + 1) * BLOCK)
                        out_ref[0, k, rows, tile * TILE : (tile + 1) * TILE] = value
                        kept[frame, tile, rows, :] = value.astype(f32)

                order = [(f, tile) for f in range(2) for tile in [tiles] + list(range(tiles))]
                for p in range(0, len(order), 2):
                    pair = order[p : p + 2]
                    stacks = []
                    for f, tile in pair:
                        frame = (at - steps_1) * frame_step + k2 * 2 + f
                        high = chi[frame, tile, row : row + depth, :]
                        low = clo[frame, tile, row : row + depth, :]
                        stacks.append(jnp.concatenate([high, low, high], axis=0))
                    both = jnp.dot(
                        w2_ref[...], jnp.concatenate(stacks, axis=1), preferred_element_type=f32
                    )
                    for q, (f, tile) in enumerate(pair):
                        for m in parts_of:
                            for b in range(SIDE):
                                at_row = (m * SIDE + b) * BLOCK
                                part = both[at_row : at_row + BLOCK, q * TILE : (q + 1) * TILE]
                                if b != REACH:
                                    part = pltpu.roll(part, (REACH - b) % TILE, 1)
                                turned[f, m, b, tile] = part
                    for f in range(2):
                        while done[f] < tiles and (f, 0, 0, done[f]) in turned:
                            after = min(done[f] + 1, tiles)
                            if (f, 0, 0, after) not in turned:
                                break
                            finish(f, done[f])
                            done[f] += 1
            return unused

        lax.fori_loop(0, frame_step // 2, two_frames, 0)

    @pl.when(at == steps_1 + steps_2)
    def _():
        slot_count = flat.shape[0] // PATCH

        lane = iota((PATCH, TILE), 1)

        def some(i8, unused):
            for j in range(8):
                i = i8 * 8 + j
                frame, row, tile = spots_ref[0, i], spots_ref[1, i], spots_ref[2, i]
                beside, turn = spots_ref[3, i], spots_ref[4, i]
                here = kept[frame, tile, pl.ds(row, PATCH), :]
                there = kept[frame, beside, pl.ds(row, PATCH), :]
                shift = turn & (TILE - 1)
                here, there = pltpu.roll(here, shift, 1), pltpu.roll(there, shift, 1)
                part = jnp.where(lane < turn, here, there)
                flat[pl.ds(pl.multiple_of(i * PATCH, PATCH), PATCH), :] = part.astype(bf16)
            return unused

        lax.fori_loop(0, slot_count // 8, some, 0)
        low_bits = PATCH - 1
        bits = low_bits.bit_length()
        shape = (TILE, PATCH * PATCH)
        repeat = (iota(shape, 1) & low_bits == iota(shape, 0)).astype(bf16)
        rows = jnp.dot(flat[...], repeat, preferred_element_type=f32)
        mine = iota(rows.shape, 1) >> bits == iota(rows.shape, 0) & low_bits
        rows = jnp.where(mine, rows, 0.0).astype(bf16)
        shape = (slot_count, rows.shape[0])
        owner = (iota(shape, 1) >> bits == iota(shape, 0)).astype(bf16)
        values = jnp.dot(owner, rows, preferred_element_type=f32)
        mean = jnp.sum(values, axis=1, keepdims=True) / (PATCH * PATCH)
        centered = values - mean
        spread = jnp.sum(centered * centered, axis=1, keepdims=True) / (PATCH * PATCH)
        normed = centered / jnp.sqrt(spread + 1e-05)
        live = iota((slot_count, 1), 0) < spots_ref[5, 0]
        last_ref[...] = jnp.where(live, normed, 0.0).astype(bf16)


def cut_kernel(slab, frames, *refs):
    if slab == 0:
        other, refs = refs[0], refs[1:]
        rim, send_low, send_high, low, high, whole, sems = refs
    else:
        rim, low, high, whole, sems = refs
    frame_count, row_count, col_count = whole.shape
    first, last = pl.ds(0, HALF), pl.ds(frame_count - HALF, HALF)
    middle = frame_count - HALF
    fetches = [
        pltpu.make_async_copy(frames.at[slab, part], whole.at[part], sems.at[i])
        for i, part in enumerate([pl.ds(0, middle), pl.ds(middle, HALF)])
    ]
    writes = [
        pltpu.make_async_copy(whole.at[first], high, sems.at[2]),
        pltpu.make_async_copy(whole.at[last], low, sems.at[3]),
    ]
    for fetch in fetches:
        fetch.start()
    for fetch, write in zip(fetches, writes):
        fetch.wait()
        write.start()
    rows = jnp.concatenate(
        [
            whole[:, :BLOCK, :].astype(f32)[:, :REACH],
            whole[:, row_count - BLOCK :, :].astype(f32)[:, BLOCK - REACH :],
        ],
        axis=1,
    ).astype(bf16)
    line = iota((8, TILE), 0)
    lane = iota((8, TILE), 1)
    left = ((line == lane) & (line < REACH)).astype(bf16)
    right = ((line + TILE - 2 * REACH == lane) & (line >= REACH)).astype(bf16)
    over_lanes = (((1,), (1,)), ((), ()))
    cols = []
    for f in range(frame_count):
        one = lax.dot_general(left, whole[f, :, :TILE], over_lanes, preferred_element_type=f32)
        one += lax.dot_general(
            right, whole[f, :, col_count - TILE :], over_lanes, preferred_element_type=f32
        )
        cols.append(one[: 2 * REACH].astype(bf16))
    if slab == 0:
        targets = [rim.at[0], send_low.at[0], send_high.at[0]]
        starts = [0, middle, 0]
        rim[1] = other[...]
        send_low[1] = other[middle:]
        send_high[1] = other[:HALF]
    else:
        targets, starts = [rim], [0]
    for target, start in zip(targets, starts):
        target[:, :, :col_count] = rows[start : start + target.shape[0]]
        for f in range(target.shape[0]):
            target[f, :, col_count:] = cols[start + f]
    for write in writes:
        write.wait()


def cut(slab, frames, other):
    _, frame_count, row_count, col_count = frames.shape
    anywhere = pl.BlockSpec(memory_space=pl.ANY)
    near = pl.BlockSpec(memory_space=pltpu.VMEM)
    piece = jax.ShapeDtypeStruct((HALF, row_count, col_count), bf16)
    shape = (frame_count, 2 * REACH, col_count + row_count)
    if slab == 0:
        operands = [frames, other]
        shapes = [(2,) + shape, (2, HALF) + shape[1:], (2, HALF) + shape[1:]]
    else:
        operands = [frames]
        shapes = [shape]
    rims = [jax.ShapeDtypeStruct(shape, bf16) for shape in shapes]
    return pl.pallas_call(
        functools.partial(cut_kernel, slab),
        in_specs=[anywhere] + [near] * (len(operands) - 1),
        out_specs=[near] * len(rims) + [anywhere] * 2,
        out_shape=rims + [piece, piece],
        scratch_shapes=[
            pltpu.VMEM((frame_count, row_count, col_count), bf16),
            pltpu.SemaphoreType.DMA((4,)),
        ],
        compiler_params=pltpu.CompilerParams(vmem_limit_bytes=60 * 1024 * 1024),
        cost_estimate=pl.CostEstimate(flops=0, bytes_accessed=9_000_000, transcendentals=0),
        name=f"cut_{slab}",
    )(*operands)


def run_slab(slab, smoothed, spots, taps, w2, low, frames, high, edge, below, above):
    _, frame_count, row_count, col_count = frames.shape
    slot_count = spots.shape[1]
    row_step, frame_step = 32, 4
    steps_1 = row_count // row_step
    steps_2 = frame_count // frame_step
    wide = col_count + TILE
    near = frame_count + 2 * HALF

    def row_block(at):
        return jnp.minimum(at, steps_1 - 1)

    def whole(array):
        return pl.BlockSpec(array.shape, lambda at: (0,) * array.ndim)

    operands = [spots, taps, w2, low, frames, high, edge, below, above]
    in_specs = [
        pl.BlockSpec(memory_space=pltpu.SMEM),
        whole(taps),
        whole(w2),
        pl.BlockSpec((HALF, row_step, col_count), lambda at: (0, row_block(at), 0)),
        pl.BlockSpec((1, frame_count, row_step, col_count), lambda at: (slab, 0, row_block(at), 0)),
        pl.BlockSpec((HALF, row_step, col_count), lambda at: (0, row_block(at), 0)),
        pl.BlockSpec((1, near, row_step, TILE), lambda at: (slab, 0, row_block(at), 0)),
        pl.BlockSpec((1, near, REACH, wide), lambda at: (slab, 0, 0, 0)),
        pl.BlockSpec((1, near, REACH, wide), lambda at: (slab, 0, 0, 0)),
    ]
    aliases = {}
    if smoothed is not None:
        operands.append(smoothed)
        in_specs.append(pl.BlockSpec(memory_space=pl.ANY))
        aliases = {len(operands) - 1: 0}
    count = len(operands)

    def body(*refs):
        slab_kernel(row_step, frame_step, *refs[:9], *refs[count:])

    tall = row_count + 2 * EDGE
    return pl.pallas_call(
        body,
        grid=(steps_1 + steps_2 + 1,),
        in_specs=in_specs,
        out_specs=[
            pl.BlockSpec(
                (1, frame_step, row_count, col_count),
                lambda at: (slab, jnp.clip(at - steps_1, 0, steps_2 - 1), 0, 0),
            ),
            pl.BlockSpec((slot_count, PATCH * PATCH), lambda at: (0, 0)),
        ],
        out_shape=[
            jax.ShapeDtypeStruct(frames.shape, bf16),
            jax.ShapeDtypeStruct((slot_count, PATCH * PATCH), bf16),
        ],
        scratch_shapes=[
            pltpu.VMEM((16 * frame_count, 8 * near), bf16),
            pltpu.VMEM((frame_count, wide // TILE, tall, TILE), bf16),
            pltpu.VMEM((frame_count, wide // TILE, tall, TILE), bf16),
            pltpu.VMEM((frame_count, wide // TILE, EDGE, TILE), f32),
            pltpu.VMEM((frame_count, wide // TILE, EDGE, TILE), f32),
            pltpu.VMEM((frame_count, col_count // TILE, row_count, TILE), f32),
            pltpu.VMEM((slot_count * PATCH, TILE), bf16),
        ],
        input_output_aliases=aliases,
        compiler_params=pltpu.CompilerParams(vmem_limit_bytes=60 * 1024 * 1024),
        cost_estimate=pl.CostEstimate(
            flops=20_000_000_000, bytes_accessed=16_000_000, transcendentals=0
        ),
        name=f"slab_{slab}",
    )(*operands)


def shards(frames, omega_taps, smooth_kernel, spots, counts):
    _, frame_count, row_count, col_count = frames.shape
    first_frame = lax.axis_index("omega") * frame_count
    first_row = lax.axis_index("row") * row_count
    first_col = lax.axis_index("col") * col_count

    rim, send_low1, send_high1 = cut(1, frames, None)
    low1 = shifted(send_low1, "omega", 1)
    high1 = shifted(send_high1, "omega", -1)
    rim, rim_low, rim_high, send_low0, send_high0 = cut(0, frames, rim)
    rim = jnp.concatenate(
        [shifted(rim_low, "omega", 1), rim, shifted(rim_high, "omega", -1)], axis=1
    )
    lane = jnp.arange(TILE, dtype=jnp.int32)[None, :]
    step = jnp.arange(REACH, dtype=jnp.int32)[:, None]
    after = (lane == step).astype(bf16)
    before = (lane == TILE - REACH + step).astype(bf16)
    if lax.axis_size("col") == 2:
        first = lax.axis_index("col") == 0
        sides = jnp.where(first, rim[:, :, REACH:, col_count:], rim[:, :, :REACH, col_count:])
        sides = lax.ppermute(sides, "col", [(0, 1), (1, 0)])
        place = jnp.where(first, after, before)
    else:
        left = shifted(rim[:, :, REACH:, col_count:], "col", 1)
        right = shifted(rim[:, :, :REACH, col_count:], "col", -1)
        sides = jnp.concatenate([right, left], axis=2)
        place = jnp.concatenate([after, before], axis=0)
    send_low0, send_high0, sides = lax.optimization_barrier((send_low0, send_high0, sides))
    low0 = shifted(send_low0, "omega", 1)
    high0 = shifted(send_high0, "omega", -1)
    edge = jnp.einsum("sfkr,kc->sfrc", sides, place, preferred_element_type=bf16)
    ends = jnp.concatenate([edge[:, :, :REACH], edge[:, :, -REACH:]], axis=2)
    line = jnp.concatenate([rim[..., :col_count], ends], axis=3)
    above = shifted(line[:, :, REACH:], "row", 1)
    below = shifted(line[:, :, :REACH], "row", -1)

    taps = omega_matrix(
        omega_taps, first_frame, frame_count, frame_count * lax.axis_size("omega")
    )
    w2 = smooth_matrix(smooth_kernel)
    frame, row, col = spots[:, 0] - first_frame, spots[:, 1] - first_row, spots[:, 2] - first_col
    tile = col // TILE
    beside = jnp.minimum(tile + 1, col_count // TILE - 1)
    live = jnp.broadcast_to(counts, frame.shape)
    local = jnp.stack([frame, row, tile, beside, TILE - col % TILE, live], axis=1)

    smoothed, second = run_slab(1, None, local[1], taps, w2, low1, frames, high1, edge, below, above)
    count = lax.axis_size("row") * lax.axis_size("col")
    second = lax.ppermute(second, ("row", "col"), [(i, count - 1 - i) for i in range(count)])
    smoothed, first = run_slab(0, smoothed, local[0], taps, w2, low0, frames, high0, edge, below, above)
    scores = (
        lax.dot_general(first, second, (((1,), (1,)), ((), ())), preferred_element_type=f32)
        / float(PATCH * PATCH)
    )
    return (smoothed, scores)


def solution(mesh):
    return jax.shard_map(
        shards,
        mesh=mesh,
        in_specs=(
            P(None, "omega", "row", "col"),
            P(),
            P(),
            P(None, None, ("omega", "row", "col")),
            P(None, ("omega", "row", "col")),
        ),
        out_specs=(P(None, "omega", "row", "col"), P(("omega", "row", "col"), None)),
        check_vma=False,
    )
```

```python
import jax
import jax.numpy as jnp
from jax import lax
from jax.experimental import pallas as pl
from jax.experimental.pallas import tpu as pltpu
from jax.sharding import PartitionSpec as P

TAPS = 15
HALF = TAPS // 2
PATCH = 16
SIDE = 5
REACH = SIDE // 2
TILE = 128
BLOCK = 16
WINDOW = 32
EDGE = 8
GROUP = 4
bf16 = jnp.bfloat16
f32 = jnp.float32


def shifted(block, axis, step):
    count = lax.axis_size(axis)
    route = [(i, i + step) for i in range(count) if 0 <= i + step < count]
    return lax.ppermute(block, axis, route)


def split(values):
    high = lax.reduce_precision(values, 8, 7)
    return high.astype(bf16), (values - high).astype(bf16)


def omega_matrix(omega_taps, first_frame, frame_count, frame_total):
    out_ids = jnp.arange(frame_count, dtype=jnp.int32)[:, None]
    in_ids = jnp.arange(frame_count + 2 * HALF, dtype=jnp.int32)[None, :]
    source = first_frame + in_ids - HALF
    valid = (source >= 0) & (source < frame_total)
    tap = jnp.where(valid, in_ids - out_ids, -1)
    hit = tap[:, :, None] == jnp.arange(TAPS, dtype=jnp.int32)
    weights = jnp.sum(jnp.where(hit, omega_taps, 0.0), axis=2)
    norm = jnp.sum(weights, axis=1, keepdims=True)
    center = (in_ids - out_ids == HALF).astype(f32)
    matrix = center - weights / norm
    return jnp.stack(split(matrix), axis=1).reshape(2 * frame_count, matrix.shape[1])


def smooth_matrix(smooth_kernel):
    depth = WINDOW + 2 * EDGE
    out_ids = jnp.arange(WINDOW, dtype=jnp.int32)[:, None]
    in_ids = jnp.arange(depth, dtype=jnp.int32)[None, :]
    step = in_ids - out_ids - (EDGE - REACH)
    hit = step[None, :, :, None] == jnp.arange(SIDE, dtype=jnp.int32)
    table = jnp.sum(jnp.where(hit, smooth_kernel.T[:, None, None, :], 0.0), axis=3)
    table = jnp.swapaxes(table.reshape(SIDE, WINDOW // BLOCK, BLOCK, depth), 0, 1)
    high, low = split(table)
    return jnp.concatenate([high, high, low], axis=3).reshape(SIDE * WINDOW, 3 * depth)


def iota(shape, dim):
    return lax.broadcasted_iota(jnp.int32, shape, dim)


def slab_kernel(
    row_step, frame_step,
    spots_ref, taps_ref, w2_ref, low_ref, own_ref, high_ref, edge_ref, below_ref, above_ref,
    out_ref, last_ref, w1, chi, clo, carry, outer, kept, flat,
):
    frame_count, tiles, row_count, _ = kept.shape
    near = taps_ref.shape[1]
    steps_1 = row_count // row_step
    steps_2 = frame_count // frame_step
    at = pl.program_id(0)

    def filtered(block):
        part = block.reshape(near * 8, block.shape[2]).astype(bf16)
        both = jnp.dot(w1[...], part, preferred_element_type=f32)
        both = both.reshape(frame_count, 2, 8, block.shape[2])
        return both[:, 0] + both[:, 1]

    def keep(above, below, tile, place):
        value = jnp.concatenate([above, below], axis=1)
        high = value.astype(bf16)
        chi[:, tile, place, :] = high
        clo[:, tile, place, :] = (value - high.astype(f32)).astype(bf16)

    @pl.when(at == 0)
    def _():
        count = 2 * frame_count
        tall = (iota((8 * count, count), 0) // 8 == iota((8 * count, count), 1)).astype(bf16)
        wide = (iota((near, 8 * near), 1) // 8 == iota((near, 8 * near), 0)).astype(bf16)
        full = jnp.dot(tall, taps_ref[...], preferred_element_type=f32).astype(bf16)
        full = jnp.dot(full, wide, preferred_element_type=f32)
        same = iota(full.shape, 0) % 8 == iota(full.shape, 1) % 8
        w1[...] = jnp.where(same, full, 0.0).astype(bf16)
        for tile in range(0, tiles + 1, GROUP):
            pair = range(tile, min(tile + GROUP, tiles + 1))
            cols = slice(tile * TILE, (tile + len(pair)) * TILE)
            below = below_ref[0, :, :, cols].astype(f32)
            above = above_ref[0, :, :, cols].astype(f32)
            gap = jnp.zeros((near, 8 - 2 * REACH, below.shape[2]), f32)
            both = filtered(jnp.concatenate([below, gap, above], axis=1))
            for q, one in enumerate(pair):
                carry[:, one] = both[..., q * TILE : (q + 1) * TILE]
                outer[:, one] = both[..., q * TILE : (q + 1) * TILE]

    @pl.when(at < steps_1)
    def _():
        def keep_all(tile, parts):
            parts = [carry[:, tile]] + parts
            for q in range(0, len(parts) - 1, 2):
                place = pl.ds(pl.multiple_of(at * row_step + EDGE * q, BLOCK), BLOCK)
                keep(parts[q], parts[q + 1], tile, place)
            carry[:, tile] = parts[-1]

        for tile in range(0, tiles, GROUP):
            group = range(tile, min(tile + GROUP, tiles))
            cols = slice(tile * TILE, (tile + len(group)) * TILE)
            parts = []
            for h in range(0, row_step, BLOCK):
                rows = slice(h, h + BLOCK)
                block = jnp.concatenate(
                    [low_ref[:, rows, cols], own_ref[0, :, rows, cols], high_ref[:, rows, cols]],
                    axis=0,
                ).astype(f32)
                parts += [filtered(block[:, :EDGE]), filtered(block[:, EDGE:])]
            for q, one in enumerate(group):
                keep_all(one, [part[..., q * TILE : (q + 1) * TILE] for part in parts])
        wide = edge_ref[0].astype(f32)
        both = filtered(
            jnp.concatenate([wide[:, h : h + EDGE] for h in range(0, row_step, EDGE)], axis=2)
        )
        parts = [both[..., h * TILE : (h + 1) * TILE] for h in range(row_step // EDGE)]
        keep_all(tiles, parts)

    @pl.when(at == steps_1 - 1)
    def _():
        for tile in range(tiles + 1):
            keep(carry[:, tile], outer[:, tile], tile, slice(row_count, row_count + BLOCK))

    @pl.when((at >= steps_1) & (at < steps_1 + steps_2))
    def _():
        lane = iota((BLOCK, TILE), 1)
        edge_of = [lane < 2, lane < 1, None, lane >= TILE - 1, lane >= TILE - 2]

        depth = WINDOW + 2 * EDGE
        parts_of = range(WINDOW // BLOCK)

        def two_frames(k2, unused):
            for row in range(0, row_count, WINDOW):
                turned = {}
                done = [0, 0]

                def finish(f, tile):
                    k = k2 * 2 + f
                    frame = (at - steps_1) * frame_step + k
                    for m in parts_of:
                        total = turned[f, m, REACH, tile]
                        for b in range(SIDE):
                            if b != REACH:
                                beside = (tile + (1 if b > REACH else -1)) % (tiles + 1)
                                total = total + jnp.where(
                                    edge_of[b], turned[f, m, b, beside], turned[f, m, b, tile]
                                )
                        value = total.astype(bf16)
                        rows = slice(row + m * BLOCK, row + (m + 1) * BLOCK)
                        out_ref[0, k, rows, tile * TILE : (tile + 1) * TILE] = value
                        kept[frame, tile, rows, :] = value.astype(f32)

                order = [(f, tile) for f in range(2) for tile in [tiles] + list(range(tiles))]
                for p in range(0, len(order), GROUP):
                    pair = order[p : p + GROUP]
                    stacks = []
                    for f, tile in pair:
                        frame = (at - steps_1) * frame_step + k2 * 2 + f
                        high = chi[frame, tile, row : row + depth, :]
                        low = clo[frame, tile, row : row + depth, :]
                        stacks.append(jnp.concatenate([high, low, high], axis=0))
                    both = jnp.dot(
                        w2_ref[...], jnp.concatenate(stacks, axis=1), preferred_element_type=f32
                    )
                    for q, (f, tile) in enumerate(pair):
                        for m in parts_of:
                            for b in range(SIDE):
                                at_row = (m * SIDE + b) * BLOCK
                                part = both[at_row : at_row + BLOCK, q * TILE : (q + 1) * TILE]
                                if b != REACH:
                                    part = pltpu.roll(part, (REACH - b) % TILE, 1)
                                turned[f, m, b, tile] = part
                    for f in range(2):
                        while done[f] < tiles and (f, 0, 0, done[f]) in turned:
                            after = min(done[f] + 1, tiles)
                            if (f, 0, 0, after) not in turned:
                                break
                            finish(f, done[f])
                            done[f] += 1
            return unused

        lax.fori_loop(0, frame_step // 2, two_frames, 0)

    @pl.when(at == steps_1 + steps_2)
    def _():
        slot_count = flat.shape[0] // PATCH

        lane = iota((PATCH, TILE), 1)

        def some(i8, unused):
            for j in range(8):
                i = i8 * 8 + j
                frame, row, tile = spots_ref[0, i], spots_ref[1, i], spots_ref[2, i]
                beside, turn = spots_ref[3, i], spots_ref[4, i]
                here = kept[frame, tile, pl.ds(row, PATCH), :]
                there = kept[frame, beside, pl.ds(row, PATCH), :]
                shift = turn & (TILE - 1)
                here, there = pltpu.roll(here, shift, 1), pltpu.roll(there, shift, 1)
                part = jnp.where(lane < turn, here, there)
                flat[pl.ds(pl.multiple_of(i * PATCH, PATCH), PATCH), :] = part.astype(bf16)
            return unused

        lax.fori_loop(0, slot_count // 8, some, 0)
        low_bits = PATCH - 1
        bits = low_bits.bit_length()
        shape = (TILE, PATCH * PATCH)
        repeat = (iota(shape, 1) & low_bits == iota(shape, 0)).astype(bf16)
        rows = jnp.dot(flat[...], repeat, preferred_element_type=f32)
        mine = iota(rows.shape, 1) >> bits == iota(rows.shape, 0) & low_bits
        rows = jnp.where(mine, rows, 0.0).astype(bf16)
        shape = (slot_count, rows.shape[0])
        owner = (iota(shape, 1) >> bits == iota(shape, 0)).astype(bf16)
        values = jnp.dot(owner, rows, preferred_element_type=f32)
        mean = jnp.sum(values, axis=1, keepdims=True) / (PATCH * PATCH)
        centered = values - mean
        spread = jnp.sum(centered * centered, axis=1, keepdims=True) / (PATCH * PATCH)
        normed = centered / jnp.sqrt(spread + 1e-05)
        live = iota((slot_count, 1), 0) < spots_ref[5, 0]
        last_ref[...] = jnp.where(live, normed, 0.0).astype(bf16)


def edges_of(top, bottom, left, right):
    rows = jnp.concatenate(
        [top[...].astype(f32)[:, :REACH], bottom[...].astype(f32)[:, BLOCK - REACH :]], axis=1
    )
    line = iota((8, TILE), 0)
    lane = iota((8, TILE), 1)
    first = ((line == lane) & (line < REACH)).astype(bf16)
    last = ((line + TILE - 2 * REACH == lane) & (line >= REACH)).astype(bf16)
    over_lanes = (((1,), (1,)), ((), ()))
    cols = []
    for f in range(rows.shape[0]):
        one = lax.dot_general(first, left[f], over_lanes, preferred_element_type=f32)
        one += lax.dot_general(last, right[f], over_lanes, preferred_element_type=f32)
        cols.append(one[: 2 * REACH].astype(bf16))
    return rows.astype(bf16), cols


def send_all(frames, slab, low, high, whole, sems):
    frame_count = whole.shape[0]
    middle = frame_count - HALF
    spans = [pl.ds(0, middle), pl.ds(middle, HALF)]
    fetches = [
        pltpu.make_async_copy(frames.at[slab, span], whole.at[span], sems.at[i])
        for i, span in enumerate(spans)
    ]
    writes = [
        pltpu.make_async_copy(whole.at[pl.ds(0, HALF)], high, sems.at[2]),
        pltpu.make_async_copy(whole.at[pl.ds(middle, HALF)], low, sems.at[3]),
    ]
    return fetches, writes


def cut_kernel(frames, rim, rim_low, rim_high, low, high, whole, top, bottom, left, right, sems):
    frame_count, row_count, col_count = whole.shape
    reads = [
        pltpu.make_async_copy(source, target, sems.at[4 + i])
        for i, (source, target) in enumerate(
            [
                (frames.at[0, :, pl.ds(0, BLOCK), :], top),
                (frames.at[0, :, pl.ds(row_count - BLOCK, BLOCK), :], bottom),
                (frames.at[0, :, :, pl.ds(0, TILE)], left),
                (frames.at[0, :, :, pl.ds(col_count - TILE, TILE)], right),
            ]
        )
    ]
    fetches, writes = send_all(frames, 1, low, high, whole, sems)
    for copy in reads + fetches:
        copy.start()

    def put(slab, rows, cols):
        middle = frame_count - HALF
        for target, start in [(rim, 0), (rim_low, middle), (rim_high, 0)]:
            count = target.shape[1]
            target[slab, :, :, :col_count] = rows[start : start + count]
            for f in range(count):
                target[slab, f, :, col_count:] = cols[start + f]

    for copy in reads:
        copy.wait()
    put(0, *edges_of(top, bottom, left, right))
    for fetch, write in zip(fetches, writes):
        fetch.wait()
        write.start()
    put(
        1,
        *edges_of(
            whole.at[:, pl.ds(0, BLOCK), :],
            whole.at[:, pl.ds(row_count - BLOCK, BLOCK), :],
            whole.at[:, :, pl.ds(0, TILE)],
            whole.at[:, :, pl.ds(col_count - TILE, TILE)],
        ),
    )
    for write in writes:
        write.wait()


def late_kernel(frames, low, high, whole, sems):
    fetches, writes = send_all(frames, 0, low, high, whole, sems)
    for fetch in fetches:
        fetch.start()
    for fetch, write in zip(fetches, writes):
        fetch.wait()
        write.start()
    for write in writes:
        write.wait()


def cut(frames):
    slabs, frame_count, row_count, col_count = frames.shape
    anywhere = pl.BlockSpec(memory_space=pl.ANY)
    near = pl.BlockSpec(memory_space=pltpu.VMEM)
    piece = jax.ShapeDtypeStruct((HALF, row_count, col_count), bf16)
    wide = col_count + row_count
    rims = [
        jax.ShapeDtypeStruct((slabs, count, 2 * REACH, wide), bf16)
        for count in (frame_count, HALF, HALF)
    ]
    return pl.pallas_call(
        cut_kernel,
        in_specs=[anywhere],
        out_specs=[near] * 3 + [anywhere] * 2,
        out_shape=rims + [piece, piece],
        scratch_shapes=[
            pltpu.VMEM((frame_count, row_count, col_count), bf16),
            pltpu.VMEM((frame_count, BLOCK, col_count), bf16),
            pltpu.VMEM((frame_count, BLOCK, col_count), bf16),
            pltpu.VMEM((frame_count, row_count, TILE), bf16),
            pltpu.VMEM((frame_count, row_count, TILE), bf16),
            pltpu.SemaphoreType.DMA((8,)),
        ],
        compiler_params=pltpu.CompilerParams(vmem_limit_bytes=60 * 1024 * 1024),
        name="cut",
    )(frames)


def late_cut(frames):
    _, frame_count, row_count, col_count = frames.shape
    anywhere = pl.BlockSpec(memory_space=pl.ANY)
    piece = jax.ShapeDtypeStruct((HALF, row_count, col_count), bf16)
    return pl.pallas_call(
        late_kernel,
        in_specs=[anywhere],
        out_specs=[anywhere] * 2,
        out_shape=[piece, piece],
        scratch_shapes=[
            pltpu.VMEM((frame_count, row_count, col_count), bf16),
            pltpu.SemaphoreType.DMA((4,)),
        ],
        compiler_params=pltpu.CompilerParams(vmem_limit_bytes=60 * 1024 * 1024),
        cost_estimate=pl.CostEstimate(flops=0, bytes_accessed=9_000_000, transcendentals=0),
        name="late_cut",
    )(frames)


def run_slab(slab, smoothed, spots, taps, w2, low, frames, high, edge, below, above):
    _, frame_count, row_count, col_count = frames.shape
    slot_count = spots.shape[1]
    row_step, frame_step = 32, 4
    steps_1 = row_count // row_step
    steps_2 = frame_count // frame_step
    wide = col_count + TILE
    near = frame_count + 2 * HALF

    def row_block(at):
        return jnp.minimum(at, steps_1 - 1)

    def whole(array):
        return pl.BlockSpec(array.shape, lambda at: (0,) * array.ndim)

    operands = [spots, taps, w2, low, frames, high, edge, below, above]
    in_specs = [
        pl.BlockSpec(memory_space=pltpu.SMEM),
        whole(taps),
        whole(w2),
        pl.BlockSpec((HALF, row_step, col_count), lambda at: (0, row_block(at), 0)),
        pl.BlockSpec((1, frame_count, row_step, col_count), lambda at: (slab, 0, row_block(at), 0)),
        pl.BlockSpec((HALF, row_step, col_count), lambda at: (0, row_block(at), 0)),
        pl.BlockSpec((1, near, row_step, TILE), lambda at: (slab, 0, row_block(at), 0)),
        pl.BlockSpec((1, near, REACH, wide), lambda at: (slab, 0, 0, 0)),
        pl.BlockSpec((1, near, REACH, wide), lambda at: (slab, 0, 0, 0)),
    ]
    aliases = {}
    if smoothed is not None:
        operands.append(smoothed)
        in_specs.append(pl.BlockSpec(memory_space=pl.ANY))
        aliases = {len(operands) - 1: 0}
    count = len(operands)

    def body(*refs):
        slab_kernel(row_step, frame_step, *refs[:9], *refs[count:])

    tall = row_count + 2 * EDGE
    return pl.pallas_call(
        body,
        grid=(steps_1 + steps_2 + 1,),
        in_specs=in_specs,
        out_specs=[
            pl.BlockSpec(
                (1, frame_step, row_count, col_count),
                lambda at: (slab, jnp.clip(at - steps_1, 0, steps_2 - 1), 0, 0),
            ),
            pl.BlockSpec((slot_count, PATCH * PATCH), lambda at: (0, 0)),
        ],
        out_shape=[
            jax.ShapeDtypeStruct(frames.shape, bf16),
            jax.ShapeDtypeStruct((slot_count, PATCH * PATCH), bf16),
        ],
        scratch_shapes=[
            pltpu.VMEM((16 * frame_count, 8 * near), bf16),
            pltpu.VMEM((frame_count, wide // TILE, tall, TILE), bf16),
            pltpu.VMEM((frame_count, wide // TILE, tall, TILE), bf16),
            pltpu.VMEM((frame_count, wide // TILE, EDGE, TILE), f32),
            pltpu.VMEM((frame_count, wide // TILE, EDGE, TILE), f32),
            pltpu.VMEM((frame_count, col_count // TILE, row_count, TILE), f32),
            pltpu.VMEM((slot_count * PATCH, TILE), bf16),
        ],
        input_output_aliases=aliases,
        compiler_params=pltpu.CompilerParams(vmem_limit_bytes=60 * 1024 * 1024),
        cost_estimate=pl.CostEstimate(
            flops=20_000_000_000, bytes_accessed=16_000_000, transcendentals=0
        ),
        name=f"slab_{slab}",
    )(*operands)


def shards(frames, omega_taps, smooth_kernel, spots, counts):
    _, frame_count, row_count, col_count = frames.shape
    first_frame = lax.axis_index("omega") * frame_count
    first_row = lax.axis_index("row") * row_count
    first_col = lax.axis_index("col") * col_count

    rim, rim_low, rim_high, send_low1, send_high1 = cut(frames)
    rim = jnp.concatenate(
        [shifted(rim_low, "omega", 1), rim, shifted(rim_high, "omega", -1)], axis=1
    )
    low1 = shifted(send_low1, "omega", 1)
    high1 = shifted(send_high1, "omega", -1)
    lane = jnp.arange(TILE, dtype=jnp.int32)[None, :]
    step = jnp.arange(REACH, dtype=jnp.int32)[:, None]
    after = (lane == step).astype(bf16)
    before = (lane == TILE - REACH + step).astype(bf16)
    if lax.axis_size("col") == 2:
        first = lax.axis_index("col") == 0
        sides = jnp.where(first, rim[:, :, REACH:, col_count:], rim[:, :, :REACH, col_count:])
        sides = lax.ppermute(sides, "col", [(0, 1), (1, 0)])
        place = jnp.where(first, after, before)
    else:
        left = shifted(rim[:, :, REACH:, col_count:], "col", 1)
        right = shifted(rim[:, :, :REACH, col_count:], "col", -1)
        sides = jnp.concatenate([right, left], axis=2)
        place = jnp.concatenate([after, before], axis=0)
    later, sides = lax.optimization_barrier((frames, sides))
    send_low0, send_high0 = late_cut(later)
    low0 = shifted(send_low0, "omega", 1)
    high0 = shifted(send_high0, "omega", -1)
    edge = jnp.einsum("sfkr,kc->sfrc", sides, place, preferred_element_type=bf16)
    ends = jnp.concatenate([edge[:, :, :REACH], edge[:, :, -REACH:]], axis=2)
    line = jnp.concatenate([rim[..., :col_count], ends], axis=3)
    above = shifted(line[:, :, REACH:], "row", 1)
    below = shifted(line[:, :, :REACH], "row", -1)

    taps = omega_matrix(
        omega_taps, first_frame, frame_count, frame_count * lax.axis_size("omega")
    )
    w2 = smooth_matrix(smooth_kernel)
    frame, row, col = spots[:, 0] - first_frame, spots[:, 1] - first_row, spots[:, 2] - first_col
    tile = col // TILE
    beside = jnp.minimum(tile + 1, col_count // TILE - 1)
    live = jnp.broadcast_to(counts, frame.shape)
    local = jnp.stack([frame, row, tile, beside, TILE - col % TILE, live], axis=1)

    smoothed, second = run_slab(1, None, local[1], taps, w2, low1, frames, high1, edge, below, above)
    count = lax.axis_size("row") * lax.axis_size("col")
    second = lax.ppermute(second, ("row", "col"), [(i, count - 1 - i) for i in range(count)])
    smoothed, first = run_slab(0, smoothed, local[0], taps, w2, low0, frames, high0, edge, below, above)
    scores = (
        lax.dot_general(first, second, (((1,), (1,)), ((), ())), preferred_element_type=f32)
        / float(PATCH * PATCH)
    )
    return (smoothed, scores)


def solution(mesh):
    return jax.shard_map(
        shards,
        mesh=mesh,
        in_specs=(
            P(None, "omega", "row", "col"),
            P(),
            P(),
            P(None, None, ("omega", "row", "col")),
            P(None, ("omega", "row", "col")),
        ),
        out_specs=(P(None, "omega", "row", "col"), P(("omega", "row", "col"), None)),
        check_vma=False,
    )
```

```python
import jax
import jax.numpy as jnp
from jax import lax
from jax.experimental import pallas as pl
from jax.experimental.pallas import tpu as pltpu
from jax.sharding import PartitionSpec as P

TAPS = 15
HALF = TAPS // 2
PATCH = 16
SIDE = 5
REACH = SIDE // 2
TILE = 128
BLOCK = 16
WINDOW = 32
EDGE = 8
GROUP = 4
BY_VECTOR = (1, 2)
BY_MATRIX = (0, 3, 4)
bf16 = jnp.bfloat16
f32 = jnp.float32


def shifted(block, axis, step):
    count = lax.axis_size(axis)
    route = [(i, i + step) for i in range(count) if 0 <= i + step < count]
    return lax.ppermute(block, axis, route)


def split(values):
    high = lax.reduce_precision(values, 8, 7)
    return high.astype(bf16), (values - high).astype(bf16)


def omega_matrix(omega_taps, first_frame, frame_count, frame_total):
    out_ids = jnp.arange(frame_count, dtype=jnp.int32)[:, None]
    in_ids = jnp.arange(frame_count + 2 * HALF, dtype=jnp.int32)[None, :]
    source = first_frame + in_ids - HALF
    valid = (source >= 0) & (source < frame_total)
    tap = jnp.where(valid, in_ids - out_ids, -1)
    hit = tap[:, :, None] == jnp.arange(TAPS, dtype=jnp.int32)
    weights = jnp.sum(jnp.where(hit, omega_taps, 0.0), axis=2)
    norm = jnp.sum(weights, axis=1, keepdims=True)
    center = (in_ids - out_ids == HALF).astype(f32)
    matrix = center - weights / norm
    return jnp.stack(split(matrix), axis=1).reshape(2 * frame_count, matrix.shape[1])


def smooth_matrix(smooth_kernel):
    depth = WINDOW + 2 * EDGE
    out_ids = jnp.arange(WINDOW, dtype=jnp.int32)[:, None]
    in_ids = jnp.arange(depth, dtype=jnp.int32)[None, :]
    step = in_ids - out_ids - (EDGE - REACH)
    hit = step[None, :, :, None] == jnp.arange(SIDE, dtype=jnp.int32)
    chosen = jnp.stack([smooth_kernel[:, b] for b in BY_MATRIX])
    count = len(BY_MATRIX)
    table = jnp.sum(jnp.where(hit, chosen[:, None, None, :], 0.0), axis=3)
    table = jnp.swapaxes(table.reshape(count, WINDOW // BLOCK, BLOCK, depth), 0, 1)
    high, low = split(table)
    return jnp.concatenate([high, high, low], axis=3).reshape(count * WINDOW, 3 * depth)


def iota(shape, dim):
    return lax.broadcasted_iota(jnp.int32, shape, dim)


def slab_kernel(
    row_step, frame_step,
    spots_ref, kernel_ref, taps_ref, w2_ref, low_ref, own_ref, high_ref, edge_ref, below_ref, above_ref,
    out_ref, last_ref, w1, chi, clo, full, carry, outer, kept, flat,
):
    frame_count, tiles, row_count, _ = kept.shape
    near = taps_ref.shape[1]
    steps_1 = row_count // row_step
    steps_2 = frame_count // frame_step
    at = pl.program_id(0)

    def filtered(block):
        part = block.reshape(near * 8, block.shape[2]).astype(bf16)
        both = jnp.dot(w1[...], part, preferred_element_type=f32)
        both = both.reshape(frame_count, 2, 8, block.shape[2])
        return both[:, 0] + both[:, 1]

    def keep(above, below, tile, place):
        value = jnp.concatenate([above, below], axis=1)
        high = value.astype(bf16)
        full[:, tile, place, :] = value
        chi[:, tile, place, :] = high
        clo[:, tile, place, :] = (value - high.astype(f32)).astype(bf16)

    @pl.when(at == 0)
    def _():
        count = 2 * frame_count
        tall = (iota((8 * count, count), 0) // 8 == iota((8 * count, count), 1)).astype(bf16)
        wide = (iota((near, 8 * near), 1) // 8 == iota((near, 8 * near), 0)).astype(bf16)
        matrix = jnp.dot(tall, taps_ref[...], preferred_element_type=f32).astype(bf16)
        matrix = jnp.dot(matrix, wide, preferred_element_type=f32)
        same = iota(matrix.shape, 0) & 7 == iota(matrix.shape, 1) & 7
        w1[...] = jnp.where(same, matrix, 0.0).astype(bf16)
        for tile in range(0, tiles + 1, GROUP):
            pair = range(tile, min(tile + GROUP, tiles + 1))
            cols = slice(tile * TILE, (tile + len(pair)) * TILE)
            below = below_ref[0, :, :, cols].astype(f32)
            above = above_ref[0, :, :, cols].astype(f32)
            gap = jnp.zeros((near, 8 - 2 * REACH, below.shape[2]), f32)
            both = filtered(jnp.concatenate([below, gap, above], axis=1))
            for q, one in enumerate(pair):
                carry[:, one] = both[..., q * TILE : (q + 1) * TILE]
                outer[:, one] = both[..., q * TILE : (q + 1) * TILE]

    @pl.when(at < steps_1)
    def _():
        def keep_all(tile, parts):
            parts = [carry[:, tile]] + parts
            for q in range(0, len(parts) - 1, 2):
                place = pl.ds(pl.multiple_of(at * row_step + EDGE * q, BLOCK), BLOCK)
                keep(parts[q], parts[q + 1], tile, place)
            carry[:, tile] = parts[-1]

        for tile in range(0, tiles, GROUP):
            group = range(tile, min(tile + GROUP, tiles))
            cols = slice(tile * TILE, (tile + len(group)) * TILE)
            parts = []
            for h in range(0, row_step, BLOCK):
                rows = slice(h, h + BLOCK)
                block = jnp.concatenate(
                    [low_ref[:, rows, cols], own_ref[0, :, rows, cols], high_ref[:, rows, cols]],
                    axis=0,
                ).astype(f32)
                parts += [filtered(block[:, :EDGE]), filtered(block[:, EDGE:])]
            for q, one in enumerate(group):
                keep_all(one, [part[..., q * TILE : (q + 1) * TILE] for part in parts])
        wide = edge_ref[0].astype(f32)
        both = filtered(
            jnp.concatenate([wide[:, h : h + EDGE] for h in range(0, row_step, EDGE)], axis=2)
        )
        parts = [both[..., h * TILE : (h + 1) * TILE] for h in range(row_step // EDGE)]
        keep_all(tiles, parts)

    @pl.when(at == steps_1 - 1)
    def _():
        for tile in range(tiles + 1):
            keep(carry[:, tile], outer[:, tile], tile, slice(row_count, row_count + BLOCK))

    @pl.when((at >= steps_1) & (at < steps_1 + steps_2))
    def _():
        lane = iota((BLOCK, TILE), 1)
        edge_of = [lane < 2, lane < 1, None, lane >= TILE - 1, lane >= TILE - 2]

        depth = WINDOW + 2 * EDGE
        parts_of = range(WINDOW // BLOCK)

        def two_frames(k2, unused):
            for row in range(0, row_count, WINDOW):
                turned = {}
                done = [0, 0]

                def finish(f, tile):
                    k = k2 * 2 + f
                    frame = (at - steps_1) * frame_step + k
                    for m in parts_of:
                        total = turned[f, m, REACH, tile]
                        for b in range(SIDE):
                            if b != REACH:
                                beside = (tile + (1 if b > REACH else -1)) % (tiles + 1)
                                total = total + jnp.where(
                                    edge_of[b], turned[f, m, b, beside], turned[f, m, b, tile]
                                )
                        value = total.astype(bf16)
                        rows = slice(row + m * BLOCK, row + (m + 1) * BLOCK)
                        out_ref[0, k, rows, tile * TILE : (tile + 1) * TILE] = value
                        kept[frame, tile, rows, :] = value.astype(f32)

                order = [(f, tile) for f in range(2) for tile in [tiles] + list(range(tiles))]
                for p in range(0, len(order), GROUP):
                    pair = order[p : p + GROUP]
                    stacks = []
                    for f, tile in pair:
                        frame = (at - steps_1) * frame_step + k2 * 2 + f
                        high = chi[frame, tile, row : row + depth, :]
                        low = clo[frame, tile, row : row + depth, :]
                        stacks.append(jnp.concatenate([high, low, high], axis=0))
                    both = jnp.dot(
                        w2_ref[...], jnp.concatenate(stacks, axis=1), preferred_element_type=f32
                    )
                    for q, (f, tile) in enumerate(pair):
                        frame = (at - steps_1) * frame_step + k2 * 2 + f
                        for m in parts_of:
                            parts = {}
                            for i, b in enumerate(BY_MATRIX):
                                at_row = (m * len(BY_MATRIX) + i) * BLOCK
                                parts[b] = both[at_row : at_row + BLOCK, q * TILE : (q + 1) * TILE]
                            start = row + m * BLOCK + EDGE - REACH
                            rows = [
                                full[frame, tile, start + a : start + a + BLOCK, :]
                                for a in range(SIDE)
                            ]
                            for b in BY_VECTOR:
                                total = kernel_ref[0, b] * rows[0]
                                for a in range(1, SIDE):
                                    total = total + kernel_ref[a, b] * rows[a]
                                parts[b] = total
                            for b, part in parts.items():
                                if b != REACH:
                                    part = pltpu.roll(part, (REACH - b) % TILE, 1)
                                turned[f, m, b, tile] = part
                    for f in range(2):
                        while done[f] < tiles and (f, 0, 0, done[f]) in turned:
                            after = min(done[f] + 1, tiles)
                            if (f, 0, 0, after) not in turned:
                                break
                            finish(f, done[f])
                            done[f] += 1
            return unused

        lax.fori_loop(0, frame_step // 2, two_frames, 0)

    @pl.when(at == steps_1 + steps_2)
    def _():
        slot_count = flat.shape[0] // PATCH

        lane = iota((PATCH, TILE), 1)

        def some(i8, unused):
            for j in range(8):
                i = i8 * 8 + j
                frame, row, tile = spots_ref[0, i], spots_ref[1, i], spots_ref[2, i]
                beside, turn = spots_ref[3, i], spots_ref[4, i]
                here = kept[frame, tile, pl.ds(row, PATCH), :]
                there = kept[frame, beside, pl.ds(row, PATCH), :]
                shift = turn & (TILE - 1)
                here, there = pltpu.roll(here, shift, 1), pltpu.roll(there, shift, 1)
                part = jnp.where(lane < turn, here, there)
                flat[pl.ds(pl.multiple_of(i * PATCH, PATCH), PATCH), :] = part.astype(bf16)
            return unused

        lax.fori_loop(0, slot_count // 8, some, 0)
        low_bits = PATCH - 1
        bits = low_bits.bit_length()
        shape = (TILE, PATCH * PATCH)
        repeat = (iota(shape, 1) & low_bits == iota(shape, 0)).astype(bf16)
        rows = jnp.dot(flat[...], repeat, preferred_element_type=f32)
        mine = iota(rows.shape, 1) >> bits == iota(rows.shape, 0) & low_bits
        rows = jnp.where(mine, rows, 0.0).astype(bf16)
        shape = (slot_count, rows.shape[0])
        owner = (iota(shape, 1) >> bits == iota(shape, 0)).astype(bf16)
        values = jnp.dot(owner, rows, preferred_element_type=f32)
        mean = jnp.sum(values, axis=1, keepdims=True) / (PATCH * PATCH)
        centered = values - mean
        spread = jnp.sum(centered * centered, axis=1, keepdims=True) / (PATCH * PATCH)
        normed = centered / jnp.sqrt(spread + 1e-05)
        live = iota((slot_count, 1), 0) < spots_ref[5, 0]
        last_ref[...] = jnp.where(live, normed, 0.0).astype(bf16)


def edges_of(top, bottom, left, right):
    rows = jnp.concatenate(
        [top[...].astype(f32)[:, :REACH], bottom[...].astype(f32)[:, BLOCK - REACH :]], axis=1
    )
    line = iota((8, TILE), 0)
    lane = iota((8, TILE), 1)
    first = ((line == lane) & (line < REACH)).astype(bf16)
    last = ((line + TILE - 2 * REACH == lane) & (line >= REACH)).astype(bf16)
    over_lanes = (((1,), (1,)), ((), ()))
    cols = []
    for f in range(rows.shape[0]):
        one = lax.dot_general(first, left[f], over_lanes, preferred_element_type=f32)
        one += lax.dot_general(last, right[f], over_lanes, preferred_element_type=f32)
        cols.append(one[: 2 * REACH].astype(bf16))
    return rows.astype(bf16), cols


def send_all(frames, slab, low, high, whole, sems):
    frame_count = whole.shape[0]
    middle = frame_count - HALF
    spans = [pl.ds(0, middle), pl.ds(middle, HALF)]
    fetches = [
        pltpu.make_async_copy(frames.at[slab, span], whole.at[span], sems.at[i])
        for i, span in enumerate(spans)
    ]
    writes = [
        pltpu.make_async_copy(whole.at[pl.ds(0, HALF)], high, sems.at[2]),
        pltpu.make_async_copy(whole.at[pl.ds(middle, HALF)], low, sems.at[3]),
    ]
    return fetches, writes


def cut_kernel(frames, rim, rim_low, rim_high, low, high, whole, top, bottom, left, right, sems):
    frame_count, row_count, col_count = whole.shape
    reads = [
        pltpu.make_async_copy(source, target, sems.at[4 + i])
        for i, (source, target) in enumerate(
            [
                (frames.at[0, :, pl.ds(0, BLOCK), :], top),
                (frames.at[0, :, pl.ds(row_count - BLOCK, BLOCK), :], bottom),
                (frames.at[0, :, :, pl.ds(0, TILE)], left),
                (frames.at[0, :, :, pl.ds(col_count - TILE, TILE)], right),
            ]
        )
    ]
    fetches, writes = send_all(frames, 1, low, high, whole, sems)
    for copy in reads + fetches:
        copy.start()

    def put(slab, rows, cols):
        middle = frame_count - HALF
        for target, start in [(rim, 0), (rim_low, middle), (rim_high, 0)]:
            count = target.shape[1]
            target[slab, :, :, :col_count] = rows[start : start + count]
            for f in range(count):
                target[slab, f, :, col_count:] = cols[start + f]

    for copy in reads:
        copy.wait()
    put(0, *edges_of(top, bottom, left, right))
    for fetch, write in zip(fetches, writes):
        fetch.wait()
        write.start()
    put(
        1,
        *edges_of(
            whole.at[:, pl.ds(0, BLOCK), :],
            whole.at[:, pl.ds(row_count - BLOCK, BLOCK), :],
            whole.at[:, :, pl.ds(0, TILE)],
            whole.at[:, :, pl.ds(col_count - TILE, TILE)],
        ),
    )
    for write in writes:
        write.wait()


def late_kernel(frames, low, high, whole, sems):
    fetches, writes = send_all(frames, 0, low, high, whole, sems)
    for fetch in fetches:
        fetch.start()
    for fetch, write in zip(fetches, writes):
        fetch.wait()
        write.start()
    for write in writes:
        write.wait()


def cut(frames):
    slabs, frame_count, row_count, col_count = frames.shape
    anywhere = pl.BlockSpec(memory_space=pl.ANY)
    near = pl.BlockSpec(memory_space=pltpu.VMEM)
    piece = jax.ShapeDtypeStruct((HALF, row_count, col_count), bf16)
    wide = col_count + row_count
    rims = [
        jax.ShapeDtypeStruct((slabs, count, 2 * REACH, wide), bf16)
        for count in (frame_count, HALF, HALF)
    ]
    return pl.pallas_call(
        cut_kernel,
        in_specs=[anywhere],
        out_specs=[near] * 3 + [anywhere] * 2,
        out_shape=rims + [piece, piece],
        scratch_shapes=[
            pltpu.VMEM((frame_count, row_count, col_count), bf16),
            pltpu.VMEM((frame_count, BLOCK, col_count), bf16),
            pltpu.VMEM((frame_count, BLOCK, col_count), bf16),
            pltpu.VMEM((frame_count, row_count, TILE), bf16),
            pltpu.VMEM((frame_count, row_count, TILE), bf16),
            pltpu.SemaphoreType.DMA((8,)),
        ],
        compiler_params=pltpu.CompilerParams(vmem_limit_bytes=60 * 1024 * 1024),
        name="cut",
    )(frames)


def late_cut(frames):
    _, frame_count, row_count, col_count = frames.shape
    anywhere = pl.BlockSpec(memory_space=pl.ANY)
    piece = jax.ShapeDtypeStruct((HALF, row_count, col_count), bf16)
    return pl.pallas_call(
        late_kernel,
        in_specs=[anywhere],
        out_specs=[anywhere] * 2,
        out_shape=[piece, piece],
        scratch_shapes=[
            pltpu.VMEM((frame_count, row_count, col_count), bf16),
            pltpu.SemaphoreType.DMA((4,)),
        ],
        compiler_params=pltpu.CompilerParams(vmem_limit_bytes=60 * 1024 * 1024),
        cost_estimate=pl.CostEstimate(flops=0, bytes_accessed=9_000_000, transcendentals=0),
        name="late_cut",
    )(frames)


def run_slab(slab, smoothed, spots, kernel, taps, w2, low, frames, high, edge, below, above):
    _, frame_count, row_count, col_count = frames.shape
    slot_count = spots.shape[1]
    row_step, frame_step = 32, 4
    steps_1 = row_count // row_step
    steps_2 = frame_count // frame_step
    wide = col_count + TILE
    near = frame_count + 2 * HALF

    def row_block(at):
        return jnp.minimum(at, steps_1 - 1)

    def whole(array):
        return pl.BlockSpec(array.shape, lambda at: (0,) * array.ndim)

    operands = [spots, kernel, taps, w2, low, frames, high, edge, below, above]
    in_specs = [
        pl.BlockSpec(memory_space=pltpu.SMEM),
        pl.BlockSpec(memory_space=pltpu.SMEM),
        whole(taps),
        whole(w2),
        pl.BlockSpec((HALF, row_step, col_count), lambda at: (0, row_block(at), 0)),
        pl.BlockSpec((1, frame_count, row_step, col_count), lambda at: (slab, 0, row_block(at), 0)),
        pl.BlockSpec((HALF, row_step, col_count), lambda at: (0, row_block(at), 0)),
        pl.BlockSpec((1, near, row_step, TILE), lambda at: (slab, 0, row_block(at), 0)),
        pl.BlockSpec((1, near, REACH, wide), lambda at: (slab, 0, 0, 0)),
        pl.BlockSpec((1, near, REACH, wide), lambda at: (slab, 0, 0, 0)),
    ]
    aliases = {}
    if smoothed is not None:
        operands.append(smoothed)
        in_specs.append(pl.BlockSpec(memory_space=pl.ANY))
        aliases = {len(operands) - 1: 0}
    count = len(operands)

    def body(*refs):
        slab_kernel(row_step, frame_step, *refs[:10], *refs[count:])

    tall = row_count + 2 * EDGE
    return pl.pallas_call(
        body,
        grid=(steps_1 + steps_2 + 1,),
        in_specs=in_specs,
        out_specs=[
            pl.BlockSpec(
                (1, frame_step, row_count, col_count),
                lambda at: (slab, jnp.clip(at - steps_1, 0, steps_2 - 1), 0, 0),
            ),
            pl.BlockSpec((slot_count, PATCH * PATCH), lambda at: (0, 0)),
        ],
        out_shape=[
            jax.ShapeDtypeStruct(frames.shape, bf16),
            jax.ShapeDtypeStruct((slot_count, PATCH * PATCH), bf16),
        ],
        scratch_shapes=[
            pltpu.VMEM((16 * frame_count, 8 * near), bf16),
            pltpu.VMEM((frame_count, wide // TILE, tall, TILE), bf16),
            pltpu.VMEM((frame_count, wide // TILE, tall, TILE), bf16),
            pltpu.VMEM((frame_count, wide // TILE, tall, TILE), f32),
            pltpu.VMEM((frame_count, wide // TILE, EDGE, TILE), f32),
            pltpu.VMEM((frame_count, wide // TILE, EDGE, TILE), f32),
            pltpu.VMEM((frame_count, col_count // TILE, row_count, TILE), f32),
            pltpu.VMEM((slot_count * PATCH, TILE), bf16),
        ],
        input_output_aliases=aliases,
        compiler_params=pltpu.CompilerParams(vmem_limit_bytes=60 * 1024 * 1024),
        cost_estimate=pl.CostEstimate(
            flops=20_000_000_000, bytes_accessed=16_000_000, transcendentals=0
        ),
        name=f"slab_{slab}",
    )(*operands)


def shards(frames, omega_taps, smooth_kernel, spots, counts):
    _, frame_count, row_count, col_count = frames.shape
    first_frame = lax.axis_index("omega") * frame_count
    first_row = lax.axis_index("row") * row_count
    first_col = lax.axis_index("col") * col_count

    rim, rim_low, rim_high, send_low1, send_high1 = cut(frames)
    rim = jnp.concatenate(
        [shifted(rim_low, "omega", 1), rim, shifted(rim_high, "omega", -1)], axis=1
    )
    low1 = shifted(send_low1, "omega", 1)
    high1 = shifted(send_high1, "omega", -1)
    lane = jnp.arange(TILE, dtype=jnp.int32)[None, :]
    step = jnp.arange(REACH, dtype=jnp.int32)[:, None]
    after = (lane == step).astype(bf16)
    before = (lane == TILE - REACH + step).astype(bf16)
    if lax.axis_size("col") == 2:
        first = lax.axis_index("col") == 0
        sides = jnp.where(first, rim[:, :, REACH:, col_count:], rim[:, :, :REACH, col_count:])
        sides = lax.ppermute(sides, "col", [(0, 1), (1, 0)])
        place = jnp.where(first, after, before)
    else:
        left = shifted(rim[:, :, REACH:, col_count:], "col", 1)
        right = shifted(rim[:, :, :REACH, col_count:], "col", -1)
        sides = jnp.concatenate([right, left], axis=2)
        place = jnp.concatenate([after, before], axis=0)
    later, sides = lax.optimization_barrier((frames, sides))
    send_low0, send_high0 = late_cut(later)
    low0 = shifted(send_low0, "omega", 1)
    high0 = shifted(send_high0, "omega", -1)
    edge = jnp.einsum("sfkr,kc->sfrc", sides, place, preferred_element_type=bf16)
    ends = jnp.concatenate([edge[:, :, :REACH], edge[:, :, -REACH:]], axis=2)
    line = jnp.concatenate([rim[..., :col_count], ends], axis=3)
    above = shifted(line[:, :, REACH:], "row", 1)
    below = shifted(line[:, :, :REACH], "row", -1)

    taps = omega_matrix(
        omega_taps, first_frame, frame_count, frame_count * lax.axis_size("omega")
    )
    w2 = smooth_matrix(smooth_kernel)
    frame, row, col = spots[:, 0] - first_frame, spots[:, 1] - first_row, spots[:, 2] - first_col
    tile = col // TILE
    beside = jnp.minimum(tile + 1, col_count // TILE - 1)
    live = jnp.broadcast_to(counts, frame.shape)
    local = jnp.stack([frame, row, tile, beside, TILE - col % TILE, live], axis=1)

    smoothed, second = run_slab(1, None, local[1], smooth_kernel, taps, w2, low1, frames, high1, edge, below, above)
    count = lax.axis_size("row") * lax.axis_size("col")
    second = lax.ppermute(second, ("row", "col"), [(i, count - 1 - i) for i in range(count)])
    smoothed, first = run_slab(0, smoothed, local[0], smooth_kernel, taps, w2, low0, frames, high0, edge, below, above)
    scores = (
        lax.dot_general(first, second, (((1,), (1,)), ((), ())), preferred_element_type=f32)
        / float(PATCH * PATCH)
    )
    return (smoothed, scores)


def solution(mesh):
    return jax.shard_map(
        shards,
        mesh=mesh,
        in_specs=(
            P(None, "omega", "row", "col"),
            P(),
            P(),
            P(None, None, ("omega", "row", "col")),
            P(None, ("omega", "row", "col")),
        ),
        out_specs=(P(None, "omega", "row", "col"), P(("omega", "row", "col"), None)),
        check_vma=False,
    )
```

```python
import jax
import jax.numpy as jnp
from jax import lax
from jax.experimental import pallas as pl
from jax.experimental.pallas import tpu as pltpu
from jax.sharding import PartitionSpec as P

TAPS = 15
HALF = TAPS // 2
PATCH = 16
SIDE = 5
REACH = SIDE // 2
TILE = 128
BLOCK = 16
WINDOW = 32
EDGE = 8
GROUP = 4
bf16 = jnp.bfloat16
f32 = jnp.float32


def shifted(block, axis, step):
    count = lax.axis_size(axis)
    route = [(i, i + step) for i in range(count) if 0 <= i + step < count]
    return lax.ppermute(block, axis, route)


def split(values):
    high = lax.reduce_precision(values, 8, 7)
    return high.astype(bf16), (values - high).astype(bf16)


def omega_matrix(omega_taps, first_frame, frame_count, frame_total):
    out_ids = jnp.arange(frame_count, dtype=jnp.int32)[:, None]
    in_ids = jnp.arange(frame_count + 2 * HALF, dtype=jnp.int32)[None, :]
    source = first_frame + in_ids - HALF
    valid = (source >= 0) & (source < frame_total)
    tap = jnp.where(valid, in_ids - out_ids, -1)
    hit = tap[:, :, None] == jnp.arange(TAPS, dtype=jnp.int32)
    weights = jnp.sum(jnp.where(hit, omega_taps, 0.0), axis=2)
    norm = jnp.sum(weights, axis=1, keepdims=True)
    center = (in_ids - out_ids == HALF).astype(f32)
    matrix = center - weights / norm
    return jnp.stack(split(matrix), axis=1).reshape(2 * frame_count, matrix.shape[1])


def smooth_matrix(smooth_kernel):
    depth = WINDOW + 2 * EDGE
    out_ids = jnp.arange(WINDOW, dtype=jnp.int32)[:, None]
    in_ids = jnp.arange(depth, dtype=jnp.int32)[None, :]
    step = in_ids - out_ids - (EDGE - REACH)
    hit = step[None, :, :, None] == jnp.arange(SIDE, dtype=jnp.int32)
    table = jnp.sum(jnp.where(hit, smooth_kernel.T[:, None, None, :], 0.0), axis=3)
    table = jnp.swapaxes(table.reshape(SIDE, WINDOW // BLOCK, BLOCK, depth), 0, 1)
    high, low = split(table)
    return jnp.concatenate([high, high, low], axis=3).reshape(SIDE * WINDOW, 3 * depth)


def iota(shape, dim):
    return lax.broadcasted_iota(jnp.int32, shape, dim)


def slab_kernel(
    row_step, frame_step,
    spots_ref, taps_ref, w2_ref, low_ref, own_ref, high_ref, edge_ref, below_ref, above_ref,
    out_ref, last_ref, w1, chi, clo, carry, outer, kept, flat,
):
    frame_count, tiles, row_count, _ = kept.shape
    near = taps_ref.shape[1]
    steps_1 = row_count // row_step
    steps_2 = frame_count // frame_step
    at = pl.program_id(0)

    def filtered(block):
        part = block.reshape(near * 8, block.shape[2])
        both = jnp.dot(w1[...], part, preferred_element_type=f32)
        both = both.reshape(frame_count, 2, 8, block.shape[2])
        return both[:, 0] + both[:, 1]

    def keep(above, below, tile, place):
        value = jnp.concatenate([above, below], axis=1)
        high = value.astype(bf16)
        chi[:, tile, place, :] = high
        clo[:, tile, place, :] = (value - high.astype(f32)).astype(bf16)

    @pl.when(at == 0)
    def _():
        count = 2 * frame_count
        tall = (iota((8 * count, count), 0) // 8 == iota((8 * count, count), 1)).astype(bf16)
        wide = (iota((near, 8 * near), 1) // 8 == iota((near, 8 * near), 0)).astype(bf16)
        full = jnp.dot(tall, taps_ref[...], preferred_element_type=f32).astype(bf16)
        full = jnp.dot(full, wide, preferred_element_type=f32)
        same = iota(full.shape, 0) % 8 == iota(full.shape, 1) % 8
        w1[...] = jnp.where(same, full, 0.0).astype(bf16)
        for tile in range(0, tiles + 1, GROUP):
            pair = range(tile, min(tile + GROUP, tiles + 1))
            cols = slice(tile * TILE, (tile + len(pair)) * TILE)
            below = below_ref[0, :, :, cols].astype(f32)
            above = above_ref[0, :, :, cols].astype(f32)
            gap = jnp.zeros((near, 8 - 2 * REACH, below.shape[2]), f32)
            both = filtered(jnp.concatenate([below, gap, above], axis=1).astype(bf16))
            for q, one in enumerate(pair):
                carry[:, one] = both[..., q * TILE : (q + 1) * TILE]
                outer[:, one] = both[..., q * TILE : (q + 1) * TILE]

    @pl.when(at < steps_1)
    def _():
        def keep_all(tile, parts):
            parts = [carry[:, tile]] + parts
            for q in range(0, len(parts) - 1, 2):
                place = pl.ds(pl.multiple_of(at * row_step + EDGE * q, BLOCK), BLOCK)
                keep(parts[q], parts[q + 1], tile, place)
            carry[:, tile] = parts[-1]

        for tile in range(0, tiles, 2):
            group = range(tile, min(tile + 2, tiles))
            cols = slice(tile * TILE, (tile + len(group)) * TILE)
            parts = []
            for h in range(0, row_step, EDGE):
                rows = slice(h, h + EDGE)
                block = jnp.concatenate(
                    [low_ref[:, rows, cols], own_ref[0, :, rows, cols], high_ref[:, rows, cols]],
                    axis=0,
                )
                parts.append(filtered(block))
            for q, one in enumerate(group):
                keep_all(one, [part[..., q * TILE : (q + 1) * TILE] for part in parts])
        both = filtered(
            jnp.concatenate(
                [edge_ref[0, :, h : h + EDGE] for h in range(0, row_step, EDGE)], axis=2
            )
        )
        parts = [both[..., h * TILE : (h + 1) * TILE] for h in range(row_step // EDGE)]
        keep_all(tiles, parts)

    @pl.when(at == steps_1 - 1)
    def _():
        for tile in range(tiles + 1):
            keep(carry[:, tile], outer[:, tile], tile, slice(row_count, row_count + BLOCK))

    @pl.when((at >= steps_1) & (at < steps_1 + steps_2))
    def _():
        lane = iota((BLOCK, TILE), 1)
        edge_of = [lane < 2, lane < 1, None, lane >= TILE - 1, lane >= TILE - 2]

        depth = WINDOW + 2 * EDGE
        parts_of = range(WINDOW // BLOCK)

        def two_frames(k2, unused):
            for row in range(0, row_count, WINDOW):
                turned = {}
                done = [0, 0]

                def finish(f, tile):
                    k = k2 * 2 + f
                    frame = (at - steps_1) * frame_step + k
                    for m in parts_of:
                        total = turned[f, m, REACH, tile]
                        for b in range(SIDE):
                            if b != REACH:
                                beside = (tile + (1 if b > REACH else -1)) % (tiles + 1)
                                total = total + jnp.where(
                                    edge_of[b], turned[f, m, b, beside], turned[f, m, b, tile]
                                )
                        value = total.astype(bf16)
                        rows = slice(row + m * BLOCK, row + (m + 1) * BLOCK)
                        out_ref[0, k, rows, tile * TILE : (tile + 1) * TILE] = value
                        kept[frame, tile, rows, :] = value.astype(f32)

                order = [(f, tile) for f in range(2) for tile in [tiles] + list(range(tiles))]
                for p in range(0, len(order), GROUP):
                    pair = order[p : p + GROUP]
                    stacks = []
                    for f, tile in pair:
                        frame = (at - steps_1) * frame_step + k2 * 2 + f
                        high = chi[frame, tile, row : row + depth, :]
                        low = clo[frame, tile, row : row + depth, :]
                        stacks.append(jnp.concatenate([high, low, high], axis=0))
                    both = jnp.dot(
                        w2_ref[...], jnp.concatenate(stacks, axis=1), preferred_element_type=f32
                    )
                    for q, (f, tile) in enumerate(pair):
                        for m in parts_of:
                            for b in range(SIDE):
                                at_row = (m * SIDE + b) * BLOCK
                                part = both[at_row : at_row + BLOCK, q * TILE : (q + 1) * TILE]
                                if b != REACH:
                                    part = pltpu.roll(part, (REACH - b) % TILE, 1)
                                turned[f, m, b, tile] = part
                    for f in range(2):
                        while done[f] < tiles and (f, 0, 0, done[f]) in turned:
                            after = min(done[f] + 1, tiles)
                            if (f, 0, 0, after) not in turned:
                                break
                            finish(f, done[f])
                            done[f] += 1
            return unused

        lax.fori_loop(0, frame_step // 2, two_frames, 0)

    @pl.when(at == steps_1 + steps_2)
    def _():
        slot_count = flat.shape[0] // PATCH

        lane = iota((PATCH, TILE), 1)

        def some(i8, unused):
            for j in range(16):
                i = i8 * 16 + j
                frame, row, tile = spots_ref[0, i], spots_ref[1, i], spots_ref[2, i]
                beside, turn = spots_ref[3, i], spots_ref[4, i]
                here = kept[frame, tile, pl.ds(row, PATCH), :]
                there = kept[frame, beside, pl.ds(row, PATCH), :]
                shift = turn & (TILE - 1)
                here, there = pltpu.roll(here, shift, 1), pltpu.roll(there, shift, 1)
                part = jnp.where(lane < turn, here, there)
                flat[pl.ds(pl.multiple_of(i * PATCH, PATCH), PATCH), :] = part.astype(bf16)
            return unused

        lax.fori_loop(0, slot_count // 16, some, 0)
        low_bits = PATCH - 1
        bits = low_bits.bit_length()
        shape = (TILE, PATCH * PATCH)
        repeat = (iota(shape, 1) & low_bits == iota(shape, 0)).astype(bf16)
        rows = jnp.dot(flat[...], repeat, preferred_element_type=f32)
        mine = iota(rows.shape, 1) >> bits == iota(rows.shape, 0) & low_bits
        rows = jnp.where(mine, rows, 0.0).astype(bf16)
        shape = (slot_count, rows.shape[0])
        owner = (iota(shape, 1) >> bits == iota(shape, 0)).astype(bf16)
        values = jnp.dot(owner, rows, preferred_element_type=f32)
        mean = jnp.sum(values, axis=1, keepdims=True) / (PATCH * PATCH)
        centered = values - mean
        spread = jnp.sum(centered * centered, axis=1, keepdims=True) / (PATCH * PATCH)
        normed = centered / jnp.sqrt(spread + 1e-05)
        live = iota((slot_count, 1), 0) < spots_ref[5, 0]
        last_ref[...] = jnp.where(live, normed, 0.0).astype(bf16)


def edges_of(top, bottom, left, right):
    rows = jnp.concatenate(
        [top[...].astype(f32)[:, :REACH], bottom[...].astype(f32)[:, BLOCK - REACH :]], axis=1
    )
    line = iota((8, TILE), 0)
    lane = iota((8, TILE), 1)
    first = ((line == lane) & (line < REACH)).astype(bf16)
    last = ((line + TILE - 2 * REACH == lane) & (line >= REACH)).astype(bf16)
    over_lanes = (((1,), (1,)), ((), ()))
    cols = []
    for f in range(rows.shape[0]):
        one = lax.dot_general(first, left[f], over_lanes, preferred_element_type=f32)
        one += lax.dot_general(last, right[f], over_lanes, preferred_element_type=f32)
        cols.append(one[: 2 * REACH].astype(bf16))
    return rows.astype(bf16), cols


def send_all(frames, slab, low, high, whole, sems):
    frame_count = whole.shape[0]
    middle = frame_count - HALF
    spans = [pl.ds(0, middle), pl.ds(middle, HALF)]
    fetches = [
        pltpu.make_async_copy(frames.at[slab, span], whole.at[span], sems.at[i])
        for i, span in enumerate(spans)
    ]
    writes = [
        pltpu.make_async_copy(whole.at[pl.ds(0, HALF)], high, sems.at[2]),
        pltpu.make_async_copy(whole.at[pl.ds(middle, HALF)], low, sems.at[3]),
    ]
    return fetches, writes


def cut_kernel(frames, rim, rim_low, rim_high, low, high, whole, top, bottom, left, right, sems):
    frame_count, row_count, col_count = whole.shape
    reads = [
        pltpu.make_async_copy(source, target, sems.at[4 + i])
        for i, (source, target) in enumerate(
            [
                (frames.at[0, :, pl.ds(0, BLOCK), :], top),
                (frames.at[0, :, pl.ds(row_count - BLOCK, BLOCK), :], bottom),
                (frames.at[0, :, :, pl.ds(0, TILE)], left),
                (frames.at[0, :, :, pl.ds(col_count - TILE, TILE)], right),
            ]
        )
    ]
    fetches, writes = send_all(frames, 1, low, high, whole, sems)
    for copy in reads + fetches:
        copy.start()

    def put(slab, rows, cols):
        middle = frame_count - HALF
        for target, start in [(rim, 0), (rim_low, middle), (rim_high, 0)]:
            count = target.shape[1]
            target[slab, :, :, :col_count] = rows[start : start + count]
            for f in range(count):
                target[slab, f, :, col_count:] = cols[start + f]

    for copy in reads:
        copy.wait()
    put(0, *edges_of(top, bottom, left, right))
    for fetch, write in zip(fetches, writes):
        fetch.wait()
        write.start()
    put(
        1,
        *edges_of(
            whole.at[:, pl.ds(0, BLOCK), :],
            whole.at[:, pl.ds(row_count - BLOCK, BLOCK), :],
            whole.at[:, :, pl.ds(0, TILE)],
            whole.at[:, :, pl.ds(col_count - TILE, TILE)],
        ),
    )
    for write in writes:
        write.wait()


def late_kernel(frames, low, high, whole, sems):
    fetches, writes = send_all(frames, 0, low, high, whole, sems)
    for fetch in fetches:
        fetch.start()
    for fetch, write in zip(fetches, writes):
        fetch.wait()
        write.start()
    for write in writes:
        write.wait()


def cut(frames):
    slabs, frame_count, row_count, col_count = frames.shape
    anywhere = pl.BlockSpec(memory_space=pl.ANY)
    near = pl.BlockSpec(memory_space=pltpu.VMEM)
    piece = jax.ShapeDtypeStruct((HALF, row_count, col_count), bf16)
    wide = col_count + row_count
    rims = [
        jax.ShapeDtypeStruct((slabs, count, 2 * REACH, wide), bf16)
        for count in (frame_count, HALF, HALF)
    ]
    return pl.pallas_call(
        cut_kernel,
        in_specs=[anywhere],
        out_specs=[near] * 3 + [anywhere] * 2,
        out_shape=rims + [piece, piece],
        scratch_shapes=[
            pltpu.VMEM((frame_count, row_count, col_count), bf16),
            pltpu.VMEM((frame_count, BLOCK, col_count), bf16),
            pltpu.VMEM((frame_count, BLOCK, col_count), bf16),
            pltpu.VMEM((frame_count, row_count, TILE), bf16),
            pltpu.VMEM((frame_count, row_count, TILE), bf16),
            pltpu.SemaphoreType.DMA((8,)),
        ],
        compiler_params=pltpu.CompilerParams(vmem_limit_bytes=60 * 1024 * 1024),
        name="cut",
    )(frames)


def late_cut(frames):
    _, frame_count, row_count, col_count = frames.shape
    anywhere = pl.BlockSpec(memory_space=pl.ANY)
    piece = jax.ShapeDtypeStruct((HALF, row_count, col_count), bf16)
    return pl.pallas_call(
        late_kernel,
        in_specs=[anywhere],
        out_specs=[anywhere] * 2,
        out_shape=[piece, piece],
        scratch_shapes=[
            pltpu.VMEM((frame_count, row_count, col_count), bf16),
            pltpu.SemaphoreType.DMA((4,)),
        ],
        compiler_params=pltpu.CompilerParams(vmem_limit_bytes=60 * 1024 * 1024),
        cost_estimate=pl.CostEstimate(flops=0, bytes_accessed=9_000_000, transcendentals=0),
        name="late_cut",
    )(frames)


def run_slab(slab, smoothed, spots, taps, w2, low, frames, high, edge, below, above):
    _, frame_count, row_count, col_count = frames.shape
    slot_count = spots.shape[1]
    row_step, frame_step = 32, 4
    steps_1 = row_count // row_step
    steps_2 = frame_count // frame_step
    wide = col_count + TILE
    near = frame_count + 2 * HALF

    def row_block(at):
        return jnp.minimum(at, steps_1 - 1)

    def whole(array):
        return pl.BlockSpec(array.shape, lambda at: (0,) * array.ndim)

    operands = [spots, taps, w2, low, frames, high, edge, below, above]
    in_specs = [
        pl.BlockSpec(memory_space=pltpu.SMEM),
        whole(taps),
        whole(w2),
        pl.BlockSpec((HALF, row_step, col_count), lambda at: (0, row_block(at), 0)),
        pl.BlockSpec((1, frame_count, row_step, col_count), lambda at: (slab, 0, row_block(at), 0)),
        pl.BlockSpec((HALF, row_step, col_count), lambda at: (0, row_block(at), 0)),
        pl.BlockSpec((1, near, row_step, TILE), lambda at: (slab, 0, row_block(at), 0)),
        pl.BlockSpec((1, near, REACH, wide), lambda at: (slab, 0, 0, 0)),
        pl.BlockSpec((1, near, REACH, wide), lambda at: (slab, 0, 0, 0)),
    ]
    aliases = {}
    if smoothed is not None:
        operands.append(smoothed)
        in_specs.append(pl.BlockSpec(memory_space=pl.ANY))
        aliases = {len(operands) - 1: 0}
    count = len(operands)

    def body(*refs):
        slab_kernel(row_step, frame_step, *refs[:9], *refs[count:])

    tall = row_count + 2 * EDGE
    return pl.pallas_call(
        body,
        grid=(steps_1 + steps_2 + 1,),
        in_specs=in_specs,
        out_specs=[
            pl.BlockSpec(
                (1, frame_step, row_count, col_count),
                lambda at: (slab, jnp.clip(at - steps_1, 0, steps_2 - 1), 0, 0),
            ),
            pl.BlockSpec((slot_count, PATCH * PATCH), lambda at: (0, 0)),
        ],
        out_shape=[
            jax.ShapeDtypeStruct(frames.shape, bf16),
            jax.ShapeDtypeStruct((slot_count, PATCH * PATCH), bf16),
        ],
        scratch_shapes=[
            pltpu.VMEM((16 * frame_count, 8 * near), bf16),
            pltpu.VMEM((frame_count, wide // TILE, tall, TILE), bf16),
            pltpu.VMEM((frame_count, wide // TILE, tall, TILE), bf16),
            pltpu.VMEM((frame_count, wide // TILE, EDGE, TILE), f32),
            pltpu.VMEM((frame_count, wide // TILE, EDGE, TILE), f32),
            pltpu.VMEM((frame_count, col_count // TILE, row_count, TILE), f32),
            pltpu.VMEM((slot_count * PATCH, TILE), bf16),
        ],
        input_output_aliases=aliases,
        compiler_params=pltpu.CompilerParams(vmem_limit_bytes=60 * 1024 * 1024),
        cost_estimate=pl.CostEstimate(
            flops=20_000_000_000, bytes_accessed=16_000_000, transcendentals=0
        ),
        name=f"slab_{slab}",
    )(*operands)


def shards(frames, omega_taps, smooth_kernel, spots, counts):
    _, frame_count, row_count, col_count = frames.shape
    first_frame = lax.axis_index("omega") * frame_count
    first_row = lax.axis_index("row") * row_count
    first_col = lax.axis_index("col") * col_count

    rim, rim_low, rim_high, send_low1, send_high1 = cut(frames)
    rim = jnp.concatenate(
        [shifted(rim_low, "omega", 1), rim, shifted(rim_high, "omega", -1)], axis=1
    )
    low1 = shifted(send_low1, "omega", 1)
    high1 = shifted(send_high1, "omega", -1)
    lane = jnp.arange(TILE, dtype=jnp.int32)[None, :]
    step = jnp.arange(REACH, dtype=jnp.int32)[:, None]
    after = (lane == step).astype(bf16)
    before = (lane == TILE - REACH + step).astype(bf16)
    if lax.axis_size("col") == 2:
        first = lax.axis_index("col") == 0
        sides = jnp.where(first, rim[:, :, REACH:, col_count:], rim[:, :, :REACH, col_count:])
        sides = lax.ppermute(sides, "col", [(0, 1), (1, 0)])
        place = jnp.where(first, after, before)
    else:
        left = shifted(rim[:, :, REACH:, col_count:], "col", 1)
        right = shifted(rim[:, :, :REACH, col_count:], "col", -1)
        sides = jnp.concatenate([right, left], axis=2)
        place = jnp.concatenate([after, before], axis=0)
    later, sides = lax.optimization_barrier((frames, sides))
    send_low0, send_high0 = late_cut(later)
    low0 = shifted(send_low0, "omega", 1)
    high0 = shifted(send_high0, "omega", -1)
    edge = jnp.einsum("sfkr,kc->sfrc", sides, place, preferred_element_type=bf16)
    ends = jnp.concatenate([edge[:, :, :REACH], edge[:, :, -REACH:]], axis=2)
    line = jnp.concatenate([rim[..., :col_count], ends], axis=3)
    above = shifted(line[:, :, REACH:], "row", 1)
    below = shifted(line[:, :, :REACH], "row", -1)

    taps = omega_matrix(
        omega_taps, first_frame, frame_count, frame_count * lax.axis_size("omega")
    )
    w2 = smooth_matrix(smooth_kernel)
    frame, row, col = spots[:, 0] - first_frame, spots[:, 1] - first_row, spots[:, 2] - first_col
    tile = col // TILE
    beside = jnp.minimum(tile + 1, col_count // TILE - 1)
    live = jnp.broadcast_to(counts, frame.shape)
    local = jnp.stack([frame, row, tile, beside, TILE - col % TILE, live], axis=1)

    smoothed, second = run_slab(1, None, local[1], taps, w2, low1, frames, high1, edge, below, above)
    count = lax.axis_size("row") * lax.axis_size("col")
    second = lax.ppermute(second, ("row", "col"), [(i, count - 1 - i) for i in range(count)])
    smoothed, first = run_slab(0, smoothed, local[0], taps, w2, low0, frames, high0, edge, below, above)
    scores = (
        lax.dot_general(first, second, (((1,), (1,)), ((), ())), preferred_element_type=f32)
        / float(PATCH * PATCH)
    )
    return (smoothed, scores)


def solution(mesh):
    return jax.shard_map(
        shards,
        mesh=mesh,
        in_specs=(
            P(None, "omega", "row", "col"),
            P(),
            P(),
            P(None, None, ("omega", "row", "col")),
            P(None, ("omega", "row", "col")),
        ),
        out_specs=(P(None, "omega", "row", "col"), P(("omega", "row", "col"), None)),
        check_vma=False,
    )
```

```python
import jax
import jax.numpy as jnp
from jax import lax
from jax.experimental import pallas as pl
from jax.experimental.pallas import tpu as pltpu
from jax.sharding import PartitionSpec as P

TAPS = 15
HALF = TAPS // 2
PATCH = 16
SIDE = 5
REACH = SIDE // 2
TILE = 128
BLOCK = 16
WINDOW = 16
EDGE = 8
GROUP = 4
bf16 = jnp.bfloat16
f32 = jnp.float32


def shifted(block, axis, step):
    count = lax.axis_size(axis)
    route = [(i, i + step) for i in range(count) if 0 <= i + step < count]
    return lax.ppermute(block, axis, route)


def split(values):
    high = lax.reduce_precision(values, 8, 7)
    return high.astype(bf16), (values - high).astype(bf16)


def omega_matrix(omega_taps, first_frame, frame_count, frame_total):
    out_ids = jnp.arange(frame_count, dtype=jnp.int32)[:, None]
    in_ids = jnp.arange(frame_count + 2 * HALF, dtype=jnp.int32)[None, :]
    source = first_frame + in_ids - HALF
    valid = (source >= 0) & (source < frame_total)
    tap = jnp.where(valid, in_ids - out_ids, -1)
    hit = tap[:, :, None] == jnp.arange(TAPS, dtype=jnp.int32)
    weights = jnp.sum(jnp.where(hit, omega_taps, 0.0), axis=2)
    norm = jnp.sum(weights, axis=1, keepdims=True)
    center = (in_ids - out_ids == HALF).astype(f32)
    matrix = center - weights / norm
    return jnp.stack(split(matrix), axis=1).reshape(2 * frame_count, matrix.shape[1])


def smooth_matrix(smooth_kernel):
    depth = WINDOW + 2 * EDGE
    out_ids = jnp.arange(WINDOW, dtype=jnp.int32)[:, None]
    in_ids = jnp.arange(depth, dtype=jnp.int32)[None, :]
    step = in_ids - out_ids - (EDGE - REACH)
    hit = step[None, :, :, None] == jnp.arange(SIDE, dtype=jnp.int32)
    steps = jnp.concatenate([smooth_kernel.T, jnp.zeros((1, SIDE), f32)], axis=0)
    table = jnp.sum(jnp.where(hit, steps[:, None, None, :], 0.0), axis=3)
    high, low = split(table)
    table = jnp.concatenate([high, high, low], axis=2)
    table = table.reshape((SIDE + 1) // 2, 2, WINDOW, 3 * depth)
    return jnp.concatenate([table[:, 0], table[:, 1]], axis=2).reshape(-1, 6 * depth)


def iota(shape, dim):
    return lax.broadcasted_iota(jnp.int32, shape, dim)


def slab_kernel(
    row_step, frame_step,
    spots_ref, taps_ref, w2_ref, low_ref, own_ref, high_ref, edge_ref, below_ref, above_ref,
    out_ref, last_ref, w1, chi, clo, chi1, clo1, carry, outer, kept, flat,
):
    frame_count, tiles, row_count, _ = kept.shape
    near = taps_ref.shape[1]
    steps_1 = row_count // row_step
    steps_2 = frame_count // frame_step
    at = pl.program_id(0)

    def filtered(block):
        part = block.reshape(near * 8, block.shape[2])
        both = jnp.dot(w1[...], part, preferred_element_type=f32)
        both = both.reshape(frame_count, 2, 8, block.shape[2])
        return both[:, 0] + both[:, 1]

    def keep_one(value, highs, lows, tile, place):
        high = value.astype(bf16)
        highs[:, tile, place, :] = high
        lows[:, tile, place, :] = (value - high.astype(f32)).astype(bf16)

    def keep(value, tile, place):
        keep_one(value, chi, clo, tile, place)

    def keep_shifted(turned, after, tile, place):
        last = iota(turned.shape, 2) == TILE - 1
        keep_one(jnp.where(last, after, turned), chi1, clo1, tile, place)

    def turn(value):
        return pltpu.roll(value, TILE - 1, 2)

    @pl.when(at == 0)
    def _():
        count = 2 * frame_count
        tall = (iota((8 * count, count), 0) // 8 == iota((8 * count, count), 1)).astype(bf16)
        wide = (iota((near, 8 * near), 1) // 8 == iota((near, 8 * near), 0)).astype(bf16)
        full = jnp.dot(tall, taps_ref[...], preferred_element_type=f32).astype(bf16)
        full = jnp.dot(full, wide, preferred_element_type=f32)
        same = iota(full.shape, 0) % 8 == iota(full.shape, 1) % 8
        w1[...] = jnp.where(same, full, 0.0).astype(bf16)
        for tile in range(0, tiles + 1, GROUP):
            pair = range(tile, min(tile + GROUP, tiles + 1))
            cols = slice(tile * TILE, (tile + len(pair)) * TILE)
            below = below_ref[0, :, :, cols].astype(f32)
            above = above_ref[0, :, :, cols].astype(f32)
            gap = jnp.zeros((near, 8 - 2 * REACH, below.shape[2]), f32)
            both = filtered(jnp.concatenate([below, gap, above], axis=1).astype(bf16))
            for q, one in enumerate(pair):
                carry[:, one] = both[..., q * TILE : (q + 1) * TILE]
                outer[:, one] = both[..., q * TILE : (q + 1) * TILE]

    @pl.when(at < steps_1)
    def _():
        places = [
            pl.ds(pl.multiple_of(at * row_step + q * BLOCK, BLOCK), BLOCK)
            for q in range(row_step // BLOCK)
        ]
        turns = {}

        def keep_all(tile, parts):
            parts = [carry[:, tile]] + parts
            turns[tile] = []
            for q, place in enumerate(places):
                value = jnp.concatenate(parts[2 * q : 2 * q + 2], axis=1)
                keep(value, tile, place)
                turns[tile].append(turn(value))
            carry[:, tile] = parts[-1]
            before = (tile - 1) % (tiles + 1)
            if before in turns:
                for one, after, place in zip(turns[before], turns[tile], places):
                    keep_shifted(one, after, before, place)

        both = filtered(
            jnp.concatenate(
                [edge_ref[0, :, h : h + EDGE] for h in range(0, row_step, EDGE)], axis=2
            )
        )
        keep_all(tiles, [both[..., h * TILE : (h + 1) * TILE] for h in range(row_step // EDGE)])
        for tile in range(0, tiles, 2):
            group = range(tile, min(tile + 2, tiles))
            cols = slice(tile * TILE, (tile + len(group)) * TILE)
            parts = []
            for h in range(0, row_step, EDGE):
                rows = slice(h, h + EDGE)
                block = jnp.concatenate(
                    [low_ref[:, rows, cols], own_ref[0, :, rows, cols], high_ref[:, rows, cols]],
                    axis=0,
                )
                parts.append(filtered(block))
            for q, one in enumerate(group):
                keep_all(one, [part[..., q * TILE : (q + 1) * TILE] for part in parts])
        for one, after, place in zip(turns[tiles - 1], turns[tiles], places):
            keep_shifted(one, after, tiles - 1, place)

    @pl.when(at == steps_1 - 1)
    def _():
        place = slice(row_count, row_count + BLOCK)
        first = None
        for tile in range(tiles, -1, -1):
            value = jnp.concatenate([carry[:, tile], outer[:, tile]], axis=1)
            keep(value, tile, place)
            turned = turn(value)
            if tile == tiles:
                first = turned
            else:
                keep_shifted(turned, after, tile, place)
            after = turned
        keep_shifted(first, after, tiles, place)

    @pl.when((at >= steps_1) & (at < steps_1 + steps_2))
    def _():
        lane = iota((BLOCK, TILE), 1)
        depth = WINDOW + 2 * EDGE

        def two_frames(k2, unused):
            for row in range(0, row_count, WINDOW):
                turned = {}
                done = [0, 0]

                def finish(f, tile):
                    k = k2 * 2 + f
                    frame = (at - steps_1) * frame_step + k
                    before, beyond = (tile - 1) % (tiles + 1), (tile + 1) % (tiles + 1)
                    left = jnp.where(lane < REACH, turned[f, 0, before], turned[f, 0, tile])
                    right = jnp.where(
                        lane >= TILE - REACH, turned[f, 2, beyond], turned[f, 2, tile]
                    )
                    value = (turned[f, 1, tile] + left + right).astype(bf16)
                    rows = slice(row, row + BLOCK)
                    out_ref[0, k, rows, tile * TILE : (tile + 1) * TILE] = value
                    kept[frame, tile, rows, :] = value.astype(f32)

                order = [(f, tile) for f in range(2) for tile in [tiles] + list(range(tiles))]
                for p in range(0, len(order), GROUP):
                    pair = order[p : p + GROUP]
                    stacks = []
                    for f, tile in pair:
                        frame = (at - steps_1) * frame_step + k2 * 2 + f
                        stack = []
                        for highs, lows in ((chi, clo), (chi1, clo1)):
                            high = highs[frame, tile, row : row + depth, :]
                            low = lows[frame, tile, row : row + depth, :]
                            stack += [high, low, high]
                        stacks.append(jnp.concatenate(stack, axis=0))
                    both = jnp.dot(
                        w2_ref[...], jnp.concatenate(stacks, axis=1), preferred_element_type=f32
                    )
                    for q, (f, tile) in enumerate(pair):
                        for g in range((SIDE + 1) // 2):
                            part = both[g * BLOCK : (g + 1) * BLOCK, q * TILE : (q + 1) * TILE]
                            if g != 1:
                                part = pltpu.roll(part, (REACH - 2 * g) % TILE, 1)
                            turned[f, g, tile] = part
                    for f in range(2):
                        while done[f] < tiles and (f, 0, done[f]) in turned:
                            after = min(done[f] + 1, tiles)
                            if (f, 0, after) not in turned:
                                break
                            finish(f, done[f])
                            done[f] += 1
            return unused

        lax.fori_loop(0, frame_step // 2, two_frames, 0)

    @pl.when(at == steps_1 + steps_2)
    def _():
        slot_count = flat.shape[0] // PATCH

        lane = iota((PATCH, TILE), 1)

        def some(i8, unused):
            for j in range(16):
                i = i8 * 16 + j
                frame, row, tile = spots_ref[0, i], spots_ref[1, i], spots_ref[2, i]
                beside, turn = spots_ref[3, i], spots_ref[4, i]
                here = kept[frame, tile, pl.ds(row, PATCH), :]
                there = kept[frame, beside, pl.ds(row, PATCH), :]
                shift = turn & (TILE - 1)
                here, there = pltpu.roll(here, shift, 1), pltpu.roll(there, shift, 1)
                part = jnp.where(lane < turn, here, there)
                flat[pl.ds(pl.multiple_of(i * PATCH, PATCH), PATCH), :] = part.astype(bf16)
            return unused

        lax.fori_loop(0, slot_count // 16, some, 0)
        low_bits = PATCH - 1
        bits = low_bits.bit_length()
        shape = (TILE, PATCH * PATCH)
        repeat = (iota(shape, 1) & low_bits == iota(shape, 0)).astype(bf16)
        rows = jnp.dot(flat[...], repeat, preferred_element_type=f32)
        mine = iota(rows.shape, 1) >> bits == iota(rows.shape, 0) & low_bits
        rows = jnp.where(mine, rows, 0.0).astype(bf16)
        shape = (slot_count, rows.shape[0])
        owner = (iota(shape, 1) >> bits == iota(shape, 0)).astype(bf16)
        values = jnp.dot(owner, rows, preferred_element_type=f32)
        mean = jnp.sum(values, axis=1, keepdims=True) / (PATCH * PATCH)
        centered = values - mean
        spread = jnp.sum(centered * centered, axis=1, keepdims=True) / (PATCH * PATCH)
        normed = centered / jnp.sqrt(spread + 1e-05)
        live = iota((slot_count, 1), 0) < spots_ref[5, 0]
        last_ref[...] = jnp.where(live, normed, 0.0).astype(bf16)


def edges_of(top, bottom, left, right):
    rows = jnp.concatenate(
        [top[...].astype(f32)[:, :REACH], bottom[...].astype(f32)[:, BLOCK - REACH :]], axis=1
    )
    line = iota((8, TILE), 0)
    lane = iota((8, TILE), 1)
    first = ((line == lane) & (line < REACH)).astype(bf16)
    last = ((line + TILE - 2 * REACH == lane) & (line >= REACH)).astype(bf16)
    over_lanes = (((1,), (1,)), ((), ()))
    cols = []
    for f in range(rows.shape[0]):
        one = lax.dot_general(first, left[f], over_lanes, preferred_element_type=f32)
        one += lax.dot_general(last, right[f], over_lanes, preferred_element_type=f32)
        cols.append(one[: 2 * REACH].astype(bf16))
    return rows.astype(bf16), cols


def send_all(frames, slab, low, high, whole, sems):
    frame_count = whole.shape[0]
    middle = frame_count - HALF
    spans = [pl.ds(0, middle), pl.ds(middle, HALF)]
    fetches = [
        pltpu.make_async_copy(frames.at[slab, span], whole.at[span], sems.at[i])
        for i, span in enumerate(spans)
    ]
    writes = [
        pltpu.make_async_copy(whole.at[pl.ds(0, HALF)], high, sems.at[2]),
        pltpu.make_async_copy(whole.at[pl.ds(middle, HALF)], low, sems.at[3]),
    ]
    return fetches, writes


def cut_kernel(frames, rim, rim_low, rim_high, low, high, whole, top, bottom, left, right, sems):
    frame_count, row_count, col_count = whole.shape
    reads = [
        pltpu.make_async_copy(source, target, sems.at[4 + i])
        for i, (source, target) in enumerate(
            [
                (frames.at[0, :, pl.ds(0, BLOCK), :], top),
                (frames.at[0, :, pl.ds(row_count - BLOCK, BLOCK), :], bottom),
                (frames.at[0, :, :, pl.ds(0, TILE)], left),
                (frames.at[0, :, :, pl.ds(col_count - TILE, TILE)], right),
            ]
        )
    ]
    fetches, writes = send_all(frames, 1, low, high, whole, sems)
    for copy in reads + fetches:
        copy.start()

    def put(slab, rows, cols):
        middle = frame_count - HALF
        for target, start in [(rim, 0), (rim_low, middle), (rim_high, 0)]:
            count = target.shape[1]
            target[slab, :, :, :col_count] = rows[start : start + count]
            for f in range(count):
                target[slab, f, :, col_count:] = cols[start + f]

    for copy in reads:
        copy.wait()
    put(0, *edges_of(top, bottom, left, right))
    for fetch, write in zip(fetches, writes):
        fetch.wait()
        write.start()
    put(
        1,
        *edges_of(
            whole.at[:, pl.ds(0, BLOCK), :],
            whole.at[:, pl.ds(row_count - BLOCK, BLOCK), :],
            whole.at[:, :, pl.ds(0, TILE)],
            whole.at[:, :, pl.ds(col_count - TILE, TILE)],
        ),
    )
    for write in writes:
        write.wait()


def late_kernel(frames, low, high, whole, sems):
    fetches, writes = send_all(frames, 0, low, high, whole, sems)
    for fetch in fetches:
        fetch.start()
    for fetch, write in zip(fetches, writes):
        fetch.wait()
        write.start()
    for write in writes:
        write.wait()


def cut(frames):
    slabs, frame_count, row_count, col_count = frames.shape
    anywhere = pl.BlockSpec(memory_space=pl.ANY)
    near = pl.BlockSpec(memory_space=pltpu.VMEM)
    piece = jax.ShapeDtypeStruct((HALF, row_count, col_count), bf16)
    wide = col_count + row_count
    rims = [
        jax.ShapeDtypeStruct((slabs, count, 2 * REACH, wide), bf16)
        for count in (frame_count, HALF, HALF)
    ]
    return pl.pallas_call(
        cut_kernel,
        in_specs=[anywhere],
        out_specs=[near] * 3 + [anywhere] * 2,
        out_shape=rims + [piece, piece],
        scratch_shapes=[
            pltpu.VMEM((frame_count, row_count, col_count), bf16),
            pltpu.VMEM((frame_count, BLOCK, col_count), bf16),
            pltpu.VMEM((frame_count, BLOCK, col_count), bf16),
            pltpu.VMEM((frame_count, row_count, TILE), bf16),
            pltpu.VMEM((frame_count, row_count, TILE), bf16),
            pltpu.SemaphoreType.DMA((8,)),
        ],
        compiler_params=pltpu.CompilerParams(vmem_limit_bytes=60 * 1024 * 1024),
        name="cut",
    )(frames)


def late_cut(frames):
    _, frame_count, row_count, col_count = frames.shape
    anywhere = pl.BlockSpec(memory_space=pl.ANY)
    piece = jax.ShapeDtypeStruct((HALF, row_count, col_count), bf16)
    return pl.pallas_call(
        late_kernel,
        in_specs=[anywhere],
        out_specs=[anywhere] * 2,
        out_shape=[piece, piece],
        scratch_shapes=[
            pltpu.VMEM((frame_count, row_count, col_count), bf16),
            pltpu.SemaphoreType.DMA((4,)),
        ],
        compiler_params=pltpu.CompilerParams(vmem_limit_bytes=60 * 1024 * 1024),
        cost_estimate=pl.CostEstimate(flops=0, bytes_accessed=9_000_000, transcendentals=0),
        name="late_cut",
    )(frames)


def run_slab(slab, smoothed, spots, taps, w2, low, frames, high, edge, below, above):
    _, frame_count, row_count, col_count = frames.shape
    slot_count = spots.shape[1]
    row_step, frame_step = 32, 4
    steps_1 = row_count // row_step
    steps_2 = frame_count // frame_step
    wide = col_count + TILE
    near = frame_count + 2 * HALF

    def row_block(at):
        return jnp.minimum(at, steps_1 - 1)

    def whole(array):
        return pl.BlockSpec(array.shape, lambda at: (0,) * array.ndim)

    operands = [spots, taps, w2, low, frames, high, edge, below, above]
    in_specs = [
        pl.BlockSpec(memory_space=pltpu.SMEM),
        whole(taps),
        whole(w2),
        pl.BlockSpec((HALF, row_step, col_count), lambda at: (0, row_block(at), 0)),
        pl.BlockSpec((1, frame_count, row_step, col_count), lambda at: (slab, 0, row_block(at), 0)),
        pl.BlockSpec((HALF, row_step, col_count), lambda at: (0, row_block(at), 0)),
        pl.BlockSpec((1, near, row_step, TILE), lambda at: (slab, 0, row_block(at), 0)),
        pl.BlockSpec((1, near, REACH, wide), lambda at: (slab, 0, 0, 0)),
        pl.BlockSpec((1, near, REACH, wide), lambda at: (slab, 0, 0, 0)),
    ]
    aliases = {}
    if smoothed is not None:
        operands.append(smoothed)
        in_specs.append(pl.BlockSpec(memory_space=pl.ANY))
        aliases = {len(operands) - 1: 0}
    count = len(operands)

    def body(*refs):
        slab_kernel(row_step, frame_step, *refs[:9], *refs[count:])

    tall = row_count + 2 * EDGE
    return pl.pallas_call(
        body,
        grid=(steps_1 + steps_2 + 1,),
        in_specs=in_specs,
        out_specs=[
            pl.BlockSpec(
                (1, frame_step, row_count, col_count),
                lambda at: (slab, jnp.clip(at - steps_1, 0, steps_2 - 1), 0, 0),
            ),
            pl.BlockSpec((slot_count, PATCH * PATCH), lambda at: (0, 0)),
        ],
        out_shape=[
            jax.ShapeDtypeStruct(frames.shape, bf16),
            jax.ShapeDtypeStruct((slot_count, PATCH * PATCH), bf16),
        ],
        scratch_shapes=[
            pltpu.VMEM((16 * frame_count, 8 * near), bf16),
            pltpu.VMEM((frame_count, wide // TILE, tall, TILE), bf16),
            pltpu.VMEM((frame_count, wide // TILE, tall, TILE), bf16),
            pltpu.VMEM((frame_count, wide // TILE, tall, TILE), bf16),
            pltpu.VMEM((frame_count, wide // TILE, tall, TILE), bf16),
            pltpu.VMEM((frame_count, wide // TILE, EDGE, TILE), f32),
            pltpu.VMEM((frame_count, wide // TILE, EDGE, TILE), f32),
            pltpu.VMEM((frame_count, col_count // TILE, row_count, TILE), f32),
            pltpu.VMEM((slot_count * PATCH, TILE), bf16),
        ],
        input_output_aliases=aliases,
        compiler_params=pltpu.CompilerParams(vmem_limit_bytes=60 * 1024 * 1024),
        cost_estimate=pl.CostEstimate(
            flops=20_000_000_000, bytes_accessed=16_000_000, transcendentals=0
        ),
        name=f"slab_{slab}",
    )(*operands)


def shards(frames, omega_taps, smooth_kernel, spots, counts):
    _, frame_count, row_count, col_count = frames.shape
    first_frame = lax.axis_index("omega") * frame_count
    first_row = lax.axis_index("row") * row_count
    first_col = lax.axis_index("col") * col_count

    rim, rim_low, rim_high, send_low1, send_high1 = cut(frames)
    rim = jnp.concatenate(
        [shifted(rim_low, "omega", 1), rim, shifted(rim_high, "omega", -1)], axis=1
    )
    low1 = shifted(send_low1, "omega", 1)
    high1 = shifted(send_high1, "omega", -1)
    lane = jnp.arange(TILE, dtype=jnp.int32)[None, :]
    step = jnp.arange(REACH, dtype=jnp.int32)[:, None]
    after = (lane == step).astype(bf16)
    before = (lane == TILE - REACH + step).astype(bf16)
    if lax.axis_size("col") == 2:
        first = lax.axis_index("col") == 0
        sides = jnp.where(first, rim[:, :, REACH:, col_count:], rim[:, :, :REACH, col_count:])
        sides = lax.ppermute(sides, "col", [(0, 1), (1, 0)])
        place = jnp.where(first, after, before)
    else:
        left = shifted(rim[:, :, REACH:, col_count:], "col", 1)
        right = shifted(rim[:, :, :REACH, col_count:], "col", -1)
        sides = jnp.concatenate([right, left], axis=2)
        place = jnp.concatenate([after, before], axis=0)
    later, sides = lax.optimization_barrier((frames, sides))
    send_low0, send_high0 = late_cut(later)
    low0 = shifted(send_low0, "omega", 1)
    high0 = shifted(send_high0, "omega", -1)
    edge = jnp.einsum("sfkr,kc->sfrc", sides, place, preferred_element_type=bf16)
    ends = jnp.concatenate([edge[:, :, :REACH], edge[:, :, -REACH:]], axis=2)
    line = jnp.concatenate([rim[..., :col_count], ends], axis=3)
    above = shifted(line[:, :, REACH:], "row", 1)
    below = shifted(line[:, :, :REACH], "row", -1)

    taps = omega_matrix(
        omega_taps, first_frame, frame_count, frame_count * lax.axis_size("omega")
    )
    w2 = smooth_matrix(smooth_kernel)
    frame, row, col = spots[:, 0] - first_frame, spots[:, 1] - first_row, spots[:, 2] - first_col
    tile = col // TILE
    beside = jnp.minimum(tile + 1, col_count // TILE - 1)
    live = jnp.broadcast_to(counts, frame.shape)
    local = jnp.stack([frame, row, tile, beside, TILE - col % TILE, live], axis=1)

    smoothed, second = run_slab(1, None, local[1], taps, w2, low1, frames, high1, edge, below, above)
    count = lax.axis_size("row") * lax.axis_size("col")
    second = lax.ppermute(second, ("row", "col"), [(i, count - 1 - i) for i in range(count)])
    smoothed, first = run_slab(0, smoothed, local[0], taps, w2, low0, frames, high0, edge, below, above)
    scores = (
        lax.dot_general(first, second, (((1,), (1,)), ((), ())), preferred_element_type=f32)
        / float(PATCH * PATCH)
    )
    return (smoothed, scores)


def solution(mesh):
    return jax.shard_map(
        shards,
        mesh=mesh,
        in_specs=(
            P(None, "omega", "row", "col"),
            P(),
            P(),
            P(None, None, ("omega", "row", "col")),
            P(None, ("omega", "row", "col")),
        ),
        out_specs=(P(None, "omega", "row", "col"), P(("omega", "row", "col"), None)),
        check_vma=False,
    )
```

```python
import jax
import jax.numpy as jnp
from jax import lax
from jax.experimental import pallas as pl
from jax.experimental.pallas import tpu as pltpu
from jax.sharding import PartitionSpec as P

TAPS = 15
HALF = TAPS // 2
PATCH = 16
SIDE = 5
REACH = SIDE // 2
TILE = 128
BLOCK = 16
WINDOW = 32
EDGE = 8
GROUP = 4
bf16 = jnp.bfloat16
f32 = jnp.float32


def shifted(block, axis, step):
    count = lax.axis_size(axis)
    route = [(i, i + step) for i in range(count) if 0 <= i + step < count]
    return lax.ppermute(block, axis, route)


def split(values):
    high = lax.reduce_precision(values, 8, 7)
    return high.astype(bf16), (values - high).astype(bf16)


def omega_matrix(omega_taps, first_frame, frame_count, frame_total):
    out_ids = jnp.arange(frame_count, dtype=jnp.int32)[:, None]
    in_ids = jnp.arange(frame_count + 2 * HALF, dtype=jnp.int32)[None, :]
    source = first_frame + in_ids - HALF
    valid = (source >= 0) & (source < frame_total)
    tap = jnp.where(valid, in_ids - out_ids, -1)
    hit = tap[:, :, None] == jnp.arange(TAPS, dtype=jnp.int32)
    weights = jnp.sum(jnp.where(hit, omega_taps, 0.0), axis=2)
    norm = jnp.sum(weights, axis=1, keepdims=True)
    center = (in_ids - out_ids == HALF).astype(f32)
    matrix = center - weights / norm
    return jnp.stack(split(matrix), axis=1).reshape(2 * frame_count, matrix.shape[1])


def smooth_matrix(smooth_kernel):
    depth = WINDOW + 2 * EDGE
    out_ids = jnp.arange(WINDOW, dtype=jnp.int32)[:, None]
    in_ids = jnp.arange(depth, dtype=jnp.int32)[None, :]
    step = in_ids - out_ids - (EDGE - REACH)
    hit = step[None, :, :, None] == jnp.arange(SIDE, dtype=jnp.int32)
    table = jnp.sum(jnp.where(hit, smooth_kernel.T[:, None, None, :], 0.0), axis=3)
    table = jnp.swapaxes(table.reshape(SIDE, WINDOW // BLOCK, BLOCK, depth), 0, 1)
    high, low = split(table)
    return jnp.concatenate([high, high, low], axis=3).reshape(SIDE * WINDOW, 3 * depth)


def iota(shape, dim):
    return lax.broadcasted_iota(jnp.int32, shape, dim)


def slab_kernel(
    row_step, frame_step,
    spots_ref, taps_ref, w2_ref, low_ref, own_ref, high_ref, edge_ref, below_ref, above_ref,
    out_ref, last_ref, w1, chi, clo, carry, outer, kept, flat, offsets, placed,
):
    frame_count, tiles, row_count, _ = kept.shape
    near = taps_ref.shape[1]
    steps_1 = row_count // row_step
    steps_2 = frame_count // frame_step
    at = pl.program_id(0)

    def filtered(block):
        part = block.reshape(near * 8, block.shape[2])
        both = jnp.dot(w1[...], part, preferred_element_type=f32)
        both = both.reshape(frame_count, 2, 8, block.shape[2])
        return both[:, 0] + both[:, 1]

    def keep(above, below, tile, place):
        value = jnp.concatenate([above, below], axis=1)
        high = value.astype(bf16)
        chi[:, tile, place, :] = high
        clo[:, tile, place, :] = (value - high.astype(f32)).astype(bf16)

    @pl.when(at == 0)
    def _():
        count = 2 * frame_count
        tall = (iota((8 * count, count), 0) // 8 == iota((8 * count, count), 1)).astype(bf16)
        wide = (iota((near, 8 * near), 1) // 8 == iota((near, 8 * near), 0)).astype(bf16)
        full = jnp.dot(tall, taps_ref[...], preferred_element_type=f32).astype(bf16)
        full = jnp.dot(full, wide, preferred_element_type=f32)
        same = iota(full.shape, 0) % 8 == iota(full.shape, 1) % 8
        w1[...] = jnp.where(same, full, 0.0).astype(bf16)
        for tile in range(0, tiles + 1, GROUP):
            pair = range(tile, min(tile + GROUP, tiles + 1))
            cols = slice(tile * TILE, (tile + len(pair)) * TILE)
            below = below_ref[0, :, :, cols].astype(f32)
            above = above_ref[0, :, :, cols].astype(f32)
            gap = jnp.zeros((near, 8 - 2 * REACH, below.shape[2]), f32)
            both = filtered(jnp.concatenate([below, gap, above], axis=1).astype(bf16))
            for q, one in enumerate(pair):
                carry[:, one] = both[..., q * TILE : (q + 1) * TILE]
                outer[:, one] = both[..., q * TILE : (q + 1) * TILE]

    @pl.when(at < steps_1)
    def _():
        def keep_all(tile, parts):
            parts = [carry[:, tile]] + parts
            for q in range(0, len(parts) - 1, 2):
                place = pl.ds(pl.multiple_of(at * row_step + EDGE * q, BLOCK), BLOCK)
                keep(parts[q], parts[q + 1], tile, place)
            carry[:, tile] = parts[-1]

        for tile in range(0, tiles, 2):
            group = range(tile, min(tile + 2, tiles))
            cols = slice(tile * TILE, (tile + len(group)) * TILE)
            parts = []
            for h in range(0, row_step, EDGE):
                rows = slice(h, h + EDGE)
                block = jnp.concatenate(
                    [low_ref[:, rows, cols], own_ref[0, :, rows, cols], high_ref[:, rows, cols]],
                    axis=0,
                )
                parts.append(filtered(block))
            for q, one in enumerate(group):
                keep_all(one, [part[..., q * TILE : (q + 1) * TILE] for part in parts])
        both = filtered(
            jnp.concatenate(
                [edge_ref[0, :, h : h + EDGE] for h in range(0, row_step, EDGE)], axis=2
            )
        )
        parts = [both[..., h * TILE : (h + 1) * TILE] for h in range(row_step // EDGE)]
        keep_all(tiles, parts)

    @pl.when(at == steps_1 - 1)
    def _():
        for tile in range(tiles + 1):
            keep(carry[:, tile], outer[:, tile], tile, slice(row_count, row_count + BLOCK))

    @pl.when((at >= steps_1) & (at < steps_1 + steps_2))
    def _():
        lane = iota((BLOCK, TILE), 1)
        edge_of = [lane < 2, lane < 1, None, lane >= TILE - 1, lane >= TILE - 2]

        depth = WINDOW + 2 * EDGE
        parts_of = range(WINDOW // BLOCK)

        def two_frames(k2, unused):
            for row in range(0, row_count, WINDOW):
                turned = {}
                done = [0, 0]

                def finish(f, tile):
                    k = k2 * 2 + f
                    frame = (at - steps_1) * frame_step + k
                    for m in parts_of:
                        total = turned[f, m, REACH, tile]
                        for b in range(SIDE):
                            if b != REACH:
                                beside = (tile + (1 if b > REACH else -1)) % (tiles + 1)
                                total = total + jnp.where(
                                    edge_of[b], turned[f, m, b, beside], turned[f, m, b, tile]
                                )
                        value = total.astype(bf16)
                        rows = slice(row + m * BLOCK, row + (m + 1) * BLOCK)
                        out_ref[0, k, rows, tile * TILE : (tile + 1) * TILE] = value
                        kept[frame, tile, rows, :] = value.astype(f32)

                order = [(f, tile) for f in range(2) for tile in [tiles] + list(range(tiles))]
                for p in range(0, len(order), GROUP):
                    pair = order[p : p + GROUP]
                    stacks = []
                    for f, tile in pair:
                        frame = (at - steps_1) * frame_step + k2 * 2 + f
                        high = chi[frame, tile, row : row + depth, :]
                        low = clo[frame, tile, row : row + depth, :]
                        stacks.append(jnp.concatenate([high, low, high], axis=0))
                    both = jnp.dot(
                        w2_ref[...], jnp.concatenate(stacks, axis=1), preferred_element_type=f32
                    )
                    for q, (f, tile) in enumerate(pair):
                        for m in parts_of:
                            for b in range(SIDE):
                                at_row = (m * SIDE + b) * BLOCK
                                part = both[at_row : at_row + BLOCK, q * TILE : (q + 1) * TILE]
                                if b != REACH:
                                    part = pltpu.roll(part, (REACH - b) % TILE, 1)
                                turned[f, m, b, tile] = part
                    for f in range(2):
                        while done[f] < tiles and (f, 0, 0, done[f]) in turned:
                            after = min(done[f] + 1, tiles)
                            if (f, 0, 0, after) not in turned:
                                break
                            finish(f, done[f])
                            done[f] += 1
            return unused

        lax.fori_loop(0, frame_step // 2, two_frames, 0)

    @pl.when(at == steps_1 + steps_2)
    def _():
        slot_count = flat.shape[0] // PATCH
        lane = iota((PATCH, TILE), 1)

        def some(i16, unused):
            for j in range(16):
                i = i16 * 16 + j
                frame, row, tile = spots_ref[0, i], spots_ref[1, i], spots_ref[2, i]
                beside, offset = spots_ref[3, i], spots_ref[4, i]
                here = kept[frame, tile, pl.ds(row, PATCH), :]
                there = kept[frame, beside, pl.ds(row, PATCH), :]
                place = pl.ds(pl.multiple_of(i * PATCH, PATCH), PATCH)
                flat[place, :] = jnp.where(lane >= offset, here, there)
                offsets[place, :] = jnp.full((PATCH, TILE), offset, jnp.int32)
            return unused

        lax.fori_loop(0, slot_count // 16, some, 0)
        bits = PATCH.bit_length() - 1
        per = TILE // PATCH
        chunk = 16 * PATCH
        group = iota((chunk, TILE), 0) & (per - 1)
        mine = iota((chunk, TILE), 1) >> bits == group

        def place_rows(n, unused):
            place = pl.ds(pl.multiple_of(n * chunk, chunk), chunk)
            rows = flat[place, :]
            turn = ((group << bits) - offsets[place, :]) & (TILE - 1)
            for bit in range(TILE.bit_length() - 1):
                rows = jnp.where(
                    (turn & (1 << bit)) != 0, pltpu.roll(rows, 1 << bit, 1), rows
                )
            placed[place, :] = jnp.where(mine, rows, 0.0).astype(bf16)
            return unused

        lax.fori_loop(0, slot_count * PATCH // chunk, place_rows, 0)
        shape = (slot_count, slot_count * PATCH)
        source = iota(shape, 1) >> (per.bit_length() - 1)
        halves = []
        for half in range(PATCH // per):
            owner = (source == iota(shape, 0) * (PATCH // per) + half).astype(bf16)
            halves.append(jnp.dot(owner, placed[...], preferred_element_type=f32))
        values = jnp.concatenate(halves, axis=1)
        mean = jnp.sum(values, axis=1, keepdims=True) / (PATCH * PATCH)
        centered = values - mean
        spread = jnp.sum(centered * centered, axis=1, keepdims=True) / (PATCH * PATCH)
        normed = centered / jnp.sqrt(spread + 1e-05)
        live = iota((slot_count, 1), 0) < spots_ref[5, 0]
        last_ref[...] = jnp.where(live, normed, 0.0).astype(bf16)


def edges_of(top, bottom, left, right):
    rows = jnp.concatenate(
        [top[...].astype(f32)[:, :REACH], bottom[...].astype(f32)[:, BLOCK - REACH :]], axis=1
    )
    line = iota((8, TILE), 0)
    lane = iota((8, TILE), 1)
    first = ((line == lane) & (line < REACH)).astype(bf16)
    last = ((line + TILE - 2 * REACH == lane) & (line >= REACH)).astype(bf16)
    over_lanes = (((1,), (1,)), ((), ()))
    cols = []
    for f in range(rows.shape[0]):
        one = lax.dot_general(first, left[f], over_lanes, preferred_element_type=f32)
        one += lax.dot_general(last, right[f], over_lanes, preferred_element_type=f32)
        cols.append(one[: 2 * REACH].astype(bf16))
    return rows.astype(bf16), cols


def send_all(frames, slab, low, high, whole, sems):
    frame_count = whole.shape[0]
    middle = frame_count - HALF
    spans = [pl.ds(0, middle), pl.ds(middle, HALF)]
    fetches = [
        pltpu.make_async_copy(frames.at[slab, span], whole.at[span], sems.at[i])
        for i, span in enumerate(spans)
    ]
    writes = [
        pltpu.make_async_copy(whole.at[pl.ds(0, HALF)], high, sems.at[2]),
        pltpu.make_async_copy(whole.at[pl.ds(middle, HALF)], low, sems.at[3]),
    ]
    return fetches, writes


def cut_kernel(frames, rim, rim_low, rim_high, low, high, whole, top, bottom, left, right, sems):
    frame_count, row_count, col_count = whole.shape
    reads = [
        pltpu.make_async_copy(source, target, sems.at[4 + i])
        for i, (source, target) in enumerate(
            [
                (frames.at[0, :, pl.ds(0, BLOCK), :], top),
                (frames.at[0, :, pl.ds(row_count - BLOCK, BLOCK), :], bottom),
                (frames.at[0, :, :, pl.ds(0, TILE)], left),
                (frames.at[0, :, :, pl.ds(col_count - TILE, TILE)], right),
            ]
        )
    ]
    fetches, writes = send_all(frames, 1, low, high, whole, sems)
    for copy in reads + fetches:
        copy.start()

    def put(slab, rows, cols):
        middle = frame_count - HALF
        for target, start in [(rim, 0), (rim_low, middle), (rim_high, 0)]:
            count = target.shape[1]
            target[slab, :, :, :col_count] = rows[start : start + count]
            for f in range(count):
                target[slab, f, :, col_count:] = cols[start + f]

    for copy in reads:
        copy.wait()
    put(0, *edges_of(top, bottom, left, right))
    for fetch, write in zip(fetches, writes):
        fetch.wait()
        write.start()
    put(
        1,
        *edges_of(
            whole.at[:, pl.ds(0, BLOCK), :],
            whole.at[:, pl.ds(row_count - BLOCK, BLOCK), :],
            whole.at[:, :, pl.ds(0, TILE)],
            whole.at[:, :, pl.ds(col_count - TILE, TILE)],
        ),
    )
    for write in writes:
        write.wait()


def late_kernel(frames, low, high, whole, sems):
    fetches, writes = send_all(frames, 0, low, high, whole, sems)
    for fetch in fetches:
        fetch.start()
    for fetch, write in zip(fetches, writes):
        fetch.wait()
        write.start()
    for write in writes:
        write.wait()


def cut(frames):
    slabs, frame_count, row_count, col_count = frames.shape
    anywhere = pl.BlockSpec(memory_space=pl.ANY)
    near = pl.BlockSpec(memory_space=pltpu.VMEM)
    piece = jax.ShapeDtypeStruct((HALF, row_count, col_count), bf16)
    wide = col_count + row_count
    rims = [
        jax.ShapeDtypeStruct((slabs, count, 2 * REACH, wide), bf16)
        for count in (frame_count, HALF, HALF)
    ]
    return pl.pallas_call(
        cut_kernel,
        in_specs=[anywhere],
        out_specs=[near] * 3 + [anywhere] * 2,
        out_shape=rims + [piece, piece],
        scratch_shapes=[
            pltpu.VMEM((frame_count, row_count, col_count), bf16),
            pltpu.VMEM((frame_count, BLOCK, col_count), bf16),
            pltpu.VMEM((frame_count, BLOCK, col_count), bf16),
            pltpu.VMEM((frame_count, row_count, TILE), bf16),
            pltpu.VMEM((frame_count, row_count, TILE), bf16),
            pltpu.SemaphoreType.DMA((8,)),
        ],
        compiler_params=pltpu.CompilerParams(vmem_limit_bytes=60 * 1024 * 1024),
        name="cut",
    )(frames)


def late_cut(frames):
    _, frame_count, row_count, col_count = frames.shape
    anywhere = pl.BlockSpec(memory_space=pl.ANY)
    piece = jax.ShapeDtypeStruct((HALF, row_count, col_count), bf16)
    return pl.pallas_call(
        late_kernel,
        in_specs=[anywhere],
        out_specs=[anywhere] * 2,
        out_shape=[piece, piece],
        scratch_shapes=[
            pltpu.VMEM((frame_count, row_count, col_count), bf16),
            pltpu.SemaphoreType.DMA((4,)),
        ],
        compiler_params=pltpu.CompilerParams(vmem_limit_bytes=60 * 1024 * 1024),
        cost_estimate=pl.CostEstimate(flops=0, bytes_accessed=9_000_000, transcendentals=0),
        name="late_cut",
    )(frames)


def run_slab(slab, smoothed, spots, taps, w2, low, frames, high, edge, below, above):
    _, frame_count, row_count, col_count = frames.shape
    slot_count = spots.shape[1]
    row_step, frame_step = 32, 4
    steps_1 = row_count // row_step
    steps_2 = frame_count // frame_step
    wide = col_count + TILE
    near = frame_count + 2 * HALF

    def row_block(at):
        return jnp.minimum(at, steps_1 - 1)

    def whole(array):
        return pl.BlockSpec(array.shape, lambda at: (0,) * array.ndim)

    operands = [spots, taps, w2, low, frames, high, edge, below, above]
    in_specs = [
        pl.BlockSpec(memory_space=pltpu.SMEM),
        whole(taps),
        whole(w2),
        pl.BlockSpec((HALF, row_step, col_count), lambda at: (0, row_block(at), 0)),
        pl.BlockSpec((1, frame_count, row_step, col_count), lambda at: (slab, 0, row_block(at), 0)),
        pl.BlockSpec((HALF, row_step, col_count), lambda at: (0, row_block(at), 0)),
        pl.BlockSpec((1, near, row_step, TILE), lambda at: (slab, 0, row_block(at), 0)),
        pl.BlockSpec((1, near, REACH, wide), lambda at: (slab, 0, 0, 0)),
        pl.BlockSpec((1, near, REACH, wide), lambda at: (slab, 0, 0, 0)),
    ]
    aliases = {}
    if smoothed is not None:
        operands.append(smoothed)
        in_specs.append(pl.BlockSpec(memory_space=pl.ANY))
        aliases = {len(operands) - 1: 0}
    count = len(operands)

    def body(*refs):
        slab_kernel(row_step, frame_step, *refs[:9], *refs[count:])

    tall = row_count + 2 * EDGE
    return pl.pallas_call(
        body,
        grid=(steps_1 + steps_2 + 1,),
        in_specs=in_specs,
        out_specs=[
            pl.BlockSpec(
                (1, frame_step, row_count, col_count),
                lambda at: (slab, jnp.clip(at - steps_1, 0, steps_2 - 1), 0, 0),
            ),
            pl.BlockSpec((slot_count, PATCH * PATCH), lambda at: (0, 0)),
        ],
        out_shape=[
            jax.ShapeDtypeStruct(frames.shape, bf16),
            jax.ShapeDtypeStruct((slot_count, PATCH * PATCH), bf16),
        ],
        scratch_shapes=[
            pltpu.VMEM((16 * frame_count, 8 * near), bf16),
            pltpu.VMEM((frame_count, wide // TILE, tall, TILE), bf16),
            pltpu.VMEM((frame_count, wide // TILE, tall, TILE), bf16),
            pltpu.VMEM((frame_count, wide // TILE, EDGE, TILE), f32),
            pltpu.VMEM((frame_count, wide // TILE, EDGE, TILE), f32),
            pltpu.VMEM((frame_count, col_count // TILE, row_count, TILE), f32),
            pltpu.VMEM((slot_count * PATCH, TILE), f32),
            pltpu.VMEM((slot_count * PATCH, TILE), jnp.int32),
            pltpu.VMEM((slot_count * PATCH, TILE), bf16),
        ],
        input_output_aliases=aliases,
        compiler_params=pltpu.CompilerParams(vmem_limit_bytes=60 * 1024 * 1024),
        cost_estimate=pl.CostEstimate(
            flops=20_000_000_000, bytes_accessed=16_000_000, transcendentals=0
        ),
        name=f"slab_{slab}",
    )(*operands)


def shards(frames, omega_taps, smooth_kernel, spots, counts):
    _, frame_count, row_count, col_count = frames.shape
    first_frame = lax.axis_index("omega") * frame_count
    first_row = lax.axis_index("row") * row_count
    first_col = lax.axis_index("col") * col_count

    rim, rim_low, rim_high, send_low1, send_high1 = cut(frames)
    rim = jnp.concatenate(
        [shifted(rim_low, "omega", 1), rim, shifted(rim_high, "omega", -1)], axis=1
    )
    low1 = shifted(send_low1, "omega", 1)
    high1 = shifted(send_high1, "omega", -1)
    lane = jnp.arange(TILE, dtype=jnp.int32)[None, :]
    step = jnp.arange(REACH, dtype=jnp.int32)[:, None]
    after = (lane == step).astype(bf16)
    before = (lane == TILE - REACH + step).astype(bf16)
    if lax.axis_size("col") == 2:
        first = lax.axis_index("col") == 0
        sides = jnp.where(first, rim[:, :, REACH:, col_count:], rim[:, :, :REACH, col_count:])
        sides = lax.ppermute(sides, "col", [(0, 1), (1, 0)])
        place = jnp.where(first, after, before)
    else:
        left = shifted(rim[:, :, REACH:, col_count:], "col", 1)
        right = shifted(rim[:, :, :REACH, col_count:], "col", -1)
        sides = jnp.concatenate([right, left], axis=2)
        place = jnp.concatenate([after, before], axis=0)
    later, sides = lax.optimization_barrier((frames, sides))
    send_low0, send_high0 = late_cut(later)
    low0 = shifted(send_low0, "omega", 1)
    high0 = shifted(send_high0, "omega", -1)
    edge = jnp.einsum("sfkr,kc->sfrc", sides, place, preferred_element_type=bf16)
    ends = jnp.concatenate([edge[:, :, :REACH], edge[:, :, -REACH:]], axis=2)
    line = jnp.concatenate([rim[..., :col_count], ends], axis=3)
    above = shifted(line[:, :, REACH:], "row", 1)
    below = shifted(line[:, :, :REACH], "row", -1)

    taps = omega_matrix(
        omega_taps, first_frame, frame_count, frame_count * lax.axis_size("omega")
    )
    w2 = smooth_matrix(smooth_kernel)
    frame, row, col = spots[:, 0] - first_frame, spots[:, 1] - first_row, spots[:, 2] - first_col
    tile = col // TILE
    beside = jnp.minimum(tile + 1, col_count // TILE - 1)
    live = jnp.broadcast_to(counts, frame.shape)
    local = jnp.stack([frame, row, tile, beside, col % TILE, live], axis=1)

    smoothed, second = run_slab(1, None, local[1], taps, w2, low1, frames, high1, edge, below, above)
    count = lax.axis_size("row") * lax.axis_size("col")
    second = lax.ppermute(second, ("row", "col"), [(i, count - 1 - i) for i in range(count)])
    smoothed, first = run_slab(0, smoothed, local[0], taps, w2, low0, frames, high0, edge, below, above)
    scores = (
        lax.dot_general(first, second, (((1,), (1,)), ((), ())), preferred_element_type=f32)
        / float(PATCH * PATCH)
    )
    return (smoothed, scores)


def solution(mesh):
    return jax.shard_map(
        shards,
        mesh=mesh,
        in_specs=(
            P(None, "omega", "row", "col"),
            P(),
            P(),
            P(None, None, ("omega", "row", "col")),
            P(None, ("omega", "row", "col")),
        ),
        out_specs=(P(None, "omega", "row", "col"), P(("omega", "row", "col"), None)),
        check_vma=False,
    )
```

```python
import jax
import jax.numpy as jnp
from jax import lax
from jax.experimental import pallas as pl
from jax.experimental.pallas import tpu as pltpu
from jax.sharding import PartitionSpec as P

TAPS = 15
HALF = TAPS // 2
PATCH = 16
SIDE = 5
REACH = SIDE // 2
TILE = 128
BLOCK = 16
WINDOW = 32
EDGE = 8
GROUP = 4
BY_MATRIX = (0, 1, 3, 4)
bf16 = jnp.bfloat16
f32 = jnp.float32


def shifted(block, axis, step):
    count = lax.axis_size(axis)
    route = [(i, i + step) for i in range(count) if 0 <= i + step < count]
    return lax.ppermute(block, axis, route)


def omega_matrix(omega_taps, first_frame, frame_count, frame_total):
    row = jnp.arange(2 * frame_count, dtype=jnp.int32)[:, None]
    out_ids = row // 2
    in_ids = jnp.arange(frame_count + 2 * HALF, dtype=jnp.int32)[None, :]
    source = first_frame + in_ids - HALF
    valid = (source >= 0) & (source < frame_total)
    tap = jnp.where(valid, in_ids - out_ids, -1)
    hit = tap[:, :, None] == jnp.arange(TAPS, dtype=jnp.int32)
    weights = jnp.sum(jnp.where(hit, omega_taps, 0.0), axis=2)
    norm = jnp.sum(weights, axis=1, keepdims=True)
    center = (in_ids - out_ids == HALF).astype(f32)
    matrix = center - weights / norm
    high = lax.reduce_precision(matrix, 8, 7)
    return jnp.where(row % 2 == 0, high, matrix - high).astype(bf16)


def smooth_matrix(smooth_kernel):
    depth = WINDOW + 2 * EDGE
    count = len(BY_MATRIX)
    row = jnp.arange(count * WINDOW, dtype=jnp.int32)[:, None]
    out_ids = row // (count * BLOCK) * BLOCK + row % BLOCK
    step_id = row // BLOCK % count
    col = jnp.arange(3 * depth, dtype=jnp.int32)[None, :]
    step = col % depth - out_ids - (EDGE - REACH)
    table = jnp.zeros((count * WINDOW, 3 * depth), f32)
    for i, b in enumerate(BY_MATRIX):
        for a in range(SIDE):
            table = jnp.where((step_id == i) & (step == a), smooth_kernel[a, b], table)
    high = lax.reduce_precision(table, 8, 7)
    return jnp.where(col < 2 * depth, high, table - high).astype(bf16)


def iota(shape, dim):
    return lax.broadcasted_iota(jnp.int32, shape, dim)


def slab_kernel(
    slab, row_step, frame_step,
    spots_ref, kernel_ref, taps_ref, w2_ref, low_ref, own_ref, high_ref, edge_ref, below_ref, above_ref,
    out_ref, last_ref, w1, chi, clo, full, carry, outer, kept, flat,
):
    frame_count, tiles, row_count, _ = kept.shape
    near = taps_ref.shape[1]
    steps_1 = row_count // row_step
    steps_2 = frame_count // frame_step
    at = pl.program_id(0)

    def filtered(block):
        part = block.reshape(near * 8, block.shape[2])
        both = jnp.dot(w1[...], part, preferred_element_type=f32)
        both = both.reshape(frame_count, 2, 8, block.shape[2])
        return both[:, 0] + both[:, 1]

    def keep(above, below, tile, place):
        value = jnp.concatenate([above, below], axis=1)
        high = value.astype(bf16)
        full[:, tile, place, :] = value
        chi[:, tile, place, :] = high
        clo[:, tile, place, :] = (value - high.astype(f32)).astype(bf16)

    @pl.when(at == 0)
    def _():
        count = 2 * frame_count
        tall = (iota((8 * count, count), 0) // 8 == iota((8 * count, count), 1)).astype(bf16)
        wide = (iota((near, 8 * near), 1) // 8 == iota((near, 8 * near), 0)).astype(bf16)
        matrix = jnp.dot(tall, taps_ref[...], preferred_element_type=f32).astype(bf16)
        matrix = jnp.dot(matrix, wide, preferred_element_type=f32)
        same = iota(matrix.shape, 0) & 7 == iota(matrix.shape, 1) & 7
        w1[...] = jnp.where(same, matrix, 0.0).astype(bf16)
        for tile in range(0, tiles + 1, GROUP):
            pair = range(tile, min(tile + GROUP, tiles + 1))
            cols = slice(tile * TILE, (tile + len(pair)) * TILE)
            below = below_ref[0, :, :, cols].astype(f32)
            above = above_ref[0, :, :, cols].astype(f32)
            gap = jnp.zeros((near, 8 - 2 * REACH, below.shape[2]), f32)
            both = filtered(jnp.concatenate([below, gap, above], axis=1).astype(bf16))
            for q, one in enumerate(pair):
                carry[:, one] = both[..., q * TILE : (q + 1) * TILE]
                outer[:, one] = both[..., q * TILE : (q + 1) * TILE]

    @pl.when(at < steps_1)
    def _():
        def keep_all(tile, parts):
            parts = [carry[:, tile]] + parts
            for q in range(0, len(parts) - 1, 2):
                place = pl.ds(pl.multiple_of(at * row_step + EDGE * q, BLOCK), BLOCK)
                keep(parts[q], parts[q + 1], tile, place)
            carry[:, tile] = parts[-1]

        for tile in range(0, tiles, 2):
            group = range(tile, min(tile + 2, tiles))
            cols = slice(tile * TILE, (tile + len(group)) * TILE)
            parts = []
            for h in range(0, row_step, EDGE):
                rows = slice(h, h + EDGE)
                block = jnp.concatenate(
                    [low_ref[:, rows, cols], own_ref[0, :, rows, cols], high_ref[:, rows, cols]],
                    axis=0,
                )
                parts.append(filtered(block))
            for q, one in enumerate(group):
                keep_all(one, [part[..., q * TILE : (q + 1) * TILE] for part in parts])
        both = filtered(
            jnp.concatenate(
                [edge_ref[0, :, h : h + EDGE] for h in range(0, row_step, EDGE)], axis=2
            )
        )
        parts = [both[..., h * TILE : (h + 1) * TILE] for h in range(row_step // EDGE)]
        keep_all(tiles, parts)

    @pl.when(at == steps_1 - 1)
    def _():
        for tile in range(tiles + 1):
            keep(carry[:, tile], outer[:, tile], tile, slice(row_count, row_count + BLOCK))

    @pl.when((at >= steps_1) & (at < steps_1 + steps_2))
    def _():
        lane = iota((BLOCK, TILE), 1)
        edge_of = [lane < 2, lane < 1, None, lane >= TILE - 1, lane >= TILE - 2]

        depth = WINDOW + 2 * EDGE
        parts_of = range(WINDOW // BLOCK)

        def two_frames(k2, unused):
            for row in range(0, row_count, WINDOW):
                turned = {}
                done = [0, 0]

                def finish(f, tile):
                    k = k2 * 2 + f
                    frame = (at - steps_1) * frame_step + k
                    for m in parts_of:
                        start = row + m * BLOCK + EDGE - REACH
                        total = kernel_ref[0, REACH] * full[frame, tile, start : start + BLOCK, :]
                        for a in range(1, SIDE):
                            rows = slice(start + a, start + a + BLOCK)
                            total = total + kernel_ref[a, REACH] * full[frame, tile, rows, :]
                        for b in BY_MATRIX:
                            beside = (tile + (1 if b > REACH else -1)) % (tiles + 1)
                            total = total + jnp.where(
                                edge_of[b], turned[f, m, b, beside], turned[f, m, b, tile]
                            )
                        value = total.astype(bf16)
                        rows = slice(row + m * BLOCK, row + (m + 1) * BLOCK)
                        out_ref[0, k, rows, tile * TILE : (tile + 1) * TILE] = value
                        kept[frame, tile, rows, :] = value.astype(f32)

                order = [(f, tile) for f in range(2) for tile in [tiles] + list(range(tiles))]
                for p in range(0, len(order), GROUP):
                    pair = order[p : p + GROUP]
                    stacks = []
                    for f, tile in pair:
                        frame = (at - steps_1) * frame_step + k2 * 2 + f
                        high = chi[frame, tile, row : row + depth, :]
                        low = clo[frame, tile, row : row + depth, :]
                        stacks.append(jnp.concatenate([high, low, high], axis=0))
                    both = jnp.dot(
                        w2_ref[...], jnp.concatenate(stacks, axis=1), preferred_element_type=f32
                    )
                    for q, (f, tile) in enumerate(pair):
                        for m in parts_of:
                            for i, b in enumerate(BY_MATRIX):
                                at_row = (m * len(BY_MATRIX) + i) * BLOCK
                                part = both[at_row : at_row + BLOCK, q * TILE : (q + 1) * TILE]
                                turned[f, m, b, tile] = pltpu.roll(part, (REACH - b) % TILE, 1)
                    for f in range(2):
                        while done[f] < tiles and (f, 0, 0, done[f]) in turned:
                            after = min(done[f] + 1, tiles)
                            if (f, 0, 0, after) not in turned:
                                break
                            finish(f, done[f])
                            done[f] += 1
            return unused

        lax.fori_loop(0, frame_step // 2, two_frames, 0)

    @pl.when(at == steps_1 + steps_2)
    def _():
        slot_count = flat.shape[0] // PATCH

        lane = iota((PATCH, TILE), 1)

        def some(i8, unused):
            for j in range(16):
                i = i8 * 16 + j
                frame, row, tile = spots_ref[slab, 0, i], spots_ref[slab, 1, i], spots_ref[slab, 2, i]
                beside, turn = spots_ref[slab, 3, i], spots_ref[slab, 4, i]
                here = kept[frame, tile, pl.ds(row, PATCH), :]
                there = kept[frame, beside, pl.ds(row, PATCH), :]
                shift = turn & (TILE - 1)
                here, there = pltpu.roll(here, shift, 1), pltpu.roll(there, shift, 1)
                part = jnp.where(lane < turn, here, there)
                flat[pl.ds(pl.multiple_of(i * PATCH, PATCH), PATCH), :] = part.astype(bf16)
            return unused

        lax.fori_loop(0, slot_count // 16, some, 0)
        low_bits = PATCH - 1
        bits = low_bits.bit_length()
        shape = (TILE, PATCH * PATCH)
        repeat = (iota(shape, 1) & low_bits == iota(shape, 0)).astype(bf16)
        rows = jnp.dot(flat[...], repeat, preferred_element_type=f32)
        mine = iota(rows.shape, 1) >> bits == iota(rows.shape, 0) & low_bits
        rows = jnp.where(mine, rows, 0.0).astype(bf16)
        shape = (slot_count, rows.shape[0])
        owner = (iota(shape, 1) >> bits == iota(shape, 0)).astype(bf16)
        values = jnp.dot(owner, rows, preferred_element_type=f32)
        mean = jnp.sum(values, axis=1, keepdims=True) / (PATCH * PATCH)
        centered = values - mean
        spread = jnp.sum(centered * centered, axis=1, keepdims=True) / (PATCH * PATCH)
        normed = centered / jnp.sqrt(spread + 1e-05)
        live = iota((slot_count, 1), 0) < spots_ref[slab, 5, 0]
        last_ref[...] = jnp.where(live, normed, 0.0).astype(bf16)


def edges_of(top, bottom, left, right):
    rows = jnp.concatenate(
        [top[...].astype(f32)[:, :REACH], bottom[...].astype(f32)[:, BLOCK - REACH :]], axis=1
    )
    line = iota((8, TILE), 0)
    lane = iota((8, TILE), 1)
    first = ((line == lane) & (line < REACH)).astype(bf16)
    last = ((line + TILE - 2 * REACH == lane) & (line >= REACH)).astype(bf16)
    over_lanes = (((1,), (1,)), ((), ()))
    cols = []
    for f in range(rows.shape[0]):
        one = lax.dot_general(first, left[f], over_lanes, preferred_element_type=f32)
        one += lax.dot_general(last, right[f], over_lanes, preferred_element_type=f32)
        cols.append(one[: 2 * REACH].astype(bf16))
    return rows.astype(bf16), cols


def send_all(frames, slab, low, high, whole, sems):
    frame_count = whole.shape[0]
    middle = frame_count - HALF
    spans = [pl.ds(0, middle), pl.ds(middle, HALF)]
    fetches = [
        pltpu.make_async_copy(frames.at[slab, span], whole.at[span], sems.at[i])
        for i, span in enumerate(spans)
    ]
    writes = [
        pltpu.make_async_copy(whole.at[pl.ds(0, HALF)], high, sems.at[2]),
        pltpu.make_async_copy(whole.at[pl.ds(middle, HALF)], low, sems.at[3]),
    ]
    return fetches, writes


def cut_kernel(frames, rim, rim_low, rim_high, low, high, whole, top, bottom, left, right, sems):
    frame_count, row_count, col_count = whole.shape
    reads = [
        pltpu.make_async_copy(source, target, sems.at[4 + i])
        for i, (source, target) in enumerate(
            [
                (frames.at[0, :, pl.ds(0, BLOCK), :], top),
                (frames.at[0, :, pl.ds(row_count - BLOCK, BLOCK), :], bottom),
                (frames.at[0, :, :, pl.ds(0, TILE)], left),
                (frames.at[0, :, :, pl.ds(col_count - TILE, TILE)], right),
            ]
        )
    ]
    fetches, writes = send_all(frames, 1, low, high, whole, sems)
    for copy in reads + fetches:
        copy.start()

    def put(slab, rows, cols):
        middle = frame_count - HALF
        for target, start in [(rim, 0), (rim_low, middle), (rim_high, 0)]:
            count = target.shape[1]
            target[slab, :, :, :col_count] = rows[start : start + count]
            for f in range(count):
                target[slab, f, :, col_count:] = cols[start + f]

    for copy in reads:
        copy.wait()
    put(0, *edges_of(top, bottom, left, right))
    for fetch, write in zip(fetches, writes):
        fetch.wait()
        write.start()
    put(
        1,
        *edges_of(
            whole.at[:, pl.ds(0, BLOCK), :],
            whole.at[:, pl.ds(row_count - BLOCK, BLOCK), :],
            whole.at[:, :, pl.ds(0, TILE)],
            whole.at[:, :, pl.ds(col_count - TILE, TILE)],
        ),
    )
    for write in writes:
        write.wait()


def late_kernel(frames, low, high, whole, sems):
    fetches, writes = send_all(frames, 0, low, high, whole, sems)
    for fetch in fetches:
        fetch.start()
    for fetch, write in zip(fetches, writes):
        fetch.wait()
        write.start()
    for write in writes:
        write.wait()


def cut(frames):
    slabs, frame_count, row_count, col_count = frames.shape
    anywhere = pl.BlockSpec(memory_space=pl.ANY)
    near = pl.BlockSpec(memory_space=pltpu.VMEM)
    piece = jax.ShapeDtypeStruct((HALF, row_count, col_count), bf16)
    wide = col_count + row_count
    rims = [
        jax.ShapeDtypeStruct((slabs, count, 2 * REACH, wide), bf16)
        for count in (frame_count, HALF, HALF)
    ]
    return pl.pallas_call(
        cut_kernel,
        in_specs=[anywhere],
        out_specs=[near] * 3 + [anywhere] * 2,
        out_shape=rims + [piece, piece],
        scratch_shapes=[
            pltpu.VMEM((frame_count, row_count, col_count), bf16),
            pltpu.VMEM((frame_count, BLOCK, col_count), bf16),
            pltpu.VMEM((frame_count, BLOCK, col_count), bf16),
            pltpu.VMEM((frame_count, row_count, TILE), bf16),
            pltpu.VMEM((frame_count, row_count, TILE), bf16),
            pltpu.SemaphoreType.DMA((8,)),
        ],
        compiler_params=pltpu.CompilerParams(vmem_limit_bytes=60 * 1024 * 1024),
        name="cut",
    )(frames)


def late_cut(frames):
    _, frame_count, row_count, col_count = frames.shape
    anywhere = pl.BlockSpec(memory_space=pl.ANY)
    piece = jax.ShapeDtypeStruct((HALF, row_count, col_count), bf16)
    return pl.pallas_call(
        late_kernel,
        in_specs=[anywhere],
        out_specs=[anywhere] * 2,
        out_shape=[piece, piece],
        scratch_shapes=[
            pltpu.VMEM((frame_count, row_count, col_count), bf16),
            pltpu.SemaphoreType.DMA((4,)),
        ],
        compiler_params=pltpu.CompilerParams(vmem_limit_bytes=60 * 1024 * 1024),
        cost_estimate=pl.CostEstimate(flops=0, bytes_accessed=9_000_000, transcendentals=0),
        name="late_cut",
    )(frames)


def run_slab(slab, smoothed, spots, kernel, taps, w2, low, frames, high, edge, below, above):
    _, frame_count, row_count, col_count = frames.shape
    slot_count = spots.shape[2]
    row_step, frame_step = 32, 4
    steps_1 = row_count // row_step
    steps_2 = frame_count // frame_step
    wide = col_count + TILE
    near = frame_count + 2 * HALF

    def row_block(at):
        return jnp.minimum(at, steps_1 - 1)

    def whole(array):
        return pl.BlockSpec(array.shape, lambda at: (0,) * array.ndim)

    operands = [spots, kernel, taps, w2, low, frames, high, edge, below, above]
    in_specs = [
        pl.BlockSpec(memory_space=pltpu.SMEM),
        pl.BlockSpec(memory_space=pltpu.SMEM),
        whole(taps),
        whole(w2),
        pl.BlockSpec((HALF, row_step, col_count), lambda at: (0, row_block(at), 0)),
        pl.BlockSpec((1, frame_count, row_step, col_count), lambda at: (slab, 0, row_block(at), 0)),
        pl.BlockSpec((HALF, row_step, col_count), lambda at: (0, row_block(at), 0)),
        pl.BlockSpec((1, near, row_step, TILE), lambda at: (slab, 0, row_block(at), 0)),
        pl.BlockSpec((1, near, REACH, wide), lambda at: (slab, 0, 0, 0)),
        pl.BlockSpec((1, near, REACH, wide), lambda at: (slab, 0, 0, 0)),
    ]
    aliases = {}
    if smoothed is not None:
        operands.append(smoothed)
        in_specs.append(pl.BlockSpec(memory_space=pl.ANY))
        aliases = {len(operands) - 1: 0}
    count = len(operands)

    def body(*refs):
        slab_kernel(slab, row_step, frame_step, *refs[:10], *refs[count:])

    tall = row_count + 2 * EDGE
    return pl.pallas_call(
        body,
        grid=(steps_1 + steps_2 + 1,),
        in_specs=in_specs,
        out_specs=[
            pl.BlockSpec(
                (1, frame_step, row_count, col_count),
                lambda at: (slab, jnp.clip(at - steps_1, 0, steps_2 - 1), 0, 0),
            ),
            pl.BlockSpec((slot_count, PATCH * PATCH), lambda at: (0, 0)),
        ],
        out_shape=[
            jax.ShapeDtypeStruct(frames.shape, bf16),
            jax.ShapeDtypeStruct((slot_count, PATCH * PATCH), bf16),
        ],
        scratch_shapes=[
            pltpu.VMEM((16 * frame_count, 8 * near), bf16),
            pltpu.VMEM((frame_count, wide // TILE, tall, TILE), bf16),
            pltpu.VMEM((frame_count, wide // TILE, tall, TILE), bf16),
            pltpu.VMEM((frame_count, wide // TILE, tall, TILE), f32),
            pltpu.VMEM((frame_count, wide // TILE, EDGE, TILE), f32),
            pltpu.VMEM((frame_count, wide // TILE, EDGE, TILE), f32),
            pltpu.VMEM((frame_count, col_count // TILE, row_count, TILE), f32),
            pltpu.VMEM((slot_count * PATCH, TILE), bf16),
        ],
        input_output_aliases=aliases,
        compiler_params=pltpu.CompilerParams(vmem_limit_bytes=60 * 1024 * 1024),
        cost_estimate=pl.CostEstimate(
            flops=20_000_000_000, bytes_accessed=16_000_000, transcendentals=0
        ),
        name=f"slab_{slab}",
    )(*operands)


def shards(frames, omega_taps, smooth_kernel, spots, counts):
    _, frame_count, row_count, col_count = frames.shape
    first_frame = lax.axis_index("omega") * frame_count
    first_row = lax.axis_index("row") * row_count
    first_col = lax.axis_index("col") * col_count

    rim, rim_low, rim_high, send_low1, send_high1 = cut(frames)
    rims = [shifted(rim_low, "omega", 1), rim, shifted(rim_high, "omega", -1)]
    rim_cols = jnp.concatenate([part[..., col_count:] for part in rims], axis=1)
    low1 = shifted(send_low1, "omega", 1)
    high1 = shifted(send_high1, "omega", -1)
    lane = jnp.arange(TILE, dtype=jnp.int32)[None, :]
    step = jnp.arange(REACH, dtype=jnp.int32)[:, None]
    after = (lane == step).astype(bf16)
    before = (lane == TILE - REACH + step).astype(bf16)
    if lax.axis_size("col") == 2:
        first = lax.axis_index("col") == 0
        sides = jnp.where(first, rim_cols[:, :, REACH:], rim_cols[:, :, :REACH])
        sides = lax.ppermute(sides, "col", [(0, 1), (1, 0)])
        place = jnp.where(first, after, before)
    else:
        left = shifted(rim_cols[:, :, REACH:], "col", 1)
        right = shifted(rim_cols[:, :, :REACH], "col", -1)
        sides = jnp.concatenate([right, left], axis=2)
        place = jnp.concatenate([after, before], axis=0)
    later, sides = lax.optimization_barrier((frames, sides))
    send_low0, send_high0 = late_cut(later)
    low0 = shifted(send_low0, "omega", 1)
    high0 = shifted(send_high0, "omega", -1)
    edge = jnp.einsum("sfkr,kc->sfrc", sides, place, preferred_element_type=bf16)
    ends = jnp.concatenate([edge[:, :, :REACH], edge[:, :, -REACH:]], axis=2)
    rim_rows = jnp.concatenate([part[..., :col_count] for part in rims], axis=1)
    line = jnp.concatenate([rim_rows, ends], axis=3)
    above = shifted(line[:, :, REACH:], "row", 1)
    below = shifted(line[:, :, :REACH], "row", -1)

    taps = omega_matrix(
        omega_taps, first_frame, frame_count, frame_count * lax.axis_size("omega")
    )
    w2 = smooth_matrix(smooth_kernel)
    frame, row, col = spots[:, 0] - first_frame, spots[:, 1] - first_row, spots[:, 2] - first_col
    tile = col // TILE
    beside = jnp.minimum(tile + 1, col_count // TILE - 1)
    live = jnp.broadcast_to(counts, frame.shape)
    local = jnp.stack([frame, row, tile, beside, TILE - col % TILE, live], axis=1)

    smoothed, second = run_slab(1, None, local, smooth_kernel, taps, w2, low1, frames, high1, edge, below, above)
    count = lax.axis_size("row") * lax.axis_size("col")
    second = lax.ppermute(second, ("row", "col"), [(i, count - 1 - i) for i in range(count)])
    smoothed, first = run_slab(0, smoothed, local, smooth_kernel, taps, w2, low0, frames, high0, edge, below, above)
    scores = (
        lax.dot_general(first, second, (((1,), (1,)), ((), ())), preferred_element_type=f32)
        / float(PATCH * PATCH)
    )
    return (smoothed, scores)


def solution(mesh):
    return jax.shard_map(
        shards,
        mesh=mesh,
        in_specs=(
            P(None, "omega", "row", "col"),
            P(),
            P(),
            P(None, None, ("omega", "row", "col")),
            P(None, ("omega", "row", "col")),
        ),
        out_specs=(P(None, "omega", "row", "col"), P(("omega", "row", "col"), None)),
        check_vma=False,
    )
```

```python
import jax
import jax.numpy as jnp
from jax import lax
from jax.experimental import pallas as pl
from jax.experimental.pallas import tpu as pltpu
from jax.sharding import PartitionSpec as P

TAPS = 15
HALF = TAPS // 2
PATCH = 16
SIDE = 5
REACH = SIDE // 2
TILE = 128
BLOCK = 16
WINDOW = 32
EDGE = 8
GROUP = 4
bf16 = jnp.bfloat16
f32 = jnp.float32


def shifted(block, axis, step):
    count = lax.axis_size(axis)
    route = [(i, i + step) for i in range(count) if 0 <= i + step < count]
    return lax.ppermute(block, axis, route)


def split(values):
    high = lax.reduce_precision(values, 8, 7)
    return high.astype(bf16), (values - high).astype(bf16)


def omega_matrix(omega_taps, first_frame, frame_count, frame_total):
    out_ids = jnp.arange(frame_count, dtype=jnp.int32)[:, None]
    in_ids = jnp.arange(frame_count + 2 * HALF, dtype=jnp.int32)[None, :]
    source = first_frame + in_ids - HALF
    valid = (source >= 0) & (source < frame_total)
    tap = jnp.where(valid, in_ids - out_ids, -1)
    hit = tap[:, :, None] == jnp.arange(TAPS, dtype=jnp.int32)
    weights = jnp.sum(jnp.where(hit, omega_taps, 0.0), axis=2)
    norm = jnp.sum(weights, axis=1, keepdims=True)
    center = (in_ids - out_ids == HALF).astype(f32)
    matrix = center - weights / norm
    return jnp.stack(split(matrix), axis=1).reshape(2 * frame_count, matrix.shape[1])


def smooth_matrix(smooth_kernel):
    depth = WINDOW + 2 * EDGE
    parts = WINDOW // BLOCK
    out_ids = jnp.arange(WINDOW, dtype=jnp.int32).reshape(parts, 1, BLOCK, 1)
    in_ids = jnp.arange(depth, dtype=jnp.int32)
    step = in_ids - out_ids - (EDGE - REACH)
    hit = step[..., None] == jnp.arange(SIDE, dtype=jnp.int32)
    table = jnp.sum(jnp.where(hit, smooth_kernel.T[None, :, None, None, :], 0.0), axis=4)
    high, low = split(table)
    return jnp.concatenate([high, high, low], axis=3).reshape(SIDE * WINDOW, 3 * depth)


def iota(shape, dim):
    return lax.broadcasted_iota(jnp.int32, shape, dim)


def slab_kernel(
    row_step, frame_step,
    spots_ref, taps_ref, w2_ref, low_ref, own_ref, high_ref, edge_ref, below_ref, above_ref,
    out_ref, last_ref, w1, chi, clo, carry, outer, kept, flat,
):
    frame_count, tiles, row_count, _ = kept.shape
    near = taps_ref.shape[1]
    steps_1 = row_count // row_step
    steps_2 = frame_count // frame_step
    at = pl.program_id(0)

    def filtered(block):
        part = block.reshape(near * 8, block.shape[2])
        both = jnp.dot(w1[...], part, preferred_element_type=f32)
        both = both.reshape(frame_count, 2, 8, block.shape[2])
        return both[:, 0] + both[:, 1]

    def keep(above, below, tile, place):
        value = jnp.concatenate([above, below], axis=1)
        high = value.astype(bf16)
        chi[:, tile, place, :] = high
        clo[:, tile, place, :] = (value - high.astype(f32)).astype(bf16)

    @pl.when(at == 0)
    def _():
        count = 2 * frame_count
        tall = (iota((8 * count, count), 0) // 8 == iota((8 * count, count), 1)).astype(bf16)
        wide = (iota((near, 8 * near), 1) // 8 == iota((near, 8 * near), 0)).astype(bf16)
        full = jnp.dot(tall, taps_ref[...], preferred_element_type=f32).astype(bf16)
        full = jnp.dot(full, wide, preferred_element_type=f32)
        same = iota(full.shape, 0) % 8 == iota(full.shape, 1) % 8
        w1[...] = jnp.where(same, full, 0.0).astype(bf16)
        for tile in range(0, tiles + 1, GROUP):
            pair = range(tile, min(tile + GROUP, tiles + 1))
            cols = slice(tile * TILE, (tile + len(pair)) * TILE)
            below = below_ref[0, :, :, cols].astype(f32)
            above = above_ref[0, :, :, cols].astype(f32)
            gap = jnp.zeros((near, 8 - 2 * REACH, below.shape[2]), f32)
            both = filtered(jnp.concatenate([below, gap, above], axis=1).astype(bf16))
            for q, one in enumerate(pair):
                carry[:, one] = both[..., q * TILE : (q + 1) * TILE]
                outer[:, one] = both[..., q * TILE : (q + 1) * TILE]

    @pl.when(at < steps_1)
    def _():
        def keep_all(tile, parts):
            parts = [carry[:, tile]] + parts
            for q in range(0, len(parts) - 1, 2):
                place = pl.ds(pl.multiple_of(at * row_step + EDGE * q, BLOCK), BLOCK)
                keep(parts[q], parts[q + 1], tile, place)
            carry[:, tile] = parts[-1]

        for tile in range(0, tiles, 2):
            group = range(tile, min(tile + 2, tiles))
            cols = slice(tile * TILE, (tile + len(group)) * TILE)
            parts = []
            for h in range(0, row_step, EDGE):
                rows = slice(h, h + EDGE)
                block = jnp.concatenate(
                    [low_ref[:, rows, cols], own_ref[0, :, rows, cols], high_ref[:, rows, cols]],
                    axis=0,
                )
                parts.append(filtered(block))
            for q, one in enumerate(group):
                keep_all(one, [part[..., q * TILE : (q + 1) * TILE] for part in parts])
        both = filtered(
            jnp.concatenate(
                [edge_ref[0, :, h : h + EDGE] for h in range(0, row_step, EDGE)], axis=2
            )
        )
        parts = [both[..., h * TILE : (h + 1) * TILE] for h in range(row_step // EDGE)]
        keep_all(tiles, parts)

    @pl.when(at == steps_1 - 1)
    def _():
        for tile in range(tiles + 1):
            keep(carry[:, tile], outer[:, tile], tile, slice(row_count, row_count + BLOCK))

    @pl.when((at >= steps_1) & (at < steps_1 + steps_2))
    def _():
        lane = iota((BLOCK, TILE), 1)
        edge_of = [lane < 2, lane < 1, None, lane >= TILE - 1, lane >= TILE - 2]

        depth = WINDOW + 2 * EDGE
        parts_of = range(WINDOW // BLOCK)

        def two_frames(k2, unused):
            for row in range(0, row_count, WINDOW):
                turned = {}
                done = [0, 0]

                def finish(f, tile):
                    k = k2 * 2 + f
                    frame = (at - steps_1) * frame_step + k
                    for m in parts_of:
                        total = turned[f, m, REACH, tile]
                        for b in range(SIDE):
                            if b != REACH:
                                beside = (tile + (1 if b > REACH else -1)) % (tiles + 1)
                                total = total + jnp.where(
                                    edge_of[b], turned[f, m, b, beside], turned[f, m, b, tile]
                                )
                        value = total.astype(bf16)
                        rows = slice(row + m * BLOCK, row + (m + 1) * BLOCK)
                        out_ref[0, k, rows, tile * TILE : (tile + 1) * TILE] = value
                        kept[frame, tile, rows, :] = value.astype(f32)

                order = [(f, tile) for f in range(2) for tile in [tiles] + list(range(tiles))]
                for p in range(0, len(order), GROUP):
                    pair = order[p : p + GROUP]
                    stacks = []
                    for f, tile in pair:
                        frame = (at - steps_1) * frame_step + k2 * 2 + f
                        high = chi[frame, tile, row : row + depth, :]
                        low = clo[frame, tile, row : row + depth, :]
                        stacks.append(jnp.concatenate([high, low, high], axis=0))
                    both = jnp.dot(
                        w2_ref[...], jnp.concatenate(stacks, axis=1), preferred_element_type=f32
                    )
                    for q, (f, tile) in enumerate(pair):
                        for m in parts_of:
                            for b in range(SIDE):
                                at_row = (m * SIDE + b) * BLOCK
                                part = both[at_row : at_row + BLOCK, q * TILE : (q + 1) * TILE]
                                if b != REACH:
                                    part = pltpu.roll(part, (REACH - b) % TILE, 1)
                                turned[f, m, b, tile] = part
                    for f in range(2):
                        while done[f] < tiles and (f, 0, 0, done[f]) in turned:
                            after = min(done[f] + 1, tiles)
                            if (f, 0, 0, after) not in turned:
                                break
                            finish(f, done[f])
                            done[f] += 1
            return unused

        lax.fori_loop(0, frame_step // 2, two_frames, 0)

    @pl.when(at == steps_1 + steps_2)
    def _():
        slot_count = flat.shape[0] // PATCH

        lane = iota((PATCH, TILE), 1)

        def some(i8, unused):
            for j in range(16):
                i = i8 * 16 + j
                frame, row, tile = spots_ref[0, i], spots_ref[1, i], spots_ref[2, i]
                beside, turn = spots_ref[3, i], spots_ref[4, i]
                here = kept[frame, tile, pl.ds(row, PATCH), :]
                there = kept[frame, beside, pl.ds(row, PATCH), :]
                shift = turn & (TILE - 1)
                here, there = pltpu.roll(here, shift, 1), pltpu.roll(there, shift, 1)
                part = jnp.where(lane < turn, here, there)
                flat[pl.ds(pl.multiple_of(i * PATCH, PATCH), PATCH), :] = part.astype(bf16)
            return unused

        lax.fori_loop(0, slot_count // 16, some, 0)
        low_bits = PATCH - 1
        bits = low_bits.bit_length()
        shape = (TILE, PATCH * PATCH)
        repeat = (iota(shape, 1) & low_bits == iota(shape, 0)).astype(bf16)
        rows = jnp.dot(flat[...], repeat, preferred_element_type=f32)
        mine = iota(rows.shape, 1) >> bits == iota(rows.shape, 0) & low_bits
        rows = jnp.where(mine, rows, 0.0).astype(bf16)
        shape = (slot_count, rows.shape[0])
        owner = (iota(shape, 1) >> bits == iota(shape, 0)).astype(bf16)
        values = jnp.dot(owner, rows, preferred_element_type=f32)
        mean = jnp.sum(values, axis=1, keepdims=True) / (PATCH * PATCH)
        centered = values - mean
        spread = jnp.sum(centered * centered, axis=1, keepdims=True) / (PATCH * PATCH)
        normed = centered / jnp.sqrt(spread + 1e-05)
        live = iota((slot_count, 1), 0) < spots_ref[5, 0]
        last_ref[...] = jnp.where(live, normed, 0.0).astype(bf16)


def edges_of(top, bottom, left, right):
    rows = jnp.concatenate(
        [top[...].astype(f32)[:, :REACH], bottom[...].astype(f32)[:, BLOCK - REACH :]], axis=1
    )
    line = iota((8, TILE), 0)
    lane = iota((8, TILE), 1)
    first = ((line == lane) & (line < REACH)).astype(bf16)
    last = ((line + TILE - 2 * REACH == lane) & (line >= REACH)).astype(bf16)
    over_lanes = (((1,), (1,)), ((), ()))
    cols = []
    for f in range(rows.shape[0]):
        one = lax.dot_general(first, left[f], over_lanes, preferred_element_type=f32)
        one += lax.dot_general(last, right[f], over_lanes, preferred_element_type=f32)
        cols.append(one[: 2 * REACH].astype(bf16))
    return rows.astype(bf16), cols


def send_all(frames, slab, low, high, whole, sems):
    frame_count = whole.shape[0]
    half = (HALF + 1) // 2
    spans = []
    for target, base in ((high, 0), (low, frame_count - HALF)):
        for start, count in ((0, half), (half, HALF - half)):
            spans.append((target, base + start, start, count))
    fetches, writes = [], []
    for i, (target, source, start, count) in enumerate(spans):
        here = whole.at[pl.ds(source, count)]
        fetches.append(
            pltpu.make_async_copy(frames.at[slab, pl.ds(source, count)], here, sems.at[2 * i])
        )
        writes.append(
            pltpu.make_async_copy(here, target.at[pl.ds(start, count)], sems.at[2 * i + 1])
        )
    return fetches, writes


def cut_kernel(frames, rim, rim_low, rim_high, low, high, whole, top, bottom, left, right, sems):
    frame_count, row_count, col_count = whole.shape
    reads = [
        pltpu.make_async_copy(source, target, sems.at[8 + i])
        for i, (source, target) in enumerate(
            [
                (frames.at[0, :, pl.ds(0, BLOCK), :], top),
                (frames.at[0, :, pl.ds(row_count - BLOCK, BLOCK), :], bottom),
                (frames.at[0, :, :, pl.ds(0, TILE)], left),
                (frames.at[0, :, :, pl.ds(col_count - TILE, TILE)], right),
                (frames.at[1, pl.ds(HALF, frame_count - 2 * HALF)],
                 whole.at[pl.ds(HALF, frame_count - 2 * HALF)]),
            ]
        )
    ]
    fetches, writes = send_all(frames, 1, low, high, whole, sems)
    for copy in reads + fetches:
        copy.start()

    def put(slab, rows, cols):
        middle = frame_count - HALF
        for target, start in [(rim, 0), (rim_low, middle), (rim_high, 0)]:
            count = target.shape[1]
            target[slab, :, :, :col_count] = rows[start : start + count]
            for f in range(count):
                target[slab, f, :, col_count:] = cols[start + f]

    for copy in reads:
        copy.wait()
    put(0, *edges_of(top, bottom, left, right))
    for fetch, write in zip(fetches, writes):
        fetch.wait()
        write.start()
    put(
        1,
        *edges_of(
            whole.at[:, pl.ds(0, BLOCK), :],
            whole.at[:, pl.ds(row_count - BLOCK, BLOCK), :],
            whole.at[:, :, pl.ds(0, TILE)],
            whole.at[:, :, pl.ds(col_count - TILE, TILE)],
        ),
    )
    for write in writes:
        write.wait()


def late_kernel(frames, low, high, whole, sems):
    fetches, writes = send_all(frames, 0, low, high, whole, sems)
    for fetch in fetches:
        fetch.start()
    for fetch, write in zip(fetches, writes):
        fetch.wait()
        write.start()
    for write in writes:
        write.wait()


def cut(frames):
    slabs, frame_count, row_count, col_count = frames.shape
    anywhere = pl.BlockSpec(memory_space=pl.ANY)
    near = pl.BlockSpec(memory_space=pltpu.VMEM)
    piece = jax.ShapeDtypeStruct((HALF, row_count, col_count), bf16)
    wide = col_count + row_count
    rims = [
        jax.ShapeDtypeStruct((slabs, count, 2 * REACH, wide), bf16)
        for count in (frame_count, HALF, HALF)
    ]
    return pl.pallas_call(
        cut_kernel,
        in_specs=[anywhere],
        out_specs=[near] * 3 + [anywhere] * 2,
        out_shape=rims + [piece, piece],
        scratch_shapes=[
            pltpu.VMEM((frame_count, row_count, col_count), bf16),
            pltpu.VMEM((frame_count, BLOCK, col_count), bf16),
            pltpu.VMEM((frame_count, BLOCK, col_count), bf16),
            pltpu.VMEM((frame_count, row_count, TILE), bf16),
            pltpu.VMEM((frame_count, row_count, TILE), bf16),
            pltpu.SemaphoreType.DMA((13,)),
        ],
        compiler_params=pltpu.CompilerParams(vmem_limit_bytes=60 * 1024 * 1024),
        name="cut",
    )(frames)


def late_cut(frames):
    _, frame_count, row_count, col_count = frames.shape
    anywhere = pl.BlockSpec(memory_space=pl.ANY)
    piece = jax.ShapeDtypeStruct((HALF, row_count, col_count), bf16)
    return pl.pallas_call(
        late_kernel,
        in_specs=[anywhere],
        out_specs=[anywhere] * 2,
        out_shape=[piece, piece],
        scratch_shapes=[
            pltpu.VMEM((frame_count, row_count, col_count), bf16),
            pltpu.SemaphoreType.DMA((8,)),
        ],
        compiler_params=pltpu.CompilerParams(vmem_limit_bytes=60 * 1024 * 1024),
        cost_estimate=pl.CostEstimate(flops=0, bytes_accessed=9_000_000, transcendentals=0),
        name="late_cut",
    )(frames)


def run_slab(slab, smoothed, spots, taps, w2, low, frames, high, edge, below, above):
    _, frame_count, row_count, col_count = frames.shape
    slot_count = spots.shape[1]
    row_step, frame_step = 32, 8
    steps_1 = row_count // row_step
    steps_2 = frame_count // frame_step
    wide = col_count + TILE
    near = frame_count + 2 * HALF

    def row_block(at):
        return jnp.minimum(at, steps_1 - 1)

    def whole(array):
        return pl.BlockSpec(array.shape, lambda at: (0,) * array.ndim)

    operands = [spots, taps, w2, low, frames, high, edge, below, above]
    in_specs = [
        pl.BlockSpec(memory_space=pltpu.SMEM),
        whole(taps),
        whole(w2),
        pl.BlockSpec((HALF, row_step, col_count), lambda at: (0, row_block(at), 0)),
        pl.BlockSpec((1, frame_count, row_step, col_count), lambda at: (slab, 0, row_block(at), 0)),
        pl.BlockSpec((HALF, row_step, col_count), lambda at: (0, row_block(at), 0)),
        pl.BlockSpec((1, near, row_step, TILE), lambda at: (slab, 0, row_block(at), 0)),
        pl.BlockSpec((1, near, REACH, wide), lambda at: (slab, 0, 0, 0)),
        pl.BlockSpec((1, near, REACH, wide), lambda at: (slab, 0, 0, 0)),
    ]
    aliases = {}
    if smoothed is not None:
        operands.append(smoothed)
        in_specs.append(pl.BlockSpec(memory_space=pl.ANY))
        aliases = {len(operands) - 1: 0}
    count = len(operands)

    def body(*refs):
        slab_kernel(row_step, frame_step, *refs[:9], *refs[count:])

    tall = row_count + 2 * EDGE
    return pl.pallas_call(
        body,
        grid=(steps_1 + steps_2 + 1,),
        in_specs=in_specs,
        out_specs=[
            pl.BlockSpec(
                (1, frame_step, row_count, col_count),
                lambda at: (slab, jnp.clip(at - steps_1, 0, steps_2 - 1), 0, 0),
            ),
            pl.BlockSpec((slot_count, PATCH * PATCH), lambda at: (0, 0)),
        ],
        out_shape=[
            jax.ShapeDtypeStruct(frames.shape, bf16),
            jax.ShapeDtypeStruct((slot_count, PATCH * PATCH), bf16),
        ],
        scratch_shapes=[
            pltpu.VMEM((16 * frame_count, 8 * near), bf16),
            pltpu.VMEM((frame_count, wide // TILE, tall, TILE), bf16),
            pltpu.VMEM((frame_count, wide // TILE, tall, TILE), bf16),
            pltpu.VMEM((frame_count, wide // TILE, EDGE, TILE), f32),
            pltpu.VMEM((frame_count, wide // TILE, EDGE, TILE), f32),
            pltpu.VMEM((frame_count, col_count // TILE, row_count, TILE), f32),
            pltpu.VMEM((slot_count * PATCH, TILE), bf16),
        ],
        input_output_aliases=aliases,
        compiler_params=pltpu.CompilerParams(vmem_limit_bytes=40 * 1024 * 1024),
        cost_estimate=pl.CostEstimate(
            flops=20_000_000_000, bytes_accessed=16_000_000, transcendentals=0
        ),
        name=f"slab_{slab}",
    )(*operands)


def shards(frames, omega_taps, smooth_kernel, spots, counts):
    _, frame_count, row_count, col_count = frames.shape
    first_frame = lax.axis_index("omega") * frame_count
    first_row = lax.axis_index("row") * row_count
    first_col = lax.axis_index("col") * col_count

    rim, rim_low, rim_high, send_low1, send_high1 = cut(frames)
    rim = jnp.concatenate(
        [shifted(rim_low, "omega", 1), rim, shifted(rim_high, "omega", -1)], axis=1
    )
    low1 = shifted(send_low1, "omega", 1)
    high1 = shifted(send_high1, "omega", -1)
    lane = jnp.arange(TILE, dtype=jnp.int32)[None, :]
    step = jnp.arange(REACH, dtype=jnp.int32)[:, None]
    after = (lane == step).astype(bf16)
    before = (lane == TILE - REACH + step).astype(bf16)
    if lax.axis_size("col") == 2:
        first = lax.axis_index("col") == 0
        sides = jnp.where(first, rim[:, :, REACH:, col_count:], rim[:, :, :REACH, col_count:])
        sides = lax.ppermute(sides, "col", [(0, 1), (1, 0)])
        place = jnp.where(first, after, before)
    else:
        left = shifted(rim[:, :, REACH:, col_count:], "col", 1)
        right = shifted(rim[:, :, :REACH, col_count:], "col", -1)
        sides = jnp.concatenate([right, left], axis=2)
        place = jnp.concatenate([after, before], axis=0)
    later, sides = lax.optimization_barrier((frames, sides))
    send_low0, send_high0 = late_cut(later)
    low0 = shifted(send_low0, "omega", 1)
    high0 = shifted(send_high0, "omega", -1)
    edge = jnp.einsum("sfkr,kc->sfrc", sides, place, preferred_element_type=bf16)
    ends = jnp.concatenate([edge[:, :, :REACH], edge[:, :, -REACH:]], axis=2)
    line = jnp.concatenate([rim[..., :col_count], ends], axis=3)
    above = shifted(line[:, :, REACH:], "row", 1)
    below = shifted(line[:, :, :REACH], "row", -1)

    taps = omega_matrix(
        omega_taps, first_frame, frame_count, frame_count * lax.axis_size("omega")
    )
    w2 = smooth_matrix(smooth_kernel)
    frame, row, col = spots[:, 0] - first_frame, spots[:, 1] - first_row, spots[:, 2] - first_col
    tile = col // TILE
    beside = jnp.minimum(tile + 1, col_count // TILE - 1)
    live = jnp.broadcast_to(counts, frame.shape)
    local = jnp.stack([frame, row, tile, beside, TILE - col % TILE, live], axis=1)

    smoothed, second = run_slab(1, None, local[1], taps, w2, low1, frames, high1, edge, below, above)
    count = lax.axis_size("row") * lax.axis_size("col")
    second = lax.ppermute(second, ("row", "col"), [(i, count - 1 - i) for i in range(count)])
    smoothed, first = run_slab(0, smoothed, local[0], taps, w2, low0, frames, high0, edge, below, above)
    scores = (
        lax.dot_general(first, second, (((1,), (1,)), ((), ())), preferred_element_type=f32)
        / float(PATCH * PATCH)
    )
    return (smoothed, scores)


def solution(mesh):
    return jax.shard_map(
        shards,
        mesh=mesh,
        in_specs=(
            P(None, "omega", "row", "col"),
            P(),
            P(),
            P(None, None, ("omega", "row", "col")),
            P(None, ("omega", "row", "col")),
        ),
        out_specs=(P(None, "omega", "row", "col"), P(("omega", "row", "col"), None)),
        check_vma=False,
    )
```

```python
import jax
import jax.numpy as jnp
from jax import lax
from jax.experimental import pallas as pl
from jax.experimental.pallas import tpu as pltpu
from jax.sharding import PartitionSpec as P

TAPS = 15
HALF = TAPS // 2
PATCH = 16
SIDE = 5
REACH = SIDE // 2
TILE = 128
BLOCK = 16
WINDOW = 32
EDGE = 8
GROUP = 4
bf16 = jnp.bfloat16
f32 = jnp.float32


def shifted(block, axis, step):
    count = lax.axis_size(axis)
    route = [(i, i + step) for i in range(count) if 0 <= i + step < count]
    return lax.ppermute(block, axis, route)


def split(values):
    high = lax.reduce_precision(values, 8, 7)
    return high.astype(bf16), (values - high).astype(bf16)


def omega_matrix(omega_taps, first_frame, frame_count, frame_total):
    out_ids = jnp.arange(frame_count, dtype=jnp.int32)[:, None]
    in_ids = jnp.arange(frame_count + 2 * HALF, dtype=jnp.int32)[None, :]
    source = first_frame + in_ids - HALF
    valid = (source >= 0) & (source < frame_total)
    tap = jnp.where(valid, in_ids - out_ids, -1)
    hit = tap[:, :, None] == jnp.arange(TAPS, dtype=jnp.int32)
    weights = jnp.sum(jnp.where(hit, omega_taps, 0.0), axis=2)
    norm = jnp.sum(weights, axis=1, keepdims=True)
    center = (in_ids - out_ids == HALF).astype(f32)
    matrix = center - weights / norm
    return jnp.stack(split(matrix), axis=1).reshape(2 * frame_count, matrix.shape[1])


def smooth_matrix(smooth_kernel):
    depth = WINDOW + 2 * EDGE
    parts = WINDOW // BLOCK
    out_ids = jnp.arange(WINDOW, dtype=jnp.int32).reshape(parts, 1, BLOCK, 1)
    in_ids = jnp.arange(depth, dtype=jnp.int32)
    step = in_ids - out_ids - (EDGE - REACH)
    hit = step[..., None] == jnp.arange(SIDE, dtype=jnp.int32)
    table = jnp.sum(jnp.where(hit, smooth_kernel.T[None, :, None, None, :], 0.0), axis=4)
    high, low = split(table)
    return jnp.concatenate([high, high, low], axis=3).reshape(SIDE * WINDOW, 3 * depth)


def iota(shape, dim):
    return lax.broadcasted_iota(jnp.int32, shape, dim)


def slab_kernel(
    row_step, frame_step,
    spots_ref, taps_ref, w2_ref, low_ref, own_ref, high_ref, edge_ref, below_ref, above_ref,
    out_ref, last_ref, w1, chi, clo, carry, outer, kept, flat,
):
    frame_count, tiles, row_count, _ = kept.shape
    near = taps_ref.shape[1]
    steps_1 = row_count // row_step
    steps_2 = frame_count // frame_step
    at = pl.program_id(0)

    def filtered(block):
        part = block.reshape(near * 8, block.shape[2])
        both = jnp.dot(w1[...], part, preferred_element_type=f32)
        both = both.reshape(frame_count, 2, 8, block.shape[2])
        return both[:, 0] + both[:, 1]

    def keep(above, below, tile, place):
        value = jnp.concatenate([above, below], axis=1)
        high = value.astype(bf16)
        chi[:, tile, place, :] = high
        clo[:, tile, place, :] = (value - high.astype(f32)).astype(bf16)

    @pl.when(at == 0)
    def _():
        count = 2 * frame_count
        tall = (iota((8 * count, count), 0) // 8 == iota((8 * count, count), 1)).astype(bf16)
        wide = (iota((near, 8 * near), 1) // 8 == iota((near, 8 * near), 0)).astype(bf16)
        full = jnp.dot(tall, taps_ref[...], preferred_element_type=f32).astype(bf16)
        full = jnp.dot(full, wide, preferred_element_type=f32)
        same = iota(full.shape, 0) % 8 == iota(full.shape, 1) % 8
        w1[...] = jnp.where(same, full, 0.0).astype(bf16)
        for tile in range(0, tiles + 1, GROUP):
            pair = range(tile, min(tile + GROUP, tiles + 1))
            cols = slice(tile * TILE, (tile + len(pair)) * TILE)
            below = below_ref[0, :, :, cols].astype(f32)
            above = above_ref[0, :, :, cols].astype(f32)
            gap = jnp.zeros((near, 8 - 2 * REACH, below.shape[2]), f32)
            both = filtered(jnp.concatenate([below, gap, above], axis=1).astype(bf16))
            for q, one in enumerate(pair):
                carry[:, one] = both[..., q * TILE : (q + 1) * TILE]
                outer[:, one] = both[..., q * TILE : (q + 1) * TILE]

    @pl.when(at < steps_1)
    def _():
        def keep_all(tile, parts):
            parts = [carry[:, tile]] + parts
            for q in range(0, len(parts) - 1, 2):
                place = pl.ds(pl.multiple_of(at * row_step + EDGE * q, BLOCK), BLOCK)
                keep(parts[q], parts[q + 1], tile, place)
            carry[:, tile] = parts[-1]

        for tile in range(0, tiles, 2):
            group = range(tile, min(tile + 2, tiles))
            cols = slice(tile * TILE, (tile + len(group)) * TILE)
            parts = []
            for h in range(0, row_step, EDGE):
                rows = slice(h, h + EDGE)
                block = jnp.concatenate(
                    [low_ref[:, rows, cols], own_ref[0, :, rows, cols], high_ref[:, rows, cols]],
                    axis=0,
                )
                parts.append(filtered(block))
            for q, one in enumerate(group):
                keep_all(one, [part[..., q * TILE : (q + 1) * TILE] for part in parts])
        both = filtered(
            jnp.concatenate(
                [edge_ref[0, :, h : h + EDGE] for h in range(0, row_step, EDGE)], axis=2
            )
        )
        parts = [both[..., h * TILE : (h + 1) * TILE] for h in range(row_step // EDGE)]
        keep_all(tiles, parts)

    @pl.when(at == steps_1 - 1)
    def _():
        for tile in range(tiles + 1):
            keep(carry[:, tile], outer[:, tile], tile, slice(row_count, row_count + BLOCK))

    @pl.when((at >= steps_1) & (at < steps_1 + steps_2))
    def _():
        lane = iota((BLOCK, TILE), 1)
        edge_of = [lane < 2, lane < 1, None, lane >= TILE - 1, lane >= TILE - 2]

        depth = WINDOW + 2 * EDGE
        parts_of = range(WINDOW // BLOCK)

        def two_frames(k2, unused):
            for row in range(0, row_count, WINDOW):
                turned = {}
                done = [0, 0]

                def finish(f, tile):
                    k = k2 * 2 + f
                    frame = (at - steps_1) * frame_step + k
                    for m in parts_of:
                        total = turned[f, m, REACH, tile]
                        for b in range(SIDE):
                            if b != REACH:
                                beside = (tile + (1 if b > REACH else -1)) % (tiles + 1)
                                total = total + jnp.where(
                                    edge_of[b], turned[f, m, b, beside], turned[f, m, b, tile]
                                )
                        value = total.astype(bf16)
                        rows = slice(row + m * BLOCK, row + (m + 1) * BLOCK)
                        out_ref[0, k, rows, tile * TILE : (tile + 1) * TILE] = value
                        kept[frame, tile, rows, :] = value.astype(f32)

                order = [(f, tile) for f in range(2) for tile in [tiles] + list(range(tiles))]
                for p in range(0, len(order), GROUP):
                    pair = order[p : p + GROUP]
                    stacks = []
                    for f, tile in pair:
                        frame = (at - steps_1) * frame_step + k2 * 2 + f
                        high = chi[frame, tile, row : row + depth, :]
                        low = clo[frame, tile, row : row + depth, :]
                        stacks.append(jnp.concatenate([high, low, high], axis=0))
                    both = jnp.dot(
                        w2_ref[...], jnp.concatenate(stacks, axis=1), preferred_element_type=f32
                    )
                    for q, (f, tile) in enumerate(pair):
                        for m in parts_of:
                            for b in range(SIDE):
                                at_row = (m * SIDE + b) * BLOCK
                                part = both[at_row : at_row + BLOCK, q * TILE : (q + 1) * TILE]
                                if b != REACH:
                                    part = pltpu.roll(part, (REACH - b) % TILE, 1)
                                turned[f, m, b, tile] = part
                    for f in range(2):
                        while done[f] < tiles and (f, 0, 0, done[f]) in turned:
                            after = min(done[f] + 1, tiles)
                            if (f, 0, 0, after) not in turned:
                                break
                            finish(f, done[f])
                            done[f] += 1
            return unused

        lax.fori_loop(0, frame_step // 2, two_frames, 0)

    @pl.when(at == steps_1 + steps_2)
    def _():
        slot_count = flat.shape[0] // PATCH

        lane = iota((PATCH, TILE), 1)

        def some(i8, unused):
            for j in range(16):
                i = i8 * 16 + j
                frame, row, tile = spots_ref[0, i], spots_ref[1, i], spots_ref[2, i]
                beside, offset = spots_ref[3, i], spots_ref[4, i]
                here = kept[frame, tile, pl.ds(row, PATCH), :]
                there = kept[frame, beside, pl.ds(row, PATCH), :]
                part = jnp.where(lane >= offset, here, there)
                part = pltpu.roll(part, (TILE - offset) & (TILE - 1), 1)
                flat[pl.ds(pl.multiple_of(i * PATCH, PATCH), PATCH), :] = part.astype(bf16)
            return unused

        lax.fori_loop(0, slot_count // 16, some, 0)
        low_bits = PATCH - 1
        bits = low_bits.bit_length()
        shape = (TILE, PATCH * PATCH)
        repeat = (iota(shape, 1) & low_bits == iota(shape, 0)).astype(bf16)
        rows = jnp.dot(flat[...], repeat, preferred_element_type=f32)
        mine = iota(rows.shape, 1) >> bits == iota(rows.shape, 0) & low_bits
        rows = jnp.where(mine, rows, 0.0).astype(bf16)
        shape = (slot_count, rows.shape[0])
        owner = (iota(shape, 1) >> bits == iota(shape, 0)).astype(bf16)
        values = jnp.dot(owner, rows, preferred_element_type=f32)
        mean = jnp.sum(values, axis=1, keepdims=True) / (PATCH * PATCH)
        centered = values - mean
        spread = jnp.sum(centered * centered, axis=1, keepdims=True) / (PATCH * PATCH)
        normed = centered / jnp.sqrt(spread + 1e-05)
        live = iota((slot_count, 1), 0) < spots_ref[5, 0]
        last_ref[...] = jnp.where(live, normed, 0.0).astype(bf16)


def edges_of(top, bottom, left, right):
    rows = jnp.concatenate(
        [top[...].astype(f32)[:, :REACH], bottom[...].astype(f32)[:, BLOCK - REACH :]], axis=1
    )
    line = iota((8, 2 * TILE), 0)
    lane = iota((8, 2 * TILE), 1)
    first = (line == lane) & (line < REACH)
    last = (line + 2 * TILE - 2 * REACH == lane) & (line >= REACH)
    chosen = (first | last).astype(bf16)
    row_count = left.shape[1]
    cols = []
    for f in range(0, rows.shape[0], 2):
        both = jnp.concatenate([left[f : f + 2], right[f : f + 2]], axis=2)
        both = both.reshape(2 * row_count, 2 * TILE)
        one = lax.dot_general(
            chosen, both, (((1,), (1,)), ((), ())), preferred_element_type=f32
        )
        one = one[: 2 * REACH].astype(bf16)
        cols += [one[:, :row_count], one[:, row_count:]]
    return rows.astype(bf16), cols


def send_all(frames, slab, low, high, whole, sems):
    frame_count = whole.shape[0]
    half = (HALF + 1) // 2
    spans = []
    for target, base in ((high, 0), (low, frame_count - HALF)):
        for start, count in ((0, half), (half, HALF - half)):
            spans.append((target, base + start, start, count))
    fetches, writes = [], []
    for i, (target, source, start, count) in enumerate(spans):
        here = whole.at[pl.ds(source, count)]
        fetches.append(
            pltpu.make_async_copy(frames.at[slab, pl.ds(source, count)], here, sems.at[2 * i])
        )
        writes.append(
            pltpu.make_async_copy(here, target.at[pl.ds(start, count)], sems.at[2 * i + 1])
        )
    return fetches, writes


def cut_kernel(frames, rim, rim_low, rim_high, low, high, whole, top, bottom, left, right, sems):
    frame_count, row_count, col_count = whole.shape
    reads = [
        pltpu.make_async_copy(source, target, sems.at[8 + i])
        for i, (source, target) in enumerate(
            [
                (frames.at[0, :, pl.ds(0, BLOCK), :], top),
                (frames.at[0, :, pl.ds(row_count - BLOCK, BLOCK), :], bottom),
                (frames.at[0, :, :, pl.ds(0, TILE)], left),
                (frames.at[0, :, :, pl.ds(col_count - TILE, TILE)], right),
                (frames.at[1, pl.ds(HALF, frame_count - 2 * HALF)],
                 whole.at[pl.ds(HALF, frame_count - 2 * HALF)]),
            ]
        )
    ]
    fetches, writes = send_all(frames, 1, low, high, whole, sems)
    for copy in reads + fetches:
        copy.start()

    def put(slab, rows, cols):
        middle = frame_count - HALF
        for target, start in [(rim, 0), (rim_low, middle), (rim_high, 0)]:
            count = target.shape[1]
            target[slab, :, :, :col_count] = rows[start : start + count]
            for f in range(count):
                target[slab, f, :, col_count:] = cols[start + f]

    for copy in reads:
        copy.wait()
    put(0, *edges_of(top, bottom, left, right))
    for fetch, write in zip(fetches, writes):
        fetch.wait()
        write.start()
    put(
        1,
        *edges_of(
            whole.at[:, pl.ds(0, BLOCK), :],
            whole.at[:, pl.ds(row_count - BLOCK, BLOCK), :],
            whole.at[:, :, pl.ds(0, TILE)],
            whole.at[:, :, pl.ds(col_count - TILE, TILE)],
        ),
    )
    for write in writes:
        write.wait()


def late_kernel(frames, low, high, whole, sems):
    fetches, writes = send_all(frames, 0, low, high, whole, sems)
    for fetch in fetches:
        fetch.start()
    for fetch, write in zip(fetches, writes):
        fetch.wait()
        write.start()
    for write in writes:
        write.wait()


def cut(frames):
    slabs, frame_count, row_count, col_count = frames.shape
    anywhere = pl.BlockSpec(memory_space=pl.ANY)
    near = pl.BlockSpec(memory_space=pltpu.VMEM)
    piece = jax.ShapeDtypeStruct((HALF, row_count, col_count), bf16)
    wide = col_count + row_count
    rims = [
        jax.ShapeDtypeStruct((slabs, count, 2 * REACH, wide), bf16)
        for count in (frame_count, HALF, HALF)
    ]
    return pl.pallas_call(
        cut_kernel,
        in_specs=[anywhere],
        out_specs=[near] * 3 + [anywhere] * 2,
        out_shape=rims + [piece, piece],
        scratch_shapes=[
            pltpu.VMEM((frame_count, row_count, col_count), bf16),
            pltpu.VMEM((frame_count, BLOCK, col_count), bf16),
            pltpu.VMEM((frame_count, BLOCK, col_count), bf16),
            pltpu.VMEM((frame_count, row_count, TILE), bf16),
            pltpu.VMEM((frame_count, row_count, TILE), bf16),
            pltpu.SemaphoreType.DMA((13,)),
        ],
        compiler_params=pltpu.CompilerParams(vmem_limit_bytes=60 * 1024 * 1024),
        name="cut",
    )(frames)


def late_cut(frames):
    _, frame_count, row_count, col_count = frames.shape
    anywhere = pl.BlockSpec(memory_space=pl.ANY)
    piece = jax.ShapeDtypeStruct((HALF, row_count, col_count), bf16)
    return pl.pallas_call(
        late_kernel,
        in_specs=[anywhere],
        out_specs=[anywhere] * 2,
        out_shape=[piece, piece],
        scratch_shapes=[
            pltpu.VMEM((frame_count, row_count, col_count), bf16),
            pltpu.SemaphoreType.DMA((8,)),
        ],
        compiler_params=pltpu.CompilerParams(vmem_limit_bytes=60 * 1024 * 1024),
        cost_estimate=pl.CostEstimate(flops=0, bytes_accessed=9_000_000, transcendentals=0),
        name="late_cut",
    )(frames)


def run_slab(slab, smoothed, spots, taps, w2, low, frames, high, edge, below, above):
    _, frame_count, row_count, col_count = frames.shape
    slot_count = spots.shape[1]
    row_step, frame_step = 32, 8
    steps_1 = row_count // row_step
    steps_2 = frame_count // frame_step
    wide = col_count + TILE
    near = frame_count + 2 * HALF

    def row_block(at):
        return jnp.minimum(at, steps_1 - 1)

    def whole(array):
        return pl.BlockSpec(array.shape, lambda at: (0,) * array.ndim)

    operands = [spots, taps, w2, low, frames, high, edge, below, above]
    in_specs = [
        pl.BlockSpec(memory_space=pltpu.SMEM),
        whole(taps),
        whole(w2),
        pl.BlockSpec((HALF, row_step, col_count), lambda at: (0, row_block(at), 0)),
        pl.BlockSpec((1, frame_count, row_step, col_count), lambda at: (slab, 0, row_block(at), 0)),
        pl.BlockSpec((HALF, row_step, col_count), lambda at: (0, row_block(at), 0)),
        pl.BlockSpec((1, near, row_step, TILE), lambda at: (slab, 0, row_block(at), 0)),
        pl.BlockSpec((1, near, REACH, wide), lambda at: (slab, 0, 0, 0)),
        pl.BlockSpec((1, near, REACH, wide), lambda at: (slab, 0, 0, 0)),
    ]
    aliases = {}
    if smoothed is not None:
        operands.append(smoothed)
        in_specs.append(pl.BlockSpec(memory_space=pl.ANY))
        aliases = {len(operands) - 1: 0}
    count = len(operands)

    def body(*refs):
        slab_kernel(row_step, frame_step, *refs[:9], *refs[count:])

    tall = row_count + 2 * EDGE
    return pl.pallas_call(
        body,
        grid=(steps_1 + steps_2 + 1,),
        in_specs=in_specs,
        out_specs=[
            pl.BlockSpec(
                (1, frame_step, row_count, col_count),
                lambda at: (slab, jnp.clip(at - steps_1, 0, steps_2 - 1), 0, 0),
            ),
            pl.BlockSpec((slot_count, PATCH * PATCH), lambda at: (0, 0)),
        ],
        out_shape=[
            jax.ShapeDtypeStruct(frames.shape, bf16),
            jax.ShapeDtypeStruct((slot_count, PATCH * PATCH), bf16),
        ],
        scratch_shapes=[
            pltpu.VMEM((16 * frame_count, 8 * near), bf16),
            pltpu.VMEM((frame_count, wide // TILE, tall, TILE), bf16),
            pltpu.VMEM((frame_count, wide // TILE, tall, TILE), bf16),
            pltpu.VMEM((frame_count, wide // TILE, EDGE, TILE), f32),
            pltpu.VMEM((frame_count, wide // TILE, EDGE, TILE), f32),
            pltpu.VMEM((frame_count, col_count // TILE, row_count, TILE), f32),
            pltpu.VMEM((slot_count * PATCH, TILE), bf16),
        ],
        input_output_aliases=aliases,
        compiler_params=pltpu.CompilerParams(vmem_limit_bytes=40 * 1024 * 1024),
        cost_estimate=pl.CostEstimate(
            flops=20_000_000_000, bytes_accessed=16_000_000, transcendentals=0
        ),
        name=f"slab_{slab}",
    )(*operands)


def shards(frames, omega_taps, smooth_kernel, spots, counts):
    _, frame_count, row_count, col_count = frames.shape
    first_frame = lax.axis_index("omega") * frame_count
    first_row = lax.axis_index("row") * row_count
    first_col = lax.axis_index("col") * col_count

    rim, rim_low, rim_high, send_low1, send_high1 = cut(frames)
    rim = jnp.concatenate(
        [shifted(rim_low, "omega", 1), rim, shifted(rim_high, "omega", -1)], axis=1
    )
    low1 = shifted(send_low1, "omega", 1)
    high1 = shifted(send_high1, "omega", -1)
    lane = jnp.arange(TILE, dtype=jnp.int32)[None, :]
    step = jnp.arange(REACH, dtype=jnp.int32)[:, None]
    after = (lane == step).astype(bf16)
    before = (lane == TILE - REACH + step).astype(bf16)
    if lax.axis_size("col") == 2:
        first = lax.axis_index("col") == 0
        sides = jnp.where(first, rim[:, :, REACH:, col_count:], rim[:, :, :REACH, col_count:])
        sides = lax.ppermute(sides, "col", [(0, 1), (1, 0)])
        place = jnp.where(first, after, before)
    else:
        left = shifted(rim[:, :, REACH:, col_count:], "col", 1)
        right = shifted(rim[:, :, :REACH, col_count:], "col", -1)
        sides = jnp.concatenate([right, left], axis=2)
        place = jnp.concatenate([after, before], axis=0)
    later, sides = lax.optimization_barrier((frames, sides))
    send_low0, send_high0 = late_cut(later)
    low0 = shifted(send_low0, "omega", 1)
    high0 = shifted(send_high0, "omega", -1)
    edge = jnp.einsum("sfkr,kc->sfrc", sides, place, preferred_element_type=bf16)
    ends = jnp.concatenate([edge[:, :, :REACH], edge[:, :, -REACH:]], axis=2)
    line = jnp.concatenate([rim[..., :col_count], ends], axis=3)
    above = shifted(line[:, :, REACH:], "row", 1)
    below = shifted(line[:, :, :REACH], "row", -1)

    taps = omega_matrix(
        omega_taps, first_frame, frame_count, frame_count * lax.axis_size("omega")
    )
    w2 = smooth_matrix(smooth_kernel)
    frame, row, col = spots[:, 0] - first_frame, spots[:, 1] - first_row, spots[:, 2] - first_col
    tile = col // TILE
    beside = jnp.minimum(tile + 1, col_count // TILE - 1)
    live = jnp.broadcast_to(counts, frame.shape)
    local = jnp.stack([frame, row, tile, beside, col % TILE, live], axis=1)

    smoothed, second = run_slab(1, None, local[1], taps, w2, low1, frames, high1, edge, below, above)
    count = lax.axis_size("row") * lax.axis_size("col")
    second = lax.ppermute(second, ("row", "col"), [(i, count - 1 - i) for i in range(count)])
    smoothed, first = run_slab(0, smoothed, local[0], taps, w2, low0, frames, high0, edge, below, above)
    scores = (
        lax.dot_general(first, second, (((1,), (1,)), ((), ())), preferred_element_type=f32)
        / float(PATCH * PATCH)
    )
    return (smoothed, scores)


def solution(mesh):
    return jax.shard_map(
        shards,
        mesh=mesh,
        in_specs=(
            P(None, "omega", "row", "col"),
            P(),
            P(),
            P(None, None, ("omega", "row", "col")),
            P(None, ("omega", "row", "col")),
        ),
        out_specs=(P(None, "omega", "row", "col"), P(("omega", "row", "col"), None)),
        check_vma=False,
    )
```

```python
import jax
import jax.numpy as jnp
from jax import lax
from jax.experimental import pallas as pl
from jax.experimental.pallas import tpu as pltpu
from jax.sharding import PartitionSpec as P

TAPS = 15
HALF = TAPS // 2
PATCH = 16
SIDE = 5
REACH = SIDE // 2
TILE = 128
BLOCK = 16
WINDOW = 32
EDGE = 8
GROUP = 4
bf16 = jnp.bfloat16
f32 = jnp.float32


def shifted(block, axis, step):
    count = lax.axis_size(axis)
    route = [(i, i + step) for i in range(count) if 0 <= i + step < count]
    return lax.ppermute(block, axis, route)


def split(values):
    high = lax.reduce_precision(values, 8, 7)
    return high.astype(bf16), (values - high).astype(bf16)


def omega_matrix(omega_taps, first_frame, frame_count, frame_total):
    out_ids = jnp.arange(frame_count, dtype=jnp.int32)[:, None]
    in_ids = jnp.arange(frame_count + 2 * HALF, dtype=jnp.int32)[None, :]
    source = first_frame + in_ids - HALF
    valid = (source >= 0) & (source < frame_total)
    tap = jnp.where(valid, in_ids - out_ids, -1)
    hit = tap[:, :, None] == jnp.arange(TAPS, dtype=jnp.int32)
    weights = jnp.sum(jnp.where(hit, omega_taps, 0.0), axis=2)
    norm = jnp.sum(weights, axis=1, keepdims=True)
    center = (in_ids - out_ids == HALF).astype(f32)
    matrix = center - weights / norm
    return jnp.stack(split(matrix), axis=1).reshape(2 * frame_count, matrix.shape[1])


def smooth_matrix(smooth_kernel):
    depth = WINDOW + 2 * EDGE
    parts = WINDOW // BLOCK
    out_ids = jnp.arange(WINDOW, dtype=jnp.int32).reshape(parts, 1, BLOCK, 1)
    in_ids = jnp.arange(depth, dtype=jnp.int32)
    step = in_ids - out_ids - (EDGE - REACH)
    hit = step[..., None] == jnp.arange(SIDE, dtype=jnp.int32)
    table = jnp.sum(jnp.where(hit, smooth_kernel.T[None, :, None, None, :], 0.0), axis=4)
    high, low = split(table)
    return jnp.concatenate([high, high, low], axis=3).reshape(SIDE * WINDOW, 3 * depth)


def iota(shape, dim):
    return lax.broadcasted_iota(jnp.int32, shape, dim)


def slab_kernel(
    row_step, frame_step,
    spots_ref, taps_ref, w2_ref, low_ref, own_ref, high_ref, edge_ref, below_ref, above_ref,
    out_ref, last_ref, w1, chi, clo, carry, outer, kept, flat,
):
    frame_count, tiles, row_count, _ = kept.shape
    near = taps_ref.shape[1]
    steps_1 = row_count // row_step
    steps_2 = frame_count // frame_step
    at = pl.program_id(0)

    def filtered(block):
        part = block.reshape(near * 8, block.shape[2])
        both = jnp.dot(w1[...], part, preferred_element_type=f32)
        both = both.reshape(frame_count, 2, 8, block.shape[2])
        return both[:, 0] + both[:, 1]

    def keep(above, below, tile, place):
        value = jnp.concatenate([above, below], axis=1)
        high = value.astype(bf16)
        chi[:, tile, place, :] = high
        clo[:, tile, place, :] = (value - high.astype(f32)).astype(bf16)

    @pl.when(at == 0)
    def _():
        count = 2 * frame_count
        tall = (iota((8 * count, count), 0) // 8 == iota((8 * count, count), 1)).astype(bf16)
        wide = (iota((near, 8 * near), 1) // 8 == iota((near, 8 * near), 0)).astype(bf16)
        full = jnp.dot(tall, taps_ref[...], preferred_element_type=f32).astype(bf16)
        full = jnp.dot(full, wide, preferred_element_type=f32)
        same = iota(full.shape, 0) % 8 == iota(full.shape, 1) % 8
        w1[...] = jnp.where(same, full, 0.0).astype(bf16)
        for tile in range(0, tiles + 1, GROUP):
            pair = range(tile, min(tile + GROUP, tiles + 1))
            cols = slice(tile * TILE, (tile + len(pair)) * TILE)
            below = below_ref[0, :, :, cols].astype(f32)
            above = above_ref[0, :, :, cols].astype(f32)
            gap = jnp.zeros((near, 8 - 2 * REACH, below.shape[2]), f32)
            both = filtered(jnp.concatenate([below, gap, above], axis=1).astype(bf16))
            for q, one in enumerate(pair):
                carry[:, one] = both[..., q * TILE : (q + 1) * TILE]
                outer[:, one] = both[..., q * TILE : (q + 1) * TILE]

    @pl.when(at < steps_1)
    def _():
        def keep_all(tile, parts):
            parts = [carry[:, tile]] + parts
            for q in range(0, len(parts) - 1, 2):
                place = pl.ds(pl.multiple_of(at * row_step + EDGE * q, BLOCK), BLOCK)
                keep(parts[q], parts[q + 1], tile, place)
            carry[:, tile] = parts[-1]

        for tile in range(0, tiles, 2):
            group = range(tile, min(tile + 2, tiles))
            cols = slice(tile * TILE, (tile + len(group)) * TILE)
            parts = []
            for h in range(0, row_step, EDGE):
                rows = slice(h, h + EDGE)
                block = jnp.concatenate(
                    [low_ref[:, rows, cols], own_ref[0, :, rows, cols], high_ref[:, rows, cols]],
                    axis=0,
                )
                parts.append(filtered(block))
            for q, one in enumerate(group):
                keep_all(one, [part[..., q * TILE : (q + 1) * TILE] for part in parts])
        both = filtered(
            jnp.concatenate(
                [edge_ref[0, :, h : h + EDGE] for h in range(0, row_step, EDGE)], axis=2
            )
        )
        parts = [both[..., h * TILE : (h + 1) * TILE] for h in range(row_step // EDGE)]
        keep_all(tiles, parts)

    @pl.when(at == steps_1 - 1)
    def _():
        for tile in range(tiles + 1):
            keep(carry[:, tile], outer[:, tile], tile, slice(row_count, row_count + BLOCK))

    @pl.when((at >= steps_1) & (at < steps_1 + steps_2))
    def _():
        lane = iota((BLOCK, TILE), 1)
        edge_of = [lane < 2, lane < 1, None, lane >= TILE - 1, lane >= TILE - 2]

        depth = WINDOW + 2 * EDGE
        parts_of = range(WINDOW // BLOCK)

        def two_frames(k2, unused):
            for row in range(0, row_count, WINDOW):
                turned = {}
                done = [0, 0]

                def finish(f, tile):
                    k = k2 * 2 + f
                    frame = (at - steps_1) * frame_step + k
                    for m in parts_of:
                        total = turned[f, m, REACH, tile]
                        for b in range(SIDE):
                            if b != REACH:
                                beside = (tile + (1 if b > REACH else -1)) % (tiles + 1)
                                total = total + jnp.where(
                                    edge_of[b], turned[f, m, b, beside], turned[f, m, b, tile]
                                )
                        value = total.astype(bf16)
                        rows = slice(row + m * BLOCK, row + (m + 1) * BLOCK)
                        out_ref[0, k, rows, tile * TILE : (tile + 1) * TILE] = value
                        kept[frame, tile, rows, :] = value.astype(f32)

                order = [(f, tile) for f in range(2) for tile in [tiles] + list(range(tiles))]
                for p in range(0, len(order), GROUP):
                    pair = order[p : p + GROUP]
                    stacks = []
                    for f, tile in pair:
                        frame = (at - steps_1) * frame_step + k2 * 2 + f
                        high = chi[frame, tile, row : row + depth, :]
                        low = clo[frame, tile, row : row + depth, :]
                        stacks.append(jnp.concatenate([high, low, high], axis=0))
                    both = jnp.dot(
                        w2_ref[...], jnp.concatenate(stacks, axis=1), preferred_element_type=f32
                    )
                    for q, (f, tile) in enumerate(pair):
                        for m in parts_of:
                            for b in range(SIDE):
                                at_row = (m * SIDE + b) * BLOCK
                                part = both[at_row : at_row + BLOCK, q * TILE : (q + 1) * TILE]
                                if b != REACH:
                                    part = pltpu.roll(part, (REACH - b) % TILE, 1)
                                turned[f, m, b, tile] = part
                    for f in range(2):
                        while done[f] < tiles and (f, 0, 0, done[f]) in turned:
                            after = min(done[f] + 1, tiles)
                            if (f, 0, 0, after) not in turned:
                                break
                            finish(f, done[f])
                            done[f] += 1
            return unused

        lax.fori_loop(0, frame_step // 2, two_frames, 0)

    @pl.when(at == steps_1 + steps_2)
    def _():
        slot_count = flat.shape[0]
        lane = iota((PATCH, TILE), 1)
        low_bits = PATCH - 1
        bits = low_bits.bit_length()
        size = PATCH * PATCH
        repeat = (iota((TILE, size), 1) & low_bits == iota((TILE, size), 0)).astype(bf16)
        mine = iota((size, size), 1) >> bits == iota((size, size), 0) & low_bits
        owner = (iota((PATCH, size), 1) >> bits == iota((PATCH, size), 0)).astype(bf16)

        def some(i16, unused):
            parts = []
            for j in range(PATCH):
                i = i16 * PATCH + j
                frame, row, tile = spots_ref[0, i], spots_ref[1, i], spots_ref[2, i]
                beside, offset = spots_ref[3, i], spots_ref[4, i]
                here = kept[frame, tile, pl.ds(row, PATCH), :]
                there = kept[frame, beside, pl.ds(row, PATCH), :]
                part = jnp.where(lane >= offset, here, there)
                parts.append(pltpu.roll(part, (TILE - offset) & (TILE - 1), 1))
            rows = jnp.concatenate(parts, axis=0).astype(bf16)
            rows = jnp.dot(rows, repeat, preferred_element_type=f32)
            rows = jnp.where(mine, rows, 0.0).astype(bf16)
            place = pl.ds(pl.multiple_of(i16 * PATCH, PATCH), PATCH)
            flat[place, :] = jnp.dot(owner, rows, preferred_element_type=f32)
            return unused

        lax.fori_loop(0, slot_count // PATCH, some, 0)
        values = flat[...]
        mean = jnp.sum(values, axis=1, keepdims=True) / (PATCH * PATCH)
        centered = values - mean
        spread = jnp.sum(centered * centered, axis=1, keepdims=True) / (PATCH * PATCH)
        normed = centered / jnp.sqrt(spread + 1e-05)
        live = iota((slot_count, 1), 0) < spots_ref[5, 0]
        last_ref[...] = jnp.where(live, normed, 0.0).astype(bf16)


def edges_of(top, bottom, left, right):
    rows = jnp.concatenate(
        [top[...].astype(f32)[:, :REACH], bottom[...].astype(f32)[:, BLOCK - REACH :]], axis=1
    )
    line = iota((8, 2 * TILE), 0)
    lane = iota((8, 2 * TILE), 1)
    first = (line == lane) & (line < REACH)
    last = (line + 2 * TILE - 2 * REACH == lane) & (line >= REACH)
    chosen = (first | last).astype(bf16)
    row_count = left.shape[1]
    cols = []
    for f in range(0, rows.shape[0], 2):
        both = jnp.concatenate([left[f : f + 2], right[f : f + 2]], axis=2)
        both = both.reshape(2 * row_count, 2 * TILE)
        one = lax.dot_general(
            chosen, both, (((1,), (1,)), ((), ())), preferred_element_type=f32
        )
        one = one[: 2 * REACH].astype(bf16)
        cols += [one[:, :row_count], one[:, row_count:]]
    return rows.astype(bf16), cols


def send_all(frames, slab, low, high, whole, sems):
    frame_count = whole.shape[0]
    half = (HALF + 1) // 2
    spans = []
    for target, base in ((high, 0), (low, frame_count - HALF)):
        for start, count in ((0, half), (half, HALF - half)):
            spans.append((target, base + start, start, count))
    fetches, writes = [], []
    for i, (target, source, start, count) in enumerate(spans):
        here = whole.at[pl.ds(source, count)]
        fetches.append(
            pltpu.make_async_copy(frames.at[slab, pl.ds(source, count)], here, sems.at[2 * i])
        )
        writes.append(
            pltpu.make_async_copy(here, target.at[pl.ds(start, count)], sems.at[2 * i + 1])
        )
    return fetches, writes


def cut_kernel(frames, rim, rim_low, rim_high, low, high, whole, top, bottom, left, right, sems):
    frame_count, row_count, col_count = whole.shape
    reads = [
        pltpu.make_async_copy(source, target, sems.at[8 + i])
        for i, (source, target) in enumerate(
            [
                (frames.at[0, :, pl.ds(0, BLOCK), :], top),
                (frames.at[0, :, pl.ds(row_count - BLOCK, BLOCK), :], bottom),
                (frames.at[0, :, :, pl.ds(0, TILE)], left),
                (frames.at[0, :, :, pl.ds(col_count - TILE, TILE)], right),
                (frames.at[1, pl.ds(HALF, frame_count - 2 * HALF)],
                 whole.at[pl.ds(HALF, frame_count - 2 * HALF)]),
            ]
        )
    ]
    fetches, writes = send_all(frames, 1, low, high, whole, sems)
    for copy in reads + fetches:
        copy.start()

    def put(slab, rows, cols):
        middle = frame_count - HALF
        for target, start in [(rim, 0), (rim_low, middle), (rim_high, 0)]:
            count = target.shape[1]
            target[slab, :, :, :col_count] = rows[start : start + count]
            for f in range(count):
                target[slab, f, :, col_count:] = cols[start + f]

    for copy in reads:
        copy.wait()
    put(0, *edges_of(top, bottom, left, right))
    for fetch, write in zip(fetches, writes):
        fetch.wait()
        write.start()
    put(
        1,
        *edges_of(
            whole.at[:, pl.ds(0, BLOCK), :],
            whole.at[:, pl.ds(row_count - BLOCK, BLOCK), :],
            whole.at[:, :, pl.ds(0, TILE)],
            whole.at[:, :, pl.ds(col_count - TILE, TILE)],
        ),
    )
    for write in writes:
        write.wait()


def late_kernel(frames, low, high, whole, sems):
    fetches, writes = send_all(frames, 0, low, high, whole, sems)
    for fetch in fetches:
        fetch.start()
    for fetch, write in zip(fetches, writes):
        fetch.wait()
        write.start()
    for write in writes:
        write.wait()


def cut(frames):
    slabs, frame_count, row_count, col_count = frames.shape
    anywhere = pl.BlockSpec(memory_space=pl.ANY)
    near = pl.BlockSpec(memory_space=pltpu.VMEM)
    piece = jax.ShapeDtypeStruct((HALF, row_count, col_count), bf16)
    wide = col_count + row_count
    rims = [
        jax.ShapeDtypeStruct((slabs, count, 2 * REACH, wide), bf16)
        for count in (frame_count, HALF, HALF)
    ]
    return pl.pallas_call(
        cut_kernel,
        in_specs=[anywhere],
        out_specs=[near] * 3 + [anywhere] * 2,
        out_shape=rims + [piece, piece],
        scratch_shapes=[
            pltpu.VMEM((frame_count, row_count, col_count), bf16),
            pltpu.VMEM((frame_count, BLOCK, col_count), bf16),
            pltpu.VMEM((frame_count, BLOCK, col_count), bf16),
            pltpu.VMEM((frame_count, row_count, TILE), bf16),
            pltpu.VMEM((frame_count, row_count, TILE), bf16),
            pltpu.SemaphoreType.DMA((13,)),
        ],
        compiler_params=pltpu.CompilerParams(vmem_limit_bytes=60 * 1024 * 1024),
        name="cut",
    )(frames)


def late_cut(frames):
    _, frame_count, row_count, col_count = frames.shape
    anywhere = pl.BlockSpec(memory_space=pl.ANY)
    piece = jax.ShapeDtypeStruct((HALF, row_count, col_count), bf16)
    return pl.pallas_call(
        late_kernel,
        in_specs=[anywhere],
        out_specs=[anywhere] * 2,
        out_shape=[piece, piece],
        scratch_shapes=[
            pltpu.VMEM((frame_count, row_count, col_count), bf16),
            pltpu.SemaphoreType.DMA((8,)),
        ],
        compiler_params=pltpu.CompilerParams(vmem_limit_bytes=60 * 1024 * 1024),
        cost_estimate=pl.CostEstimate(flops=0, bytes_accessed=9_000_000, transcendentals=0),
        name="late_cut",
    )(frames)


def run_slab(slab, smoothed, spots, taps, w2, low, frames, high, edge, below, above):
    _, frame_count, row_count, col_count = frames.shape
    slot_count = spots.shape[1]
    row_step, frame_step = 32, 8
    steps_1 = row_count // row_step
    steps_2 = frame_count // frame_step
    wide = col_count + TILE
    near = frame_count + 2 * HALF

    def row_block(at):
        return jnp.minimum(at, steps_1 - 1)

    def whole(array):
        return pl.BlockSpec(array.shape, lambda at: (0,) * array.ndim)

    operands = [spots, taps, w2, low, frames, high, edge, below, above]
    in_specs = [
        pl.BlockSpec(memory_space=pltpu.SMEM),
        whole(taps),
        whole(w2),
        pl.BlockSpec((HALF, row_step, col_count), lambda at: (0, row_block(at), 0)),
        pl.BlockSpec((1, frame_count, row_step, col_count), lambda at: (slab, 0, row_block(at), 0)),
        pl.BlockSpec((HALF, row_step, col_count), lambda at: (0, row_block(at), 0)),
        pl.BlockSpec((1, near, row_step, TILE), lambda at: (slab, 0, row_block(at), 0)),
        pl.BlockSpec((1, near, REACH, wide), lambda at: (slab, 0, 0, 0)),
        pl.BlockSpec((1, near, REACH, wide), lambda at: (slab, 0, 0, 0)),
    ]
    aliases = {}
    if smoothed is not None:
        operands.append(smoothed)
        in_specs.append(pl.BlockSpec(memory_space=pl.ANY))
        aliases = {len(operands) - 1: 0}
    count = len(operands)

    def body(*refs):
        slab_kernel(row_step, frame_step, *refs[:9], *refs[count:])

    tall = row_count + 2 * EDGE
    return pl.pallas_call(
        body,
        grid=(steps_1 + steps_2 + 1,),
        in_specs=in_specs,
        out_specs=[
            pl.BlockSpec(
                (1, frame_step, row_count, col_count),
                lambda at: (slab, jnp.clip(at - steps_1, 0, steps_2 - 1), 0, 0),
            ),
            pl.BlockSpec((slot_count, PATCH * PATCH), lambda at: (0, 0)),
        ],
        out_shape=[
            jax.ShapeDtypeStruct(frames.shape, bf16),
            jax.ShapeDtypeStruct((slot_count, PATCH * PATCH), bf16),
        ],
        scratch_shapes=[
            pltpu.VMEM((16 * frame_count, 8 * near), bf16),
            pltpu.VMEM((frame_count, wide // TILE, tall, TILE), bf16),
            pltpu.VMEM((frame_count, wide // TILE, tall, TILE), bf16),
            pltpu.VMEM((frame_count, wide // TILE, EDGE, TILE), f32),
            pltpu.VMEM((frame_count, wide // TILE, EDGE, TILE), f32),
            pltpu.VMEM((frame_count, col_count // TILE, row_count, TILE), f32),
            pltpu.VMEM((slot_count, PATCH * PATCH), f32),
        ],
        input_output_aliases=aliases,
        compiler_params=pltpu.CompilerParams(vmem_limit_bytes=40 * 1024 * 1024),
        cost_estimate=pl.CostEstimate(
            flops=20_000_000_000, bytes_accessed=16_000_000, transcendentals=0
        ),
        name=f"slab_{slab}",
    )(*operands)


def shards(frames, omega_taps, smooth_kernel, spots, counts):
    _, frame_count, row_count, col_count = frames.shape
    first_frame = lax.axis_index("omega") * frame_count
    first_row = lax.axis_index("row") * row_count
    first_col = lax.axis_index("col") * col_count

    rim, rim_low, rim_high, send_low1, send_high1 = cut(frames)
    rim = jnp.concatenate(
        [shifted(rim_low, "omega", 1), rim, shifted(rim_high, "omega", -1)], axis=1
    )
    low1 = shifted(send_low1, "omega", 1)
    high1 = shifted(send_high1, "omega", -1)
    lane = jnp.arange(TILE, dtype=jnp.int32)[None, :]
    step = jnp.arange(REACH, dtype=jnp.int32)[:, None]
    after = (lane == step).astype(bf16)
    before = (lane == TILE - REACH + step).astype(bf16)
    if lax.axis_size("col") == 2:
        first = lax.axis_index("col") == 0
        sides = jnp.where(first, rim[:, :, REACH:, col_count:], rim[:, :, :REACH, col_count:])
        sides = lax.ppermute(sides, "col", [(0, 1), (1, 0)])
        place = jnp.where(first, after, before)
    else:
        left = shifted(rim[:, :, REACH:, col_count:], "col", 1)
        right = shifted(rim[:, :, :REACH, col_count:], "col", -1)
        sides = jnp.concatenate([right, left], axis=2)
        place = jnp.concatenate([after, before], axis=0)
    later, sides = lax.optimization_barrier((frames, sides))
    send_low0, send_high0 = late_cut(later)
    low0 = shifted(send_low0, "omega", 1)
    high0 = shifted(send_high0, "omega", -1)
    edge = jnp.einsum("sfkr,kc->sfrc", sides, place, preferred_element_type=bf16)
    ends = jnp.concatenate([edge[:, :, :REACH], edge[:, :, -REACH:]], axis=2)
    line = jnp.concatenate([rim[..., :col_count], ends], axis=3)
    above = shifted(line[:, :, REACH:], "row", 1)
    below = shifted(line[:, :, :REACH], "row", -1)

    taps = omega_matrix(
        omega_taps, first_frame, frame_count, frame_count * lax.axis_size("omega")
    )
    w2 = smooth_matrix(smooth_kernel)
    frame, row, col = spots[:, 0] - first_frame, spots[:, 1] - first_row, spots[:, 2] - first_col
    tile = col // TILE
    beside = jnp.minimum(tile + 1, col_count // TILE - 1)
    live = jnp.broadcast_to(counts, frame.shape)
    local = jnp.stack([frame, row, tile, beside, col % TILE, live], axis=1)

    smoothed, second = run_slab(1, None, local[1], taps, w2, low1, frames, high1, edge, below, above)
    count = lax.axis_size("row") * lax.axis_size("col")
    second = lax.ppermute(second, ("row", "col"), [(i, count - 1 - i) for i in range(count)])
    smoothed, first = run_slab(0, smoothed, local[0], taps, w2, low0, frames, high0, edge, below, above)
    scores = (
        lax.dot_general(first, second, (((1,), (1,)), ((), ())), preferred_element_type=f32)
        / float(PATCH * PATCH)
    )
    return (smoothed, scores)


def solution(mesh):
    return jax.shard_map(
        shards,
        mesh=mesh,
        in_specs=(
            P(None, "omega", "row", "col"),
            P(),
            P(),
            P(None, None, ("omega", "row", "col")),
            P(None, ("omega", "row", "col")),
        ),
        out_specs=(P(None, "omega", "row", "col"), P(("omega", "row", "col"), None)),
        check_vma=False,
    )
```

```python
import jax
import jax.numpy as jnp
from jax import lax
from jax.experimental import pallas as pl
from jax.experimental.pallas import tpu as pltpu
from jax.sharding import PartitionSpec as P

TAPS = 15
HALF = TAPS // 2
PATCH = 16
SIDE = 5
REACH = SIDE // 2
TILE = 128
BLOCK = 16
WINDOW = 32
EDGE = 8
GROUP = 4
bf16 = jnp.bfloat16
f32 = jnp.float32


def shifted(block, axis, step):
    count = lax.axis_size(axis)
    route = [(i, i + step) for i in range(count) if 0 <= i + step < count]
    return lax.ppermute(block, axis, route)


def split(values):
    high = lax.reduce_precision(values, 8, 7)
    return high.astype(bf16), (values - high).astype(bf16)


def omega_matrix(omega_taps, first_frame, frame_count, frame_total):
    out_ids = jnp.arange(frame_count, dtype=jnp.int32)[:, None]
    in_ids = jnp.arange(frame_count + 2 * HALF, dtype=jnp.int32)[None, :]
    source = first_frame + in_ids - HALF
    valid = (source >= 0) & (source < frame_total)
    tap = jnp.where(valid, in_ids - out_ids, -1)
    hit = tap[:, :, None] == jnp.arange(TAPS, dtype=jnp.int32)
    weights = jnp.sum(jnp.where(hit, omega_taps, 0.0), axis=2)
    norm = jnp.sum(weights, axis=1, keepdims=True)
    center = (in_ids - out_ids == HALF).astype(f32)
    matrix = center - weights / norm
    return jnp.stack(split(matrix), axis=1).reshape(2 * frame_count, matrix.shape[1])


def smooth_matrix(smooth_kernel):
    depth = WINDOW + 2 * EDGE
    parts = WINDOW // BLOCK
    out_ids = jnp.arange(WINDOW, dtype=jnp.int32).reshape(parts, 1, BLOCK, 1)
    in_ids = jnp.arange(depth, dtype=jnp.int32)
    step = in_ids - out_ids - (EDGE - REACH)
    hit = step[..., None] == jnp.arange(SIDE, dtype=jnp.int32)
    table = jnp.sum(jnp.where(hit, smooth_kernel.T[None, :, None, None, :], 0.0), axis=4)
    high, low = split(table)
    return jnp.concatenate([high, high, low], axis=3).reshape(SIDE * WINDOW, 3 * depth)


def iota(shape, dim):
    return lax.broadcasted_iota(jnp.int32, shape, dim)


def slab_kernel(
    row_step, frame_step,
    spots_ref, taps_ref, w2_ref, low_ref, own_ref, high_ref, edge_ref, below_ref, above_ref,
    out_ref, last_ref, w1, chi, clo, carry, outer, kept, flat,
):
    frame_count, tiles, row_count, _ = kept.shape
    near = taps_ref.shape[1]
    steps_1 = row_count // row_step
    steps_2 = frame_count // frame_step
    at = pl.program_id(0)

    def filtered(block):
        part = block.reshape(near * 8, block.shape[2])
        both = jnp.dot(w1[...], part, preferred_element_type=f32)
        both = both.reshape(frame_count, 2, 8, block.shape[2])
        return both[:, 0] + both[:, 1]

    def keep(above, below, tile, place):
        value = jnp.concatenate([above, below], axis=1)
        high = value.astype(bf16)
        chi[:, tile, place, :] = high
        clo[:, tile, place, :] = (value - high.astype(f32)).astype(bf16)

    @pl.when(at == 0)
    def _():
        count = 2 * frame_count
        tall = (iota((8 * count, count), 0) // 8 == iota((8 * count, count), 1)).astype(bf16)
        wide = (iota((near, 8 * near), 1) // 8 == iota((near, 8 * near), 0)).astype(bf16)
        full = jnp.dot(tall, taps_ref[...], preferred_element_type=f32).astype(bf16)
        full = jnp.dot(full, wide, preferred_element_type=f32)
        same = iota(full.shape, 0) % 8 == iota(full.shape, 1) % 8
        w1[...] = jnp.where(same, full, 0.0).astype(bf16)
        for tile in range(0, tiles + 1, GROUP):
            pair = range(tile, min(tile + GROUP, tiles + 1))
            cols = slice(tile * TILE, (tile + len(pair)) * TILE)
            below = below_ref[0, :, :, cols].astype(f32)
            above = above_ref[0, :, :, cols].astype(f32)
            gap = jnp.zeros((near, 8 - 2 * REACH, below.shape[2]), f32)
            both = filtered(jnp.concatenate([below, gap, above], axis=1).astype(bf16))
            for q, one in enumerate(pair):
                carry[:, one] = both[..., q * TILE : (q + 1) * TILE]
                outer[:, one] = both[..., q * TILE : (q + 1) * TILE]

    @pl.when(at < steps_1)
    def _():
        def keep_all(tile, parts):
            parts = [carry[:, tile]] + parts
            for q in range(0, len(parts) - 1, 2):
                place = pl.ds(pl.multiple_of(at * row_step + EDGE * q, BLOCK), BLOCK)
                keep(parts[q], parts[q + 1], tile, place)
            carry[:, tile] = parts[-1]

        for tile in range(0, tiles, 2):
            group = range(tile, min(tile + 2, tiles))
            cols = slice(tile * TILE, (tile + len(group)) * TILE)
            parts = []
            for h in range(0, row_step, EDGE):
                rows = slice(h, h + EDGE)
                block = jnp.concatenate(
                    [low_ref[:, rows, cols], own_ref[0, :, rows, cols], high_ref[:, rows, cols]],
                    axis=0,
                )
                parts.append(filtered(block))
            for q, one in enumerate(group):
                keep_all(one, [part[..., q * TILE : (q + 1) * TILE] for part in parts])
        both = filtered(
            jnp.concatenate(
                [edge_ref[0, :, h : h + EDGE] for h in range(0, row_step, EDGE)], axis=2
            )
        )
        parts = [both[..., h * TILE : (h + 1) * TILE] for h in range(row_step // EDGE)]
        keep_all(tiles, parts)

    @pl.when(at == steps_1 - 1)
    def _():
        for tile in range(tiles + 1):
            keep(carry[:, tile], outer[:, tile], tile, slice(row_count, row_count + BLOCK))

    @pl.when((at >= steps_1) & (at < steps_1 + steps_2))
    def _():
        lane = iota((BLOCK, TILE), 1)
        edge_of = [lane < 2, lane < 1, None, lane >= TILE - 1, lane >= TILE - 2]

        depth = WINDOW + 2 * EDGE
        parts_of = range(WINDOW // BLOCK)

        def two_frames(k2, unused):
            for row in range(0, row_count, WINDOW):
                turned = {}
                done = [0, 0]

                def finish(f, tile):
                    k = k2 * 2 + f
                    frame = (at - steps_1) * frame_step + k
                    for m in parts_of:
                        total = turned[f, m, REACH, tile]
                        for b in range(SIDE):
                            if b != REACH:
                                beside = (tile + (1 if b > REACH else -1)) % (tiles + 1)
                                total = total + jnp.where(
                                    edge_of[b], turned[f, m, b, beside], turned[f, m, b, tile]
                                )
                        value = total.astype(bf16)
                        rows = slice(row + m * BLOCK, row + (m + 1) * BLOCK)
                        out_ref[0, k, rows, tile * TILE : (tile + 1) * TILE] = value
                        kept[frame, tile, rows, :] = value.astype(f32)

                order = [(f, tile) for f in range(2) for tile in [tiles] + list(range(tiles))]
                for p in range(0, len(order), GROUP):
                    pair = order[p : p + GROUP]
                    stacks = []
                    for f, tile in pair:
                        frame = (at - steps_1) * frame_step + k2 * 2 + f
                        high = chi[frame, tile, row : row + depth, :]
                        low = clo[frame, tile, row : row + depth, :]
                        stacks.append(jnp.concatenate([high, low, high], axis=0))
                    both = jnp.dot(
                        w2_ref[...], jnp.concatenate(stacks, axis=1), preferred_element_type=f32
                    )
                    for q, (f, tile) in enumerate(pair):
                        for m in parts_of:
                            for b in range(SIDE):
                                at_row = (m * SIDE + b) * BLOCK
                                part = both[at_row : at_row + BLOCK, q * TILE : (q + 1) * TILE]
                                if b != REACH:
                                    part = pltpu.roll(part, (REACH - b) % TILE, 1)
                                turned[f, m, b, tile] = part
                    for f in range(2):
                        while done[f] < tiles and (f, 0, 0, done[f]) in turned:
                            after = min(done[f] + 1, tiles)
                            if (f, 0, 0, after) not in turned:
                                break
                            finish(f, done[f])
                            done[f] += 1
            return unused

        lax.fori_loop(0, frame_step // 2, two_frames, 0)

    @pl.when(at == steps_1 + steps_2)
    def _():
        slot_count = flat.shape[0] // PATCH

        lane = iota((PATCH, TILE), 1)

        def some(i8, unused):
            for j in range(16):
                i = i8 * 16 + j
                frame, row, tile = spots_ref[0, i], spots_ref[1, i], spots_ref[2, i]
                beside, offset = spots_ref[3, i], spots_ref[4, i]
                here = kept[frame, tile, pl.ds(row, PATCH), :]
                there = kept[frame, beside, pl.ds(row, PATCH), :]
                part = jnp.where(lane >= offset, here, there)
                part = pltpu.roll(part, (TILE - offset) & (TILE - 1), 1)
                flat[pl.ds(pl.multiple_of(i * PATCH, PATCH), PATCH), :] = part.astype(bf16)
            return unused

        lax.fori_loop(0, slot_count // 16, some, 0)
        low_bits = PATCH - 1
        bits = low_bits.bit_length()
        shape = (TILE, PATCH * PATCH)
        repeat = (iota(shape, 1) & low_bits == iota(shape, 0)).astype(bf16)
        rows = jnp.dot(flat[...], repeat, preferred_element_type=f32)
        mine = iota(rows.shape, 1) >> bits == iota(rows.shape, 0) & low_bits
        rows = jnp.where(mine, rows, 0.0).astype(bf16)
        shape = (slot_count, rows.shape[0])
        owner = (iota(shape, 1) >> bits == iota(shape, 0)).astype(bf16)
        values = jnp.dot(owner, rows, preferred_element_type=f32)
        mean = jnp.sum(values, axis=1, keepdims=True) / (PATCH * PATCH)
        centered = values - mean
        spread = jnp.sum(centered * centered, axis=1, keepdims=True) / (PATCH * PATCH)
        normed = centered / jnp.sqrt(spread + 1e-05)
        live = iota((slot_count, 1), 0) < spots_ref[5, 0]
        last_ref[...] = jnp.where(live, normed, 0.0).astype(bf16)


def edges_of(top, bottom, left, right):
    rows = jnp.concatenate(
        [top[...].astype(f32)[:, :REACH], bottom[...].astype(f32)[:, BLOCK - REACH :]], axis=1
    )
    line = iota((8, 2 * TILE), 0)
    lane = iota((8, 2 * TILE), 1)
    first = (line == lane) & (line < REACH)
    last = (line + 2 * TILE - 2 * REACH == lane) & (line >= REACH)
    chosen = (first | last).astype(bf16)
    row_count = left.shape[1]
    cols = []
    for f in range(0, rows.shape[0], 2):
        both = jnp.concatenate([left[f : f + 2], right[f : f + 2]], axis=2)
        both = both.reshape(2 * row_count, 2 * TILE)
        one = lax.dot_general(
            chosen, both, (((1,), (1,)), ((), ())), preferred_element_type=f32
        )
        one = one[: 2 * REACH].astype(bf16)
        cols += [one[:, :row_count], one[:, row_count:]]
    return rows.astype(bf16), cols


def send_all(frames, slab, low, high, whole, sems):
    frame_count = whole.shape[0]
    half = (HALF + 1) // 2
    spans = []
    for target, base in ((high, 0), (low, frame_count - HALF)):
        for start, count in ((0, half), (half, HALF - half)):
            spans.append((target, base + start, start, count))
    fetches, writes = [], []
    for i, (target, source, start, count) in enumerate(spans):
        here = whole.at[pl.ds(source, count)]
        fetches.append(
            pltpu.make_async_copy(frames.at[slab, pl.ds(source, count)], here, sems.at[2 * i])
        )
        writes.append(
            pltpu.make_async_copy(here, target.at[pl.ds(start, count)], sems.at[2 * i + 1])
        )
    return fetches, writes


def cut_kernel(frames, rim, rim_low, rim_high, low, high, whole, top, bottom, left, right, sems):
    frame_count, row_count, col_count = whole.shape
    reads = [
        pltpu.make_async_copy(source, target, sems.at[8 + i])
        for i, (source, target) in enumerate(
            [
                (frames.at[0, :, pl.ds(0, BLOCK), :], top),
                (frames.at[0, :, pl.ds(row_count - BLOCK, BLOCK), :], bottom),
                (frames.at[0, :, :, pl.ds(0, TILE)], left),
                (frames.at[0, :, :, pl.ds(col_count - TILE, TILE)], right),
                (frames.at[1, pl.ds(HALF, frame_count - 2 * HALF)],
                 whole.at[pl.ds(HALF, frame_count - 2 * HALF)]),
            ]
        )
    ]
    fetches, writes = send_all(frames, 1, low, high, whole, sems)
    for copy in reads + fetches:
        copy.start()

    def put(slab, rows, cols):
        middle = frame_count - HALF
        for target, start in [(rim, 0), (rim_low, middle), (rim_high, 0)]:
            count = target.shape[1]
            target[slab, :, :, :col_count] = rows[start : start + count]
            for f in range(count):
                target[slab, f, :, col_count:] = cols[start + f]

    for copy in reads:
        copy.wait()
    put(0, *edges_of(top, bottom, left, right))
    for fetch, write in zip(fetches, writes):
        fetch.wait()
        write.start()
    put(
        1,
        *edges_of(
            whole.at[:, pl.ds(0, BLOCK), :],
            whole.at[:, pl.ds(row_count - BLOCK, BLOCK), :],
            whole.at[:, :, pl.ds(0, TILE)],
            whole.at[:, :, pl.ds(col_count - TILE, TILE)],
        ),
    )
    for write in writes:
        write.wait()


def late_kernel(frames, low, high, whole, sems):
    fetches, writes = send_all(frames, 0, low, high, whole, sems)
    for fetch in fetches:
        fetch.start()
    for fetch, write in zip(fetches, writes):
        fetch.wait()
        write.start()
    for write in writes:
        write.wait()


def cut(frames):
    slabs, frame_count, row_count, col_count = frames.shape
    anywhere = pl.BlockSpec(memory_space=pl.ANY)
    near = pl.BlockSpec(memory_space=pltpu.VMEM)
    piece = jax.ShapeDtypeStruct((HALF, row_count, col_count), bf16)
    wide = col_count + row_count
    rims = [
        jax.ShapeDtypeStruct((slabs, count, 2 * REACH, wide), bf16)
        for count in (frame_count, HALF, HALF)
    ]
    return pl.pallas_call(
        cut_kernel,
        in_specs=[anywhere],
        out_specs=[near] * 3 + [anywhere] * 2,
        out_shape=rims + [piece, piece],
        scratch_shapes=[
            pltpu.VMEM((frame_count, row_count, col_count), bf16),
            pltpu.VMEM((frame_count, BLOCK, col_count), bf16),
            pltpu.VMEM((frame_count, BLOCK, col_count), bf16),
            pltpu.VMEM((frame_count, row_count, TILE), bf16),
            pltpu.VMEM((frame_count, row_count, TILE), bf16),
            pltpu.SemaphoreType.DMA((13,)),
        ],
        compiler_params=pltpu.CompilerParams(vmem_limit_bytes=60 * 1024 * 1024),
        name="cut",
    )(frames)


def late_cut(frames):
    _, frame_count, row_count, col_count = frames.shape
    anywhere = pl.BlockSpec(memory_space=pl.ANY)
    piece = jax.ShapeDtypeStruct((HALF, row_count, col_count), bf16)
    return pl.pallas_call(
        late_kernel,
        in_specs=[anywhere],
        out_specs=[anywhere] * 2,
        out_shape=[piece, piece],
        scratch_shapes=[
            pltpu.VMEM((frame_count, row_count, col_count), bf16),
            pltpu.SemaphoreType.DMA((8,)),
        ],
        compiler_params=pltpu.CompilerParams(vmem_limit_bytes=60 * 1024 * 1024),
        cost_estimate=pl.CostEstimate(flops=0, bytes_accessed=9_000_000, transcendentals=0),
        name="late_cut",
    )(frames)


def run_slab(slab, smoothed, spots, taps, w2, low, frames, high, edge, below, above):
    _, frame_count, row_count, col_count = frames.shape
    slot_count = spots.shape[1]
    row_step, frame_step = 64, 8
    steps_1 = row_count // row_step
    steps_2 = frame_count // frame_step
    wide = col_count + TILE
    near = frame_count + 2 * HALF

    def row_block(at):
        return jnp.minimum(at, steps_1 - 1)

    def whole(array):
        return pl.BlockSpec(array.shape, lambda at: (0,) * array.ndim)

    operands = [spots, taps, w2, low, frames, high, edge, below, above]
    in_specs = [
        pl.BlockSpec(memory_space=pltpu.SMEM),
        whole(taps),
        whole(w2),
        pl.BlockSpec((HALF, row_step, col_count), lambda at: (0, row_block(at), 0)),
        pl.BlockSpec((1, frame_count, row_step, col_count), lambda at: (slab, 0, row_block(at), 0)),
        pl.BlockSpec((HALF, row_step, col_count), lambda at: (0, row_block(at), 0)),
        pl.BlockSpec((1, near, row_step, TILE), lambda at: (slab, 0, row_block(at), 0)),
        pl.BlockSpec((1, near, REACH, wide), lambda at: (slab, 0, 0, 0)),
        pl.BlockSpec((1, near, REACH, wide), lambda at: (slab, 0, 0, 0)),
    ]
    aliases = {}
    if smoothed is not None:
        operands.append(smoothed)
        in_specs.append(pl.BlockSpec(memory_space=pl.ANY))
        aliases = {len(operands) - 1: 0}
    count = len(operands)

    def body(*refs):
        slab_kernel(row_step, frame_step, *refs[:9], *refs[count:])

    tall = row_count + 2 * EDGE
    return pl.pallas_call(
        body,
        grid=(steps_1 + steps_2 + 1,),
        in_specs=in_specs,
        out_specs=[
            pl.BlockSpec(
                (1, frame_step, row_count, col_count),
                lambda at: (slab, jnp.clip(at - steps_1, 0, steps_2 - 1), 0, 0),
            ),
            pl.BlockSpec((slot_count, PATCH * PATCH), lambda at: (0, 0)),
        ],
        out_shape=[
            jax.ShapeDtypeStruct(frames.shape, bf16),
            jax.ShapeDtypeStruct((slot_count, PATCH * PATCH), bf16),
        ],
        scratch_shapes=[
            pltpu.VMEM((16 * frame_count, 8 * near), bf16),
            pltpu.VMEM((frame_count, wide // TILE, tall, TILE), bf16),
            pltpu.VMEM((frame_count, wide // TILE, tall, TILE), bf16),
            pltpu.VMEM((frame_count, wide // TILE, EDGE, TILE), f32),
            pltpu.VMEM((frame_count, wide // TILE, EDGE, TILE), f32),
            pltpu.VMEM((frame_count, col_count // TILE, row_count, TILE), f32),
            pltpu.VMEM((slot_count * PATCH, TILE), bf16),
        ],
        input_output_aliases=aliases,
        compiler_params=pltpu.CompilerParams(vmem_limit_bytes=40 * 1024 * 1024),
        cost_estimate=pl.CostEstimate(
            flops=20_000_000_000, bytes_accessed=16_000_000, transcendentals=0
        ),
        name=f"slab_{slab}",
    )(*operands)


def shards(frames, omega_taps, smooth_kernel, spots, counts):
    _, frame_count, row_count, col_count = frames.shape
    first_frame = lax.axis_index("omega") * frame_count
    first_row = lax.axis_index("row") * row_count
    first_col = lax.axis_index("col") * col_count

    rim, rim_low, rim_high, send_low1, send_high1 = cut(frames)
    rim = jnp.concatenate(
        [shifted(rim_low, "omega", 1), rim, shifted(rim_high, "omega", -1)], axis=1
    )
    low1 = shifted(send_low1, "omega", 1)
    high1 = shifted(send_high1, "omega", -1)
    lane = jnp.arange(TILE, dtype=jnp.int32)[None, :]
    step = jnp.arange(REACH, dtype=jnp.int32)[:, None]
    after = (lane == step).astype(bf16)
    before = (lane == TILE - REACH + step).astype(bf16)
    if lax.axis_size("col") == 2:
        first = lax.axis_index("col") == 0
        sides = jnp.where(first, rim[:, :, REACH:, col_count:], rim[:, :, :REACH, col_count:])
        sides = lax.ppermute(sides, "col", [(0, 1), (1, 0)])
        place = jnp.where(first, after, before)
    else:
        left = shifted(rim[:, :, REACH:, col_count:], "col", 1)
        right = shifted(rim[:, :, :REACH, col_count:], "col", -1)
        sides = jnp.concatenate([right, left], axis=2)
        place = jnp.concatenate([after, before], axis=0)
    later, sides = lax.optimization_barrier((frames, sides))
    send_low0, send_high0 = late_cut(later)
    low0 = shifted(send_low0, "omega", 1)
    high0 = shifted(send_high0, "omega", -1)
    edge = jnp.einsum("sfkr,kc->sfrc", sides, place, preferred_element_type=bf16)
    ends = jnp.concatenate([edge[:, :, :REACH], edge[:, :, -REACH:]], axis=2)
    line = jnp.concatenate([rim[..., :col_count], ends], axis=3)
    above = shifted(line[:, :, REACH:], "row", 1)
    below = shifted(line[:, :, :REACH], "row", -1)

    taps = omega_matrix(
        omega_taps, first_frame, frame_count, frame_count * lax.axis_size("omega")
    )
    w2 = smooth_matrix(smooth_kernel)
    frame, row, col = spots[:, 0] - first_frame, spots[:, 1] - first_row, spots[:, 2] - first_col
    tile = col // TILE
    beside = jnp.minimum(tile + 1, col_count // TILE - 1)
    live = jnp.broadcast_to(counts, frame.shape)
    local = jnp.stack([frame, row, tile, beside, col % TILE, live], axis=1)

    smoothed, second = run_slab(1, None, local[1], taps, w2, low1, frames, high1, edge, below, above)
    count = lax.axis_size("row") * lax.axis_size("col")
    second = lax.ppermute(second, ("row", "col"), [(i, count - 1 - i) for i in range(count)])
    smoothed, first = run_slab(0, smoothed, local[0], taps, w2, low0, frames, high0, edge, below, above)
    scores = (
        lax.dot_general(first, second, (((1,), (1,)), ((), ())), preferred_element_type=f32)
        / float(PATCH * PATCH)
    )
    return (smoothed, scores)


def solution(mesh):
    return jax.shard_map(
        shards,
        mesh=mesh,
        in_specs=(
            P(None, "omega", "row", "col"),
            P(),
            P(),
            P(None, None, ("omega", "row", "col")),
            P(None, ("omega", "row", "col")),
        ),
        out_specs=(P(None, "omega", "row", "col"), P(("omega", "row", "col"), None)),
        check_vma=False,
    )
```
